32 devices in a mesh: dp: 8 (over y, x, core), tensor: 4 (over z).
Axes of the slice: x: 2, y: 2, z: 4, core: 2. Of those that a mesh axis runs over, the one named last changes fastest.
Arguments:
- latents: bfloat16 [8, 512, 1536], P('dp', 'tensor'), may hold values from -6 to 6
- features: bfloat16 [8, 2048, 1536], P('dp', 'tensor'), may hold values from -6 to 6
- lengths: int32 [8, 8], P('dp'), may hold values from 1 to 512, 2048 in all within a row
- valid_media: int32 [8, 8], P('dp'), may hold values from 0 to 1, as said below
- media_gain: float32 [1536], replicated, may hold values from 0.5 to 1.5
- media_shift: float32 [1536], replicated, may hold values from -2 to 2
- latent_gain: float32 [1536], replicated, may hold values from 0.5 to 1.5
- latent_shift: float32 [1536], replicated, may hold values from -2 to 2
- feed_gain: float32 [1536], replicated, may hold values from 0.5 to 1.5
- feed_shift: float32 [1536], replicated, may hold values from -2 to 2
- query_weight: bfloat16 [1536, 1536], P(None, 'tensor'), may hold values from -0.15625 to 0.15625
- key_value_weight: bfloat16 [1536, 2, 1536], P(None, None, 'tensor'), may hold values from -0.15625 to 0.15625
- output_weight: bfloat16 [1536, 1536], P('tensor'), may hold values from -1.5 to 1.5
- up_weight: bfloat16 [1536, 6144], P(None, 'tensor'), may hold values from -0.15625 to 0.15625
- down_weight: bfloat16 [6144, 1536], P('tensor'), may hold values from -0.078125 to 0.078125
- cotangent: bfloat16 [8, 512, 1536], P('dp', 'tensor'), may hold values from -0.00059890747 to 0.00059890747
Outputs:
- result: bfloat16 [8, 512, 1536], P('dp', 'tensor')
- penalty: float32 [], replicated
- latents_grad: float32 [8, 512, 1536], P('dp', 'tensor')
- features_grad: float32 [8, 2048, 1536], P('dp', 'tensor')
- media_gain_grad: float32 [1536], P(('dp', 'tensor'))
- media_shift_grad: float32 [1536], P(('dp', 'tensor'))
- latent_gain_grad: float32 [1536], P(('dp', 'tensor'))
- latent_shift_grad: float32 [1536], P(('dp', 'tensor'))
- feed_gain_grad: float32 [1536], P(('dp', 'tensor'))
- feed_shift_grad: float32 [1536], P(('dp', 'tensor'))
- query_grad: float32 [1536, 1536], P('dp', 'tensor')
- keyval_grad: float32 [1536, 2, 1536], P('dp', None, 'tensor')
- output_grad: float32 [1536, 1536], P('tensor', 'dp')
- up_grad: float32 [1536, 6144], P('dp', 'tensor')
- down_grad: float32 [6144, 1536], P('tensor', 'dp')
The draws below stay inside these ranges and needn't reach their ends.
Inputs may be any that keep to these rules, and one draw needn't show every extreme that they name: `lengths`: each row holds the patch counts of 8 image slots that sum to 2048; the largest of each row is exactly 512. `valid_media`: 0 or 1; the first slot of every sequence holds 1.
All inputs are finite; a program needn't handle non-finite values.
Results may differ from the reference program's by a relative error of at most 0.012.
Values may be sent and summed in bfloat16 or wider, within the bound.
No kernel may reach another device: no remote copies, remote signals or barrier semaphores. Data moves between devices by JAX's collectives and lax.ppermute only.
A program may use at most 192 MiB of HBM per device.

```python
import math
import jax
import jax.numpy as jnp
import numpy as np
from jax import lax

D = 1536
HEADS = 16
HD = 96
FF = 6144
LAT = 64
IMGS = 8
P_SEQ = 2048
SEQS = 8
MOST_PATCH = 512


def draw_valid_media(key, part):
    key = jax.random.fold_in(key, 7)
    picked = jax.random.randint(key, (SEQS, IMGS), 0, 4)
    marks = (picked > 0).astype(jnp.int32)
    return marks.at[:, 0].set(1)


def steps_of(rng, extent, cuts, least, top_value):
    def one(position, blocks):
        heights = jax.random.uniform(jax.random.fold_in(jax.random.fold_in(rng, 6), position), (blocks,), jnp.float32, least / len(cuts), top_value / len(cuts))
        return jnp.repeat(jnp.exp(heights), extent[position] // blocks).reshape((-1,) + (1,) * (len(extent) - position - 1))

    gain = one(*cuts[0])
    for cut in cuts[1:]:
        gain = gain * one(*cut)
    return gain


def length_profile(count, total, reach, skew):
    weights = [(1 << 20) // math.isqrt(standing ** skew) + 1 for standing in range(2, count + 1)]
    surplus, given = total - reach - (count - 1), [1] * (count - 1)
    while surplus > 0:
        free = [i for i in range(count - 1) if given[i] < reach]
        pool, budget = sum([weights[i] for i in free]), surplus
        for i in free:
            more = min(reach - given[i], max(1, budget * weights[i] // pool), surplus)
            given[i] = given[i] + more
            surplus = surplus - more
    return np.array([reach] + given)


def uneven(rng, amount, total, bound, slope):
    if amount == 2:
        one = jax.random.randint(rng, (), max(1, total - bound), min(bound, total - 1) + 1)
        return jnp.stack([one, total - one])
    tallies = jnp.asarray(length_profile(amount, total, bound, slope), jnp.int32)
    twos = (amount - 1) // 2
    giver, taker = tallies[1:1 + 2 * twos:2], tallies[2:2 + 2 * twos:2]
    margin = jnp.minimum(giver - 1, bound - taker)
    moved = jax.random.randint(jax.random.fold_in(rng, 1), (twos,), 0, 1 << 20) % (margin + 1)
    tallies = tallies.at[1:1 + 2 * twos:2].set(giver - moved).at[2:2 + 2 * twos:2].set(taker + moved)
    return tallies[jax.random.permutation(jax.random.fold_in(rng, 2), amount)]


def gaussian(own_key, shape, spread, bound, shards=(), held_as=jnp.bfloat16):
    gain = steps_of(own_key, shape, shards, -0.22, 0.18) if shards else 1.0
    drawn = jax.random.normal(own_key, shape, jnp.float32) * spread * gain
    return jnp.minimum(jnp.maximum(drawn, -bound), bound).astype(held_as)


def setup_inputs(seed: int = 0) -> dict:
    key_of = jax.random.split(jax.random.key(seed), 17)
    return {
        "latents": gaussian(key_of[0], (SEQS, LAT * IMGS, D), 1.0, 6.0, ((0, 8), (1, 4))),
        "features": gaussian(key_of[1], (SEQS, P_SEQ, D), 1.0, 6.0, ((0, 8), (1, 4))),
        "lengths": jax.vmap(lambda own: uneven(own, IMGS, P_SEQ, MOST_PATCH, 1))(jax.random.split(key_of[2], SEQS)).reshape((SEQS, IMGS)).astype(jnp.int32),
        "valid_media": draw_valid_media(jax.random.fold_in(key_of[16], 71), 0),
        "media_gain": jnp.clip(1.0 + 0.1 * jax.random.normal(key_of[4], (D,), jnp.float32), 0.5, 1.5),
        "media_shift": gaussian(key_of[5], (D,), 0.3, 2.0, (), jnp.float32),
        "latent_gain": jnp.clip(1.0 + 0.1 * jax.random.normal(key_of[6], (D,), jnp.float32), 0.5, 1.5),
        "latent_shift": gaussian(key_of[7], (D,), 0.3, 2.0, (), jnp.float32),
        "feed_gain": jnp.clip(1.0 + 0.1 * jax.random.normal(key_of[8], (D,), jnp.float32), 0.5, 1.5),
        "feed_shift": gaussian(key_of[9], (D,), 0.3, 2.0, (), jnp.float32),
        "query_weight": gaussian(key_of[10], (D, HEADS * HD), D ** -0.5, 0.15625, ((1, 4),)),
        "key_value_weight": gaussian(key_of[11], (D, 2, HEADS * HD), D ** -0.5, 0.15625, ((2, 4),)),
        "output_weight": gaussian(key_of[12], (HEADS * HD, D), (max(HEADS * HD // 96, 1)) ** -0.5, 1.5, ((0, 4),)),
        "up_weight": gaussian(key_of[13], (D, FF), D ** -0.5, 0.15625, ((1, 4),)),
        "down_weight": gaussian(key_of[14], (FF, D), FF ** -0.5, 0.078125, ((0, 4),)),
        "cotangent": gaussian(key_of[15], (SEQS, LAT * IMGS, D), 0.0001, 0.00059890747, ((0, 8), (1, 4))),
    }


EPSILON = 1e-05
NEGATIVE = -1e+30
FULL_PRECISION = lax.Precision.HIGHEST

@jax.custom_vjp
def lower_precision(v):
    return lax.optimization_barrier(v.astype(jnp.bfloat16)).astype(jnp.float32)

@jax.custom_vjp
def lower_precision_backward(v):
    return v

def low_keep(v):
    return (lower_precision(v), None)

def low_pass(kept, grad):
    return (grad,)

def back_keep(v):
    return (v, None)

def back_low(kept, grad):
    return (lower_precision(grad),)
lower_precision.defvjp(low_keep, low_pass)
lower_precision_backward.defvjp(back_keep, back_low)

def layer_norm(values, gain_row, offset):
    center = values - lax.optimization_barrier(jnp.mean(values, axis=-1, keepdims=True))
    inv_root = lax.rsqrt(lax.optimization_barrier(jnp.mean(center * center, axis=-1, keepdims=True)) + EPSILON)
    return center * inv_root * gain_row + offset

def key_tables(lengths, valid_media):
    ends_at = jnp.cumsum(lengths, axis=1)
    positions = jnp.arange(P_SEQ, dtype=jnp.int32)
    patch_segment = lax.optimization_barrier(jnp.sum((positions[None, :, None] >= ends_at[:, None, :]).astype(jnp.int32), axis=2))
    image_index = jnp.arange(IMGS, dtype=jnp.int32)
    patch_valid = lax.optimization_barrier(jnp.sum(jnp.where(patch_segment[:, :, None] == image_index[None, None, :], valid_media[:, None, :], 0), axis=2)).astype(jnp.int32)
    latent_segment = jnp.arange(LAT * IMGS, dtype=jnp.int32) // LAT
    seq_total = lengths.shape[0]
    key_segment = jnp.concatenate([patch_segment, jnp.broadcast_to(latent_segment, (seq_total, LAT * IMGS))], axis=1)
    key_valid = jnp.concatenate([patch_valid, jnp.ones((seq_total, LAT * IMGS), jnp.int32)], axis=1)
    row_weight = jnp.repeat(valid_media, LAT, axis=1).astype(jnp.float32)
    return (key_segment, key_valid, row_weight)

def sequence_forward(parameters, latent_rows, media_rows, key_segment, key_valid, row_weight):
    media_gain, media_shift, latent_gain, latent_shift, feed_gain, feed_shift, query_weight, key_value_weight, output_weight, up_weight, down_weight = parameters
    media_normed = lower_precision(layer_norm(media_rows, media_gain, media_shift))
    latent_normed = lower_precision(layer_norm(latent_rows, latent_gain, latent_shift))
    queries = lower_precision(lower_precision_backward(jnp.dot(latent_normed, query_weight, precision=FULL_PRECISION)))
    media_key_input = jnp.concatenate([media_normed, latent_normed], axis=0)
    key_value_rows = lower_precision(lower_precision_backward(jnp.einsum('ob,bmu->mou', media_key_input, key_value_weight, precision=FULL_PRECISION)))
    rows_all = latent_rows.shape[0]
    head_query = queries.reshape(rows_all, HEADS, HD)
    head_key = key_value_rows[0].reshape(-1, HEADS, HD)
    head_value = key_value_rows[1].reshape(-1, HEADS, HD)
    scores = lower_precision_backward(jnp.einsum('qhe,khe->hqk', head_query, head_key, precision=FULL_PRECISION) * HD ** (-0.5))
    latent_segment = jnp.arange(rows_all, dtype=jnp.int32) // LAT
    allowed = (latent_segment[:, None] == key_segment[None, :]) & (key_valid[None, :] > 0)
    masked = jnp.where(allowed[None], scores, NEGATIVE)
    top_score = lax.optimization_barrier(jnp.max(masked, axis=-1, keepdims=True))
    unnormed = jnp.where(allowed[None], jnp.exp(masked - top_score), 0.0)
    denominator = lax.optimization_barrier(jnp.sum(unnormed, axis=-1, keepdims=True))
    probability = unnormed / denominator
    log_total = top_score[..., 0] + jnp.log(denominator[..., 0])
    entropy = log_total - lax.optimization_barrier(jnp.sum(jnp.where(allowed[None], probability * scores, 0.0), axis=-1))
    penalty_part = jnp.sum(entropy * row_weight[None, :])
    attended = jnp.einsum('hqk,khe->qhe', lower_precision(probability), head_value, precision=FULL_PRECISION).reshape(rows_all, HEADS * HD)
    attended = lower_precision(lower_precision_backward(attended))
    middle = latent_rows + lower_precision_backward(jnp.dot(attended, output_weight, precision=FULL_PRECISION))
    feed_input = lower_precision(layer_norm(middle, feed_gain, feed_shift))
    hidden = lower_precision_backward(jnp.dot(feed_input, up_weight, precision=FULL_PRECISION))
    activation = lower_precision(jax.nn.gelu(hidden, approximate=False))
    result = middle + lower_precision_backward(jnp.dot(activation, down_weight, precision=FULL_PRECISION))
    return (result, penalty_part)

def reference(latents, features, lengths, valid_media, media_gain, media_shift, latent_gain, latent_shift, feed_gain, feed_shift, query_weight, key_value_weight, output_weight, up_weight, down_weight, cotangent):
    key_segment, key_valid, row_weight = key_tables(lengths, valid_media)
    scale_total = jnp.sum(valid_media).astype(jnp.float32)
    parameters = (media_gain.astype(jnp.float32), media_shift.astype(jnp.float32), latent_gain.astype(jnp.float32), latent_shift.astype(jnp.float32), feed_gain.astype(jnp.float32), feed_shift.astype(jnp.float32), query_weight.astype(jnp.float32), key_value_weight.astype(jnp.float32), output_weight.astype(jnp.float32), up_weight.astype(jnp.float32), down_weight.astype(jnp.float32))

    def forward(params_in, latent_all, media_all):

        def per_sequence(running, pieces):
            result_rows, penalty_part = jax.checkpoint(sequence_forward)(params_in, pieces[0], pieces[1], pieces[2], pieces[3], pieces[4])
            return (running + penalty_part, result_rows)
        penalty_sum, results = lax.scan(per_sequence, jnp.zeros((), jnp.float32), (latent_all, media_all, key_segment, key_valid, row_weight))
        return (results, penalty_sum / scale_total)
    (results, penalty), pullback = jax.vjp(forward, parameters, latents.astype(jnp.float32), features.astype(jnp.float32))
    param_grads, latents_grad, features_grad = pullback((cotangent.astype(jnp.float32), jnp.ones((), jnp.float32)))
    return (results.astype(jnp.bfloat16), penalty, latents_grad, features_grad, param_grads[0], param_grads[1], param_grads[2], param_grads[3], param_grads[4], param_grads[5], param_grads[6], param_grads[7], param_grads[8], param_grads[9], param_grads[10])
```

```python
from functools import partial

import jax
import jax.numpy as jnp
from jax import lax
from jax.experimental import pallas as pl
from jax.experimental.pallas import tpu as pltpu
from jax.sharding import PartitionSpec as P

HD = 96
LAT = 64
EPSILON = 1e-05
NEGATIVE = -1e30
SCALE = HD ** (-0.5)
BF = jnp.bfloat16
F32 = jnp.float32
VMEM_LIMIT = 48 * 1024 * 1024


def rotate(x, count, shift):
    return lax.ppermute(x, "tensor", [(i, (i + shift) % count) for i in range(count)])


def gather_blocks(x, count):
    return [x] + [rotate(x, count, k) for k in range(1, count)]


def scatter_blocks(blocks, count):
    arrived = [rotate(blocks[k], count, -k) for k in range(1, count)]
    total = blocks[0].astype(F32)
    for part in arrived:
        total = total + part.astype(F32)
    return total


def swap(x, axis, count, bit):
    return lax.ppermute(x, axis, [(i, i ^ (1 << bit)) for i in range(count)])


def bits_of(count):
    return count.bit_length() - 1


def halve(parts, left, bit, count):
    place = left.index(bit)
    rest = parts.shape[1:]
    split = parts.reshape((1 << place, 2, 1 << (len(left) - place - 1)) + rest)
    mine = (lax.axis_index("dp") >> bit) & 1
    send = lax.dynamic_index_in_dim(split, 1 - mine, 1, keepdims=False)
    keep = lax.dynamic_index_in_dim(split, mine, 1, keepdims=False)
    got = swap(send, "dp", count, bit)
    total = keep.astype(F32) + got.astype(F32)
    left = [b for b in left if b != bit]
    return total.reshape((1 << len(left),) + rest), left


def bit_orders(count):
    outer = list(range(1, bits_of(count)))
    half = (len(outer) + 1) // 2
    return outer, outer[half:] + outer[:half]


def reduce_pair(one, two, count):
    left = list(range(bits_of(count) - 1, -1, -1))
    both, left = halve(jnp.stack([one, two], axis=1), left, 0, count)
    both = both.astype(BF)
    out = []
    for which, order in enumerate(bit_orders(count)):
        part, still = both[:, which], left
        for bit in order:
            part, still = halve(part.astype(BF), still, bit, count)
        out.append(part[0])
    return out


def all_sum(x, axes):
    for axis, count in axes:
        for bit in range(bits_of(count)):
            x = x + swap(x, axis, count, bit)
    return x


def place_kernel(n_dp, n_t, offsets, at_ref, own_ref, even_ref, odd_ref, out_ref, sem):
    z, p = at_ref[0], at_ref[1]
    copies = [pltpu.make_async_copy(own_ref, out_ref.at[z], sem)]
    for k in range(1, n_t):
        shard = lax.rem(z - k + n_t, n_t)
        for i, off in enumerate(offsets):
            copies.append(
                pltpu.make_async_copy(even_ref.at[i, k - 1], out_ref.at[shard, p ^ off], sem)
            )
            copies.append(
                pltpu.make_async_copy(
                    odd_ref.at[i, k - 1], out_ref.at[shard, p ^ (off ^ 1)], sem
                )
            )
    for copy in copies:
        copy.start()
    for copy in copies:
        copy.wait()


def place(own, even, odd, offsets, at, n_dp, n_t):
    unit = own.shape[0] // n_dp
    width = own.shape[1]
    out = pl.pallas_call(
        partial(place_kernel, n_dp, n_t, offsets),
        out_shape=jax.ShapeDtypeStruct((n_t, n_dp, unit, width), own.dtype),
        in_specs=[pl.BlockSpec(memory_space=pltpu.SMEM)] + [pl.BlockSpec(memory_space=pl.ANY)] * 3,
        out_specs=pl.BlockSpec(memory_space=pl.ANY),
        scratch_shapes=[pltpu.SemaphoreType.DMA],
    )(at, own.reshape(n_dp, unit, width), even, odd)
    return out.reshape(n_t * own.shape[0], width)


def gather_pair(one, two, at, n_dp, n_t):
    unit = one.shape[0] // n_dp
    width = one.shape[1]
    slices = jnp.stack([one, two]).reshape(2, n_dp, unit, width)
    mine = lax.dynamic_index_in_dim(slices, lax.axis_index("dp"), 1, keepdims=False)
    arrived = jnp.stack([rotate(mine, n_t, k) for k in range(1, n_t)], axis=1)
    out = []
    for which, (own, order) in enumerate(zip((one, two), bit_orders(n_dp))):
        held, offsets = arrived[which][None], [0]
        for bit in order:
            held = jnp.concatenate([held, swap(held, "dp", n_dp, bit)], axis=0)
            offsets = offsets + [o ^ (1 << bit) for o in offsets]
        other = swap(held, "dp", n_dp, 0)
        out.append(place(own, held, other, offsets, at, n_dp, n_t))
    return out


def three(x):
    high = x.astype(BF)
    left = x - high.astype(F32)
    middle = left.astype(BF)
    low = (left - middle.astype(F32)).astype(BF)
    return jnp.concatenate([high, middle, low], axis=0)


def join(x, count):
    x = x.astype(F32)
    return x[:count] + x[count : 2 * count] + x[2 * count :]


def forward_kernel(heads, n_t, q_ref, k_ref, v_ref, seg_ref, img_ref, *rest):
    msgs, stat = rest[:n_t], rest[n_t]
    h = pl.program_id(0)
    rows = q_ref.shape[1] // n_t
    scores = (
        lax.dot_general(
            k_ref[...], q_ref[...], (((0,), (0,)), ((), ())), preferred_element_type=F32
        )
        * SCALE
    )
    allowed = seg_ref[...] == img_ref[...]
    masked = jnp.where(allowed, scores, NEGATIVE)
    top = jnp.max(masked, axis=0, keepdims=True)
    weight = jnp.where(allowed, jnp.exp(masked - top), 0.0)
    total = jnp.sum(weight, axis=0, keepdims=True)
    mean = jnp.sum(weight * scores, axis=0, keepdims=True)
    some = total > 0.0
    inverse = jnp.where(some, 1.0 / jnp.where(some, total, 1.0), 0.0)
    out = jnp.dot(v_ref[...], weight.astype(BF), preferred_element_type=F32) * inverse
    stat[pl.ds(h, 1)] = jnp.where(some, top + jnp.log(jnp.where(some, total, 1.0)), NEGATIVE)
    stat[pl.ds(heads + h, 1)] = mean * inverse
    at = pl.ds(pl.multiple_of(h * HD, HD), HD)
    for k in range(n_t):
        msgs[k][at, :] = out[:, k * rows : (k + 1) * rows].astype(BF)

    @pl.when(h == heads - 1)
    def _():
        for k in range(n_t):
            cols = slice(k * rows, (k + 1) * rows)
            msgs[k][heads * HD : heads * (HD + 3), :] = three(stat[:heads, cols])
            msgs[k][heads * (HD + 3) :, :] = three(stat[heads:, cols])


def attend_forward(q, k, v, seg, img, n_t):
    heads = q.shape[0] // HD
    rows, keys = q.shape[1], k.shape[1]
    one = rows // n_t
    tall = heads * (HD + 6)
    return pl.pallas_call(
        partial(forward_kernel, heads, n_t),
        grid=(heads,),
        out_shape=[jax.ShapeDtypeStruct((tall, one), BF)] * n_t,
        in_specs=[
            pl.BlockSpec((HD, rows), lambda h: (h, 0)),
            pl.BlockSpec((HD, keys), lambda h: (h, 0)),
            pl.BlockSpec((HD, keys), lambda h: (h, 0)),
            pl.BlockSpec((keys, 1), lambda h: (0, 0)),
            pl.BlockSpec((1, rows), lambda h: (0, 0)),
        ],
        out_specs=[pl.BlockSpec((tall, one), lambda h: (0, 0))] * n_t,
        scratch_shapes=[pltpu.VMEM((2 * heads, rows), F32)],
        compiler_params=pltpu.CompilerParams(vmem_limit_bytes=VMEM_LIMIT),
    )(q, k, v, seg, img)


def combine_kernel(heads, n_t, *refs):
    msgs, (out_ref, stat_ref) = refs[:n_t], refs[n_t:]
    base = heads * HD
    logs = [join(m[base : base + 3 * heads, :], heads) for m in msgs]
    means = [join(m[base + 3 * heads :, :], heads) for m in msgs]
    top = logs[0]
    for x in logs[1:]:
        top = jnp.maximum(top, x)
    shares = [jnp.exp(x - top) for x in logs]
    total = shares[0]
    for x in shares[1:]:
        total = total + x
    shares = [x / total for x in shares]
    mean = shares[0] * means[0]
    for s, x in zip(shares[1:], means[1:]):
        mean = mean + s * x
    stat_ref[:heads, :] = top + jnp.log(total)
    stat_ref[heads:, :] = mean
    for h in range(heads):
        at = slice(h * HD, (h + 1) * HD)
        acc = msgs[0][at, :].astype(F32) * shares[0][h : h + 1, :]
        for s, m in zip(shares[1:], msgs[1:]):
            acc = acc + m[at, :].astype(F32) * s[h : h + 1, :]
        out_ref[at, :] = acc.astype(BF)


def combine(msgs, heads):
    one = msgs[0].shape[1]
    return pl.pallas_call(
        partial(combine_kernel, heads, len(msgs)),
        out_shape=[
            jax.ShapeDtypeStruct((heads * HD, one), BF),
            jax.ShapeDtypeStruct((2 * heads, one), F32),
        ],
        compiler_params=pltpu.CompilerParams(vmem_limit_bytes=VMEM_LIMIT),
    )(*msgs)


def message_kernel(heads, do_ref, out_ref, stat_ref, coef_ref, msg_ref):
    base = heads * HD
    deltas = []
    for h in range(heads):
        at = slice(h * HD, (h + 1) * HD)
        grad = do_ref[at, :].astype(F32)
        deltas.append(jnp.sum(grad * out_ref[at, :].astype(F32), axis=0, keepdims=True))
    msg_ref[:base, :] = do_ref[...]
    delta = jnp.concatenate(deltas, axis=0) - coef_ref[...] * stat_ref[heads:, :]
    msg_ref[base : base + 3 * heads, :] = three(stat_ref[:heads, :])
    msg_ref[base + 3 * heads :, :] = three(delta)


def make_message(do, out, stat, coef, heads):
    return pl.pallas_call(
        partial(message_kernel, heads),
        out_shape=jax.ShapeDtypeStruct((heads * (HD + 6), do.shape[1]), BF),
        compiler_params=pltpu.CompilerParams(vmem_limit_bytes=VMEM_LIMIT),
    )(do, out, stat, coef)


def backward_kernel(heads, n_t, q_ref, k_ref, v_ref, seg_ref, img_ref, coef_ref, *rest):
    grads, stats = rest[:n_t], rest[n_t : 2 * n_t]
    dq_ref, dk_ref, dv_ref, stat = rest[2 * n_t :]
    h = pl.program_id(0)

    @pl.when(h == 0)
    def _():
        rows = q_ref.shape[1] // n_t
        for i in range(n_t):
            cols = slice(i * rows, (i + 1) * rows)
            stat[:heads, cols] = join(stats[i][: 3 * heads, :], heads)
            stat[heads:, cols] = join(stats[i][3 * heads :, :], heads)

    q, k, v = q_ref[...], k_ref[...], v_ref[...]
    grad = jnp.concatenate([g[...] for g in grads], axis=1)
    scores = (
        lax.dot_general(k, q, (((0,), (0,)), ((), ())), preferred_element_type=F32) * SCALE
    )
    allowed = seg_ref[...] == img_ref[...]
    log_total = stat[pl.ds(h, 1)]
    delta = stat[pl.ds(heads + h, 1)]
    prob = jnp.where(allowed, jnp.exp(jnp.where(allowed, scores - log_total, 0.0)), 0.0)
    back_prob = lax.dot_general(v, grad, (((0,), (0,)), ((), ())), preferred_element_type=F32)
    back = (prob * (back_prob - coef_ref[...] * scores - delta)).astype(BF)
    dq_ref[...] = (jnp.dot(k, back, preferred_element_type=F32) * SCALE).astype(BF)
    nt = (((1,), (1,)), ((), ()))
    dk_ref[...] = (lax.dot_general(q, back, nt, preferred_element_type=F32) * SCALE).astype(BF)
    dv_ref[...] = lax.dot_general(
        grad, prob.astype(BF), nt, preferred_element_type=F32
    ).astype(BF)


def attend_backward(q, k, v, seg, img, coef, msgs):
    n_t = len(msgs)
    heads = q.shape[0] // HD
    rows, keys = q.shape[1], k.shape[1]
    one = rows // n_t
    return pl.pallas_call(
        partial(backward_kernel, heads, n_t),
        grid=(heads,),
        out_shape=[
            jax.ShapeDtypeStruct(q.shape, BF),
            jax.ShapeDtypeStruct(k.shape, BF),
            jax.ShapeDtypeStruct(v.shape, BF),
        ],
        in_specs=[
            pl.BlockSpec((HD, rows), lambda h: (h, 0)),
            pl.BlockSpec((HD, keys), lambda h: (h, 0)),
            pl.BlockSpec((HD, keys), lambda h: (h, 0)),
            pl.BlockSpec((keys, 1), lambda h: (0, 0)),
            pl.BlockSpec((1, rows), lambda h: (0, 0)),
            pl.BlockSpec((1, rows), lambda h: (0, 0)),
        ]
        + [pl.BlockSpec((HD, one), lambda h: (h, 0))] * n_t
        + [pl.BlockSpec((6 * heads, one), lambda h: (HD // 6, 0))] * n_t,
        out_specs=[
            pl.BlockSpec((HD, rows), lambda h: (h, 0)),
            pl.BlockSpec((HD, keys), lambda h: (h, 0)),
            pl.BlockSpec((HD, keys), lambda h: (h, 0)),
        ],
        scratch_shapes=[pltpu.VMEM((2 * heads, rows), F32)],
        compiler_params=pltpu.CompilerParams(vmem_limit_bytes=VMEM_LIMIT),
    )(q, k, v, seg, img, coef, *msgs, *msgs)


def norm_parts(values):
    values = values.astype(F32)
    center = values - jnp.mean(values, axis=-1, keepdims=True)
    inv_root = lax.rsqrt(jnp.mean(center * center, axis=-1, keepdims=True) + EPSILON)
    return center * inv_root, inv_root


def norm_backward(grad_rows, normal, inv_root, gain_row):
    scaled = grad_rows * gain_row
    reduced = (
        scaled
        - jnp.mean(scaled, axis=-1, keepdims=True)
        - normal * jnp.mean(scaled * normal, axis=-1, keepdims=True)
    )
    return reduced * inv_root


def gain_shift(grad_rows, normal):
    return [jnp.sum(grad_rows * normal, axis=0), jnp.sum(grad_rows, axis=0)]


def dot(equation, a, b):
    return jnp.einsum(equation, a, b, preferred_element_type=F32)


def local(
    latents,
    features,
    lengths,
    valid_media,
    media_gain,
    media_shift,
    latent_gain,
    latent_shift,
    feed_gain,
    feed_shift,
    query_weight,
    key_value_weight,
    output_weight,
    up_weight,
    down_weight,
    cotangent,
):
    n_t = lax.axis_size("tensor")
    n_dp = lax.axis_size("dp")
    z, p = lax.axis_index("tensor"), lax.axis_index("dp")
    at = jnp.stack([z, p]).astype(jnp.int32)
    latents, features, cotangent = latents[0], features[0], cotangent[0]
    lengths, valid = lengths[0], valid_media[0]
    width = latents.shape[1]
    own_rows, own_patches = latents.shape[0], features.shape[0]
    inner = query_weight.shape[1] * n_t
    heads = inner // HD
    images = lengths.shape[0]

    latent_blocks = gather_blocks(latents, n_t)
    wq, wk = gather_pair(query_weight.T, key_value_weight[:, 0].T, at, n_dp, n_t)
    wv, wo = gather_pair(key_value_weight[:, 1].T, output_weight, at, n_dp, n_t)
    cot_all = jnp.concatenate(gather_blocks(cotangent, n_t), axis=0)

    count_part = jnp.full((8, 128), jnp.sum(valid).astype(F32))
    count_total = all_sum(count_part, [("dp", n_dp)])[0, 0]

    ends = jnp.sum(
        jnp.where(jnp.arange(images)[:, None] <= jnp.arange(images)[None, :], lengths[:, None], 0),
        axis=0,
    )
    positions = z * own_patches + jnp.arange(own_patches, dtype=jnp.int32)
    segment = jnp.sum((positions[:, None] >= ends[None, :]).astype(jnp.int32), axis=1)
    hit = segment[:, None] == jnp.arange(images, dtype=jnp.int32)[None, :]
    patch_valid = jnp.sum(jnp.where(hit, valid[None, :], 0), axis=1)
    patch_segment = jnp.where(patch_valid > 0, segment, -1)
    own_images = (z * own_rows + jnp.arange(own_rows, dtype=jnp.int32)) // LAT
    key_image = jnp.concatenate([patch_segment, own_images])[:, None]
    block_of = (z - jnp.arange(n_t, dtype=jnp.int32) + n_t) % n_t
    row_index = block_of[:, None] * own_rows + jnp.arange(own_rows, dtype=jnp.int32)[None, :]
    row_image = (row_index // LAT).reshape(1, -1)
    row_valid = jnp.sum(
        jnp.where(row_image.T == jnp.arange(images, dtype=jnp.int32)[None, :], valid[None, :], 0),
        axis=1,
    ).astype(F32)[None, :]

    media_hat, media_root = norm_parts(features)
    media_normed = (media_hat * media_gain + media_shift).astype(BF)
    latent_all = jnp.concatenate(latent_blocks, axis=0)
    latent_hat, latent_root = norm_parts(latent_all)
    latent_normed = (latent_hat * latent_gain + latent_shift).astype(BF)
    key_input = jnp.concatenate([media_normed, latent_normed[:own_rows]], axis=0)
    queries = dot("hd,rd->hr", wq, latent_normed).astype(BF)
    keys = dot("hd,rd->hr", wk, key_input).astype(BF)
    values = dot("hd,rd->hr", wv, key_input).astype(BF)
    sent = attend_forward(queries, keys, values, key_image, row_image, n_t)
    got = [sent[0]] + [rotate(sent[k], n_t, -k) for k in range(1, n_t)]
    attended, stat = combine(got, heads)
    entropy = stat[:heads] - stat[heads:]
    own_valid = row_valid[:, :own_rows]
    penalty_part = jnp.sum(entropy * own_valid)

    latent_own = latents.astype(F32)
    middle = latent_own + dot("hr,hd->rd", attended, wo)
    feed_hat, feed_root = norm_parts(middle)
    feed_normed = (feed_hat * feed_gain + feed_shift).astype(BF)
    feed_all = jnp.concatenate(gather_blocks(feed_normed, n_t), axis=0)
    hidden = dot("rd,df->rf", feed_all, up_weight)
    cdf = 0.5 * (1.0 + lax.erf(hidden * (0.5**0.5)))
    slope = cdf + hidden * jnp.exp(-0.5 * hidden * hidden) * (0.5 / jnp.pi) ** 0.5
    activation = (hidden * cdf).astype(BF)
    back_activation = dot("rd,fd->rf", cot_all, down_weight)
    back_hidden = (back_activation * slope).astype(BF)
    back_terms = dot("rf,df->rd", back_hidden, up_weight).astype(BF)
    back_feed = scatter_blocks(
        [back_terms[k * own_rows : (k + 1) * own_rows] for k in range(n_t)], n_t
    )
    feed_terms = dot("rf,fd->rd", activation, down_weight).astype(BF)
    result = middle + scatter_blocks(
        [feed_terms[k * own_rows : (k + 1) * own_rows] for k in range(n_t)], n_t
    )
    grad_down = dot("rd,rf->df", cot_all, activation).astype(BF)
    grad_up = dot("rd,rf->df", feed_all, back_hidden).astype(BF)
    down_share, up_share = reduce_pair(
        grad_down.reshape(n_dp, width // n_dp, -1), grad_up.reshape(n_dp, width // n_dp, -1), n_dp
    )

    back_middle = cotangent.astype(F32) + norm_backward(back_feed, feed_hat, feed_root, feed_gain)
    back_branch = back_middle.astype(BF)
    back_attended = dot("hd,rd->hr", wo, back_branch).astype(BF)
    own_coef = own_valid / count_total
    message = make_message(back_attended, attended, stat, own_coef, heads)
    messages = gather_blocks(message, n_t)
    back_q, back_k, back_v = attend_backward(
        queries, keys, values, key_image, row_image, row_valid / count_total, messages
    )

    def shares(a, b):
        return dot("rd,hr->dh", a, b).astype(BF).reshape(n_dp, width // n_dp, inner)

    key_share, value_share = reduce_pair(shares(key_input, back_k), shares(key_input, back_v), n_dp)
    query_share, output_share = reduce_pair(
        shares(latent_normed, back_q), shares(back_branch, attended), n_dp
    )
    back_inputs = dot("hr,hd->rd", back_k, wk) + dot("hr,hd->rd", back_v, wv)
    back_media = back_inputs[:own_patches]
    latent_terms = dot("hr,hd->rd", back_q, wq)
    latent_terms = jnp.concatenate(
        [latent_terms[:own_rows] + back_inputs[own_patches:], latent_terms[own_rows:]], axis=0
    )
    terms_low = latent_terms.astype(BF)
    back_latent = scatter_blocks(
        [terms_low[k * own_rows : (k + 1) * own_rows] for k in range(n_t)], n_t
    )
    features_grad = norm_backward(back_media, media_hat, media_root, media_gain)
    latents_grad = back_middle + norm_backward(
        back_latent, latent_hat[:own_rows], latent_root[:own_rows], latent_gain
    )

    part = inner // n_t
    four = jnp.stack([query_share, key_share, value_share, output_share]).astype(BF)
    four = four.reshape(4, width // n_dp, n_t, part).transpose(2, 0, 1, 3)
    blocks = [
        lax.dynamic_index_in_dim(four, (z - k + n_t) % n_t, 0, keepdims=False) for k in range(n_t)
    ]
    four = scatter_blocks(blocks, n_t)

    sums = (
        gain_shift(back_media, media_hat)
        + gain_shift(latent_terms, latent_hat)
        + gain_shift(back_feed, feed_hat)
    )
    sums = jnp.stack(sums + [jnp.full((width,), penalty_part)] * 2)
    sums = all_sum(sums, [("dp", n_dp), ("tensor", n_t)])
    penalty = sums[6, 0] / count_total
    share = width // (n_dp * n_t)
    mine = lax.dynamic_index_in_dim(
        sums.reshape(8, n_dp * n_t, share), p * n_t + z, 1, keepdims=False
    )
    return (
        result.astype(BF)[None],
        penalty,
        latents_grad[None],
        features_grad[None],
        mine[0],
        mine[1],
        mine[2],
        mine[3],
        mine[4],
        mine[5],
        four[0],
        jnp.stack([four[1], four[2]], axis=1),
        four[3].T,
        up_share,
        down_share.T,
    )


def solution(mesh):
    return jax.shard_map(
        local,
        mesh=mesh,
        in_specs=(
            P("dp", "tensor", None),
            P("dp", "tensor", None),
            P("dp", None),
            P("dp", None),
            P(),
            P(),
            P(),
            P(),
            P(),
            P(),
            P(None, "tensor"),
            P(None, None, "tensor"),
            P("tensor", None),
            P(None, "tensor"),
            P("tensor", None),
            P("dp", "tensor", None),
        ),
        out_specs=(
            P("dp", "tensor", None),
            P(),
            P("dp", "tensor", None),
            P("dp", "tensor", None),
            P(("dp", "tensor")),
            P(("dp", "tensor")),
            P(("dp", "tensor")),
            P(("dp", "tensor")),
            P(("dp", "tensor")),
            P(("dp", "tensor")),
            P("dp", "tensor"),
            P("dp", None, "tensor"),
            P("tensor", "dp"),
            P("dp", "tensor"),
            P("tensor", "dp"),
        ),
        check_vma=False,
    )
```

```python
from functools import partial

import jax
import jax.numpy as jnp
from jax import lax
from jax.experimental import pallas as pl
from jax.experimental.pallas import tpu as pltpu
from jax.sharding import PartitionSpec as P

HD = 96
LAT = 64
EPSILON = 1e-05
NEGATIVE = -1e30
SCALE = HD ** (-0.5)
BF = jnp.bfloat16
F32 = jnp.float32
VMEM_LIMIT = 48 * 1024 * 1024


def rotate(x, count, shift):
    return lax.ppermute(x, "tensor", [(i, (i + shift) % count) for i in range(count)])


def after(x, *done):
    return lax.optimization_barrier((x, *done))[0]


def gather_blocks(x, count):
    if count != 4:
        return [x] + [rotate(x, count, k) for k in range(1, count)]
    z = lax.axis_index("tensor")
    two = rotate(x, 4, 2)
    up = lax.ppermute(x, "tensor", [(0, 1), (1, 2), (2, 3)])
    down = lax.ppermute(x, "tensor", [(1, 0), (2, 1), (3, 2)])
    ends = lax.ppermute(two, "tensor", [(2, 3), (1, 0)])
    return [x, jnp.where(z == 0, ends, up), two, jnp.where(z == 3, ends, down)]


def scatter_blocks(blocks, count):
    arrived = [rotate(blocks[k], count, -k) for k in range(1, count)]
    total = blocks[0].astype(F32)
    for part in arrived:
        total = total + part.astype(F32)
    return total


def swap(x, axis, count, bit):
    return lax.ppermute(x, axis, [(i, i ^ (1 << bit)) for i in range(count)])


def bits_of(count):
    return count.bit_length() - 1


def bit_orders(count):
    outer = list(range(1, bits_of(count)))
    half = (len(outer) + 1) // 2
    return outer, outer[half:] + outer[:half]


def gradient_kernel(natural, at_ref, even_ref, odd_ref, y_ref, keep_ref, send_ref):
    dims = (((1,), (0,)), ((), ())) if natural else (((1,), (1,)), ((), ()))
    keep_ref[0] = lax.dot_general(
        even_ref[...], y_ref[...], dims, preferred_element_type=F32
    ).astype(BF)
    send_ref[0] = lax.dot_general(
        odd_ref[...], y_ref[...], dims, preferred_element_type=F32
    ).astype(BF)


def gradient(xt, y, natural, at, n_dp):
    unit, rows = xt.shape[0] // n_dp, xt.shape[1]
    wide = y.shape[1] if natural else y.shape[0]
    half = n_dp // 2
    return pl.pallas_call(
        partial(gradient_kernel, natural),
        grid_spec=pltpu.PrefetchScalarGridSpec(
            num_scalar_prefetch=1,
            grid=(half,),
            in_specs=[
                pl.BlockSpec((unit, rows), lambda i, at: (at[1] ^ (2 * i), 0)),
                pl.BlockSpec((unit, rows), lambda i, at: (at[1] ^ (2 * i + 1), 0)),
                pl.BlockSpec(y.shape, lambda i, at: (0, 0)),
            ],
            out_specs=[pl.BlockSpec((1, unit, wide), lambda i, at: (i, 0, 0))] * 2,
        ),
        out_shape=[jax.ShapeDtypeStruct((half, unit, wide), BF)] * 2,
        compiler_params=pltpu.CompilerParams(vmem_limit_bytes=VMEM_LIMIT),
        cost_estimate=pl.CostEstimate(
            flops=2 * n_dp * unit * rows * wide,
            bytes_accessed=2 * (n_dp * unit * (rows + wide) + rows * wide),
            transcendentals=0,
        ),
    )(at, xt, xt, y)


def reduce_step(keep, got, order, step, n_dp):
    left = [b for b in range(bits_of(n_dp) - 1, 0, -1) if b not in order[:step]]
    place = left.index(order[step])
    shape = (1 << place, 2, 1 << (len(left) - place - 1)) + keep.shape[1:]
    flat = (1 << (len(left) - 1),) + keep.shape[1:]
    keep, got = keep.reshape(shape), got.reshape(shape)
    send = (keep[:, 1].astype(F32) + got[:, 1].astype(F32)).astype(BF)
    keep = (keep[:, 0].astype(F32) + got[:, 0].astype(F32)).astype(BF)
    return keep.reshape(flat), swap(send.reshape(flat), "dp", n_dp, order[step])


def reduce_outer(keep, got, order, n_dp):
    for step in range(len(order)):
        keep, got = reduce_step(keep, got, order, step, n_dp)
    return keep[0], got[0]


def blocks_kernel(n_t, pairs, at_ref, *refs):
    ins, outs = refs[: 2 * pairs], refs[2 * pairs :]
    z = at_ref[0]
    part = outs[0].shape[-1]
    for k in range(n_t):
        start = pl.multiple_of(lax.rem(z - k + n_t, n_t) * part, part)
        for m in range(pairs):
            cols = pl.ds(start, part)
            total = ins[2 * m][:, cols].astype(F32) + ins[2 * m + 1][:, cols].astype(F32)
            outs[k][m] = total.astype(outs[k].dtype)


def tensor_blocks(pairs, at, n_t):
    rows, columns = pairs[0][0].shape
    part = columns // n_t
    count = len(pairs)
    flat = [x for pair in pairs for x in pair]
    return pl.pallas_call(
        partial(blocks_kernel, n_t, count),
        in_specs=[pl.BlockSpec(memory_space=pltpu.SMEM)]
        + [pl.BlockSpec(memory_space=pltpu.VMEM)] * len(flat),
        out_shape=[jax.ShapeDtypeStruct((count, rows, part), F32 if k == 0 else BF) for k in range(n_t)],
        compiler_params=pltpu.CompilerParams(vmem_limit_bytes=VMEM_LIMIT),
    )(at, *flat)


def all_sum(x, axes):
    for axis, count in axes:
        for bit in range(bits_of(count)):
            x = x + swap(x, axis, count, bit)
    return x


def place_kernel(n_t, unit, z_rows, z_cols, offsets, parts, at_ref, own_ref, *refs):
    out_ref = refs[-1]
    z, p = at_ref[0], at_ref[1]
    rows, cols = own_ref.shape
    if z_rows:
        out_ref[pl.ds(pl.multiple_of(z * z_rows, z_rows), rows), :] = own_ref[...]
    else:
        out_ref[:, pl.ds(pl.multiple_of(z * z_cols, z_cols), cols)] = own_ref[...]
    for k in range(1, n_t):
        shard = lax.rem(z - k + n_t, n_t)
        for which, (row_at, col_at) in enumerate(parts):
            for odd in range(2):
                src = refs[2 * which + odd]
                height, wide = src.shape[2:]
                for i, off in enumerate(offsets[which]):
                    base = shard * z_rows + (p ^ (off ^ odd)) * unit + row_at
                    where = pl.ds(pl.multiple_of(base, 16), height)
                    if z_cols:
                        at = pl.ds(pl.multiple_of(shard * z_cols, z_cols), wide)
                    else:
                        at = slice(col_at, col_at + wide)
                    out_ref[where, at] = src[i, k - 1]


def reorder(x, places):
    return jnp.stack([lax.dynamic_index_in_dim(x, i, 0, keepdims=False) for i in places])


def place(own, pieces, offsets, parts, unit, by_rows, at, n_dp, n_t):
    rows, cols = own.shape
    shape = (n_t * rows, cols) if by_rows else (rows, n_t * cols)
    if unit % 16 or any(row_at % 16 for row_at, _ in parts):
        z, p = at[0], at[1]
        across = []
        for (even, odd), offs in zip(pieces, offsets):
            ordered = [None] * n_dp
            for i, off in enumerate(offs):
                ordered[off], ordered[off ^ 1] = even[i], odd[i]
            across.append(reorder(jnp.stack(ordered), [p ^ d for d in range(n_dp)]))
        axis = 2 if parts[-1][1] == 0 else 3
        whole = jnp.concatenate(across, axis=axis).transpose(1, 0, 2, 3)
        whole = whole.reshape((n_t - 1, rows, cols))
        whole = jnp.concatenate([own[None], whole], axis=0)
        whole = reorder(whole, [(z - k + n_t) % n_t for k in range(n_t)])
        return whole.reshape(shape) if by_rows else whole.transpose(1, 0, 2).reshape(shape)
    flat = [x for pair in pieces for x in pair]
    return pl.pallas_call(
        partial(place_kernel, n_t, unit, rows if by_rows else 0, 0 if by_rows else cols, offsets, parts),
        out_shape=jax.ShapeDtypeStruct(shape, own.dtype),
        in_specs=[pl.BlockSpec(memory_space=pltpu.SMEM)]
        + [pl.BlockSpec(memory_space=pltpu.VMEM)] * (1 + len(flat)),
        out_specs=pl.BlockSpec(memory_space=pltpu.VMEM),
        compiler_params=pltpu.CompilerParams(vmem_limit_bytes=VMEM_LIMIT),
    )(at, own, *flat)


def spread(slices, n_dp, n_t):
    arrived = gather_blocks(slices, n_t)[1:]
    pieces, offsets = [], []
    for which, order in enumerate(bit_orders(n_dp)):
        held, offs = jnp.stack([x[which] for x in arrived])[None], [0]
        for bit in order:
            held = jnp.concatenate([held, swap(held, "dp", n_dp, bit)], axis=0)
            offs = offs + [o ^ (1 << bit) for o in offs]
        pieces.append((held, swap(held, "dp", n_dp, 0)))
        offsets.append(offs)
    return pieces, offsets, arrived[0]


def share_of(x, axis, count):
    size = x.shape[axis] // count
    return lax.dynamic_slice_in_dim(x, lax.axis_index("dp") * size, size, axis)


def three(x):
    high = x.astype(BF)
    left = x - high.astype(F32)
    middle = left.astype(BF)
    low = (left - middle.astype(F32)).astype(BF)
    return jnp.concatenate([high, middle, low], axis=0)


def join(x, count):
    x = x.astype(F32)
    return x[:count] + x[count : 2 * count] + x[2 * count :]


def forward_kernel(heads, n_t, q_ref, k_ref, v_ref, seg_ref, img_ref, *rest):
    msgs, stat = rest[:n_t], rest[n_t]
    h = pl.program_id(0)
    rows = q_ref.shape[1] // n_t
    scores = (
        lax.dot_general(
            k_ref[...], q_ref[...], (((0,), (0,)), ((), ())), preferred_element_type=F32
        )
        * SCALE
    )
    allowed = seg_ref[...] == img_ref[...]
    masked = jnp.where(allowed, scores, NEGATIVE)
    top = jnp.max(masked, axis=0, keepdims=True)
    weight = jnp.where(allowed, jnp.exp(masked - top), 0.0)
    total = jnp.sum(weight, axis=0, keepdims=True)
    mean = jnp.sum(weight * scores, axis=0, keepdims=True)
    some = total > 0.0
    inverse = jnp.where(some, 1.0 / jnp.where(some, total, 1.0), 0.0)
    out = jnp.dot(v_ref[...], weight.astype(BF), preferred_element_type=F32) * inverse
    stat[pl.ds(h, 1)] = jnp.where(some, top + jnp.log(jnp.where(some, total, 1.0)), NEGATIVE)
    stat[pl.ds(heads + h, 1)] = mean * inverse
    at = pl.ds(pl.multiple_of(h * HD, HD), HD)
    for k in range(n_t):
        msgs[k][at, :] = out[:, k * rows : (k + 1) * rows].astype(BF)

    @pl.when(h == heads - 1)
    def _():
        for k in range(n_t):
            cols = slice(k * rows, (k + 1) * rows)
            msgs[k][heads * HD : heads * (HD + 3), :] = three(stat[:heads, cols])
            msgs[k][heads * (HD + 3) :, :] = three(stat[heads:, cols])


def attend_forward(q, k, v, seg, img, n_t):
    heads = q.shape[0] // HD
    rows, keys = q.shape[1], k.shape[1]
    one = rows // n_t
    tall = heads * (HD + 6)
    return pl.pallas_call(
        partial(forward_kernel, heads, n_t),
        grid=(heads,),
        out_shape=[jax.ShapeDtypeStruct((tall, one), BF)] * n_t,
        in_specs=[
            pl.BlockSpec((HD, rows), lambda h: (h, 0)),
            pl.BlockSpec((HD, keys), lambda h: (h, 0)),
            pl.BlockSpec((HD, keys), lambda h: (h, 0)),
            pl.BlockSpec((keys, 1), lambda h: (0, 0)),
            pl.BlockSpec((1, rows), lambda h: (0, 0)),
        ],
        out_specs=[pl.BlockSpec((tall, one), lambda h: (0, 0))] * n_t,
        scratch_shapes=[pltpu.VMEM((2 * heads, rows), F32)],
        compiler_params=pltpu.CompilerParams(vmem_limit_bytes=VMEM_LIMIT),
    )(q, k, v, seg, img)


def combine_kernel(heads, n_t, *refs):
    msgs, (out_ref, stat_ref) = refs[:n_t], refs[n_t:]
    base = heads * HD
    logs = [join(m[base : base + 3 * heads, :], heads) for m in msgs]
    means = [join(m[base + 3 * heads :, :], heads) for m in msgs]
    top = logs[0]
    for x in logs[1:]:
        top = jnp.maximum(top, x)
    shares = [jnp.exp(x - top) for x in logs]
    total = shares[0]
    for x in shares[1:]:
        total = total + x
    shares = [x / total for x in shares]
    mean = shares[0] * means[0]
    for s, x in zip(shares[1:], means[1:]):
        mean = mean + s * x
    stat_ref[:heads, :] = top + jnp.log(total)
    stat_ref[heads:, :] = mean
    for h in range(heads):
        at = slice(h * HD, (h + 1) * HD)
        acc = msgs[0][at, :].astype(F32) * shares[0][h : h + 1, :]
        for s, m in zip(shares[1:], msgs[1:]):
            acc = acc + m[at, :].astype(F32) * s[h : h + 1, :]
        out_ref[at, :] = acc.astype(BF)


def combine(msgs, heads):
    one = msgs[0].shape[1]
    return pl.pallas_call(
        partial(combine_kernel, heads, len(msgs)),
        out_shape=[
            jax.ShapeDtypeStruct((heads * HD, one), BF),
            jax.ShapeDtypeStruct((2 * heads, one), F32),
        ],
        compiler_params=pltpu.CompilerParams(vmem_limit_bytes=VMEM_LIMIT),
    )(*msgs)


def message_kernel(heads, do_ref, out_ref, stat_ref, coef_ref, msg_ref):
    base = heads * HD
    deltas = []
    for h in range(heads):
        at = slice(h * HD, (h + 1) * HD)
        grad = do_ref[at, :].astype(F32)
        deltas.append(jnp.sum(grad * out_ref[at, :].astype(F32), axis=0, keepdims=True))
    msg_ref[:base, :] = do_ref[...]
    delta = jnp.concatenate(deltas, axis=0) - coef_ref[...] * stat_ref[heads:, :]
    msg_ref[base : base + 3 * heads, :] = three(stat_ref[:heads, :])
    msg_ref[base + 3 * heads :, :] = three(delta)


def make_message(do, out, stat, coef, heads):
    return pl.pallas_call(
        partial(message_kernel, heads),
        out_shape=jax.ShapeDtypeStruct((heads * (HD + 6), do.shape[1]), BF),
        compiler_params=pltpu.CompilerParams(vmem_limit_bytes=VMEM_LIMIT),
    )(do, out, stat, coef)


def backward_kernel(heads, n_t, q_ref, k_ref, v_ref, seg_ref, img_ref, coef_ref, *rest):
    grads, stats = rest[:n_t], rest[n_t : 2 * n_t]
    dq_ref, dk_ref, dv_ref, stat = rest[2 * n_t :]
    h = pl.program_id(0)

    @pl.when(h == 0)
    def _():
        rows = q_ref.shape[1] // n_t
        for i in range(n_t):
            cols = slice(i * rows, (i + 1) * rows)
            stat[:heads, cols] = join(stats[i][: 3 * heads, :], heads)
            stat[heads:, cols] = join(stats[i][3 * heads :, :], heads)

    q, k, v = q_ref[...], k_ref[...], v_ref[...]
    grad = jnp.concatenate([g[...] for g in grads], axis=1)
    scores = (
        lax.dot_general(k, q, (((0,), (0,)), ((), ())), preferred_element_type=F32) * SCALE
    )
    allowed = seg_ref[...] == img_ref[...]
    log_total = stat[pl.ds(h, 1)]
    delta = stat[pl.ds(heads + h, 1)]
    prob = jnp.where(allowed, jnp.exp(jnp.where(allowed, scores - log_total, 0.0)), 0.0)
    back_prob = lax.dot_general(v, grad, (((0,), (0,)), ((), ())), preferred_element_type=F32)
    back = (prob * (back_prob - coef_ref[...] * scores - delta)).astype(BF)
    dq_ref[...] = (jnp.dot(k, back, preferred_element_type=F32) * SCALE).astype(BF)
    nt = (((1,), (1,)), ((), ()))
    dk_ref[...] = (lax.dot_general(q, back, nt, preferred_element_type=F32) * SCALE).astype(BF)
    dv_ref[...] = lax.dot_general(
        grad, prob.astype(BF), nt, preferred_element_type=F32
    ).astype(BF)


def attend_backward(q, k, v, seg, img, coef, msgs):
    n_t = len(msgs)
    heads = q.shape[0] // HD
    rows, keys = q.shape[1], k.shape[1]
    one = rows // n_t
    return pl.pallas_call(
        partial(backward_kernel, heads, n_t),
        grid=(heads,),
        out_shape=[
            jax.ShapeDtypeStruct(q.shape, BF),
            jax.ShapeDtypeStruct(k.shape, BF),
            jax.ShapeDtypeStruct(v.shape, BF),
        ],
        in_specs=[
            pl.BlockSpec((HD, rows), lambda h: (h, 0)),
            pl.BlockSpec((HD, keys), lambda h: (h, 0)),
            pl.BlockSpec((HD, keys), lambda h: (h, 0)),
            pl.BlockSpec((keys, 1), lambda h: (0, 0)),
            pl.BlockSpec((1, rows), lambda h: (0, 0)),
            pl.BlockSpec((1, rows), lambda h: (0, 0)),
        ]
        + [pl.BlockSpec((HD, one), lambda h: (h, 0))] * n_t
        + [pl.BlockSpec((6 * heads, one), lambda h: (HD // 6, 0))] * n_t,
        out_specs=[
            pl.BlockSpec((HD, rows), lambda h: (h, 0)),
            pl.BlockSpec((HD, keys), lambda h: (h, 0)),
            pl.BlockSpec((HD, keys), lambda h: (h, 0)),
        ],
        scratch_shapes=[pltpu.VMEM((2 * heads, rows), F32)],
        compiler_params=pltpu.CompilerParams(vmem_limit_bytes=VMEM_LIMIT),
    )(q, k, v, seg, img, coef, *msgs, *msgs)


def norm_parts(values):
    values = values.astype(F32)
    center = values - jnp.mean(values, axis=-1, keepdims=True)
    inv_root = lax.rsqrt(jnp.mean(center * center, axis=-1, keepdims=True) + EPSILON)
    return center * inv_root, inv_root


def norm_backward(grad_rows, normal, inv_root, gain_row):
    scaled = grad_rows * gain_row
    reduced = (
        scaled
        - jnp.mean(scaled, axis=-1, keepdims=True)
        - normal * jnp.mean(scaled * normal, axis=-1, keepdims=True)
    )
    return reduced * inv_root


def gain_shift(grad_rows, normal):
    return [jnp.sum(grad_rows * normal, axis=0), jnp.sum(grad_rows, axis=0)]


def dot(equation, a, b):
    return jnp.einsum(equation, a, b, preferred_element_type=F32)


def local(
    latents,
    features,
    lengths,
    valid_media,
    media_gain,
    media_shift,
    latent_gain,
    latent_shift,
    feed_gain,
    feed_shift,
    query_weight,
    key_value_weight,
    output_weight,
    up_weight,
    down_weight,
    cotangent,
):
    n_t = lax.axis_size("tensor")
    n_dp = lax.axis_size("dp")
    z, p = lax.axis_index("tensor"), lax.axis_index("dp")
    at = jnp.stack([z, p]).astype(jnp.int32)
    latents, features, cotangent = latents[0], features[0], cotangent[0]
    lengths, valid = lengths[0], valid_media[0]
    width = latents.shape[1]
    own_rows, own_patches = latents.shape[0], features.shape[0]
    inner = query_weight.shape[1] * n_t
    heads = inner // HD
    images = lengths.shape[0]

    unit = width // n_dp
    keyval = jnp.moveaxis(share_of(key_value_weight, 0, n_dp), 1, 0)
    kv_pieces, kv_offsets, near = spread(keyval, n_dp, n_t)
    q_share = share_of(query_weight, 0, n_dp).reshape(2, unit // 2, -1)
    q_pieces, q_offsets, near = spread(after(q_share, near), n_dp, n_t)
    latent_blocks = gather_blocks(after(latents, near), n_t)
    out_unit = output_weight.shape[0] // n_dp
    out_share = share_of(output_weight, 0, n_dp)
    out_share = jnp.stack([out_share[:, : width // 2], out_share[:, width // 2 :]])
    o_pieces, o_offsets, near = spread(after(out_share, latent_blocks[1]), n_dp, n_t)
    wk = place(key_value_weight[:, 0], kv_pieces[:1], kv_offsets[:1], [(0, 0)], unit, False, at, n_dp, n_t)
    wv = place(key_value_weight[:, 1], kv_pieces[1:], kv_offsets[1:], [(0, 0)], unit, False, at, n_dp, n_t)
    wq = place(query_weight, q_pieces, q_offsets, [(0, 0), (unit // 2, 0)], unit, False, at, n_dp, n_t)
    wo = place(output_weight, o_pieces, o_offsets, [(0, 0), (0, width // 2)], out_unit, True, at, n_dp, n_t)
    cot_all = jnp.concatenate(gather_blocks(after(cotangent, near), n_t), axis=0)

    count_part = jnp.full((8, 128), jnp.sum(valid).astype(F32))
    count_total = all_sum(count_part, [("dp", n_dp)])[0, 0]

    ends = jnp.sum(
        jnp.where(jnp.arange(images)[:, None] <= jnp.arange(images)[None, :], lengths[:, None], 0),
        axis=0,
    )
    positions = z * own_patches + jnp.arange(own_patches, dtype=jnp.int32)
    segment = jnp.sum((positions[:, None] >= ends[None, :]).astype(jnp.int32), axis=1)
    hit = segment[:, None] == jnp.arange(images, dtype=jnp.int32)[None, :]
    patch_valid = jnp.sum(jnp.where(hit, valid[None, :], 0), axis=1)
    patch_segment = jnp.where(patch_valid > 0, segment, -1)
    own_images = (z * own_rows + jnp.arange(own_rows, dtype=jnp.int32)) // LAT
    key_image = jnp.concatenate([patch_segment, own_images])[:, None]
    block_of = (z - jnp.arange(n_t, dtype=jnp.int32) + n_t) % n_t
    row_index = block_of[:, None] * own_rows + jnp.arange(own_rows, dtype=jnp.int32)[None, :]
    row_image = (row_index // LAT).reshape(1, -1)
    row_valid = jnp.sum(
        jnp.where(row_image.T == jnp.arange(images, dtype=jnp.int32)[None, :], valid[None, :], 0),
        axis=1,
    ).astype(F32)[None, :]

    media_hat, media_root = norm_parts(features)
    media_normed = (media_hat * media_gain + media_shift).astype(BF)
    latent_all = jnp.concatenate(latent_blocks, axis=0)
    latent_hat, latent_root = norm_parts(latent_all)
    latent_normed = (latent_hat * latent_gain + latent_shift).astype(BF)
    key_input = jnp.concatenate([media_normed, latent_normed[:own_rows]], axis=0)
    queries = dot("dh,rd->hr", wq, latent_normed).astype(BF)
    keys = dot("dh,rd->hr", wk, key_input).astype(BF)
    values = dot("dh,rd->hr", wv, key_input).astype(BF)
    sent = attend_forward(queries, keys, values, key_image, row_image, n_t)
    got = [sent[0]] + [rotate(sent[k], n_t, -k) for k in range(1, n_t)]
    attended, stat = combine(got, heads)
    entropy = stat[:heads] - stat[heads:]
    own_valid = row_valid[:, :own_rows]
    penalty_part = jnp.sum(entropy * own_valid)

    latent_own = latents.astype(F32)
    middle = latent_own + dot("hr,hd->rd", attended, wo)
    feed_hat, feed_root = norm_parts(middle)
    feed_normed = (feed_hat * feed_gain + feed_shift).astype(BF)
    feed_all = jnp.concatenate(gather_blocks(feed_normed, n_t), axis=0)
    hidden = dot("rd,df->rf", feed_all, up_weight)
    cdf = 0.5 * (1.0 + lax.erf(hidden * (0.5**0.5)))
    slope = cdf + hidden * jnp.exp(-0.5 * hidden * hidden) * (0.5 / jnp.pi) ** 0.5
    activation = (hidden * cdf).astype(BF)
    back_activation = dot("rd,fd->rf", cot_all, down_weight)
    back_hidden = (back_activation * slope).astype(BF)
    back_terms = dot("rf,df->rd", back_hidden, up_weight).astype(BF)
    back_blocks = [back_terms[k * own_rows : (k + 1) * own_rows] for k in range(n_t)]
    down_keep, down_send = gradient(cot_all.T, activation, True, at, n_dp)
    up_keep, up_send = gradient(feed_all.T, back_hidden, True, at, n_dp)
    down_got = swap(down_send, "dp", n_dp, 0)
    up_got = swap(up_send, "dp", n_dp, 0)
    back_feed = after(scatter_blocks(back_blocks, n_t), down_got, up_got)
    orders = bit_orders(n_dp)
    feed_terms = dot("rf,fd->rd", activation, down_weight).astype(BF)

    back_middle = cotangent.astype(F32) + norm_backward(back_feed, feed_hat, feed_root, feed_gain)
    back_branch = back_middle.astype(BF)
    back_attended = dot("hd,rd->hr", wo, back_branch).astype(BF)
    own_coef = own_valid / count_total
    message = make_message(back_attended, attended, stat, own_coef, heads)
    down_keep, down_got = reduce_step(down_keep, down_got, orders[0], 0, n_dp)
    up_keep, up_got = reduce_step(up_keep, up_got, orders[1], 0, n_dp)
    messages = gather_blocks(message, n_t)
    feed_terms = after(feed_terms, messages[1])
    messages = [after(m, down_got, up_got) if k else m for k, m in enumerate(messages)]
    result = middle + scatter_blocks(
        [feed_terms[k * own_rows : (k + 1) * own_rows] for k in range(n_t)], n_t
    )
    back_q, back_k, back_v = attend_backward(
        queries, keys, values, key_image, row_image, row_valid / count_total, messages
    )
    for i in range(1, len(orders[0])):
        down_keep, down_got = reduce_step(down_keep, down_got, orders[0], i, n_dp)
        up_keep, up_got = reduce_step(up_keep, up_got, orders[1], i, n_dp)
    down_share = down_keep[0].astype(F32) + down_got[0].astype(F32)
    up_share = up_keep[0].astype(F32) + up_got[0].astype(F32)

    def halves(keep, send):
        got = swap(send, "dp", n_dp, 0)
        cut = inner // 2
        one = reduce_outer(keep[..., :cut], got[..., :cut], orders[0], n_dp)
        two = reduce_outer(keep[..., cut:], got[..., cut:], orders[1], n_dp)
        return tuple(jnp.concatenate([x, y], axis=1) for x, y in zip(one, two))

    out_terms = halves(*gradient(back_branch.T, attended, False, at, n_dp))
    back_q, back_k, back_v = lax.optimization_barrier(
        (back_q, back_k, back_v, down_got, up_got)
    )[:3]
    v_keep, v_send = gradient(key_input.T, back_v, False, at, n_dp)
    k_keep, k_send = gradient(key_input.T, back_k, False, at, n_dp)
    value_terms = reduce_outer(v_keep, swap(v_send, "dp", n_dp, 0), orders[0], n_dp)
    key_terms = reduce_outer(k_keep, swap(k_send, "dp", n_dp, 0), orders[1], n_dp)
    query_terms = halves(*gradient(latent_normed.T, back_q, False, at, n_dp))
    back_inputs = dot("hr,dh->rd", back_k, wk) + dot("hr,dh->rd", back_v, wv)
    back_media = back_inputs[:own_patches]
    latent_terms = dot("hr,dh->rd", back_q, wq)
    latent_terms = jnp.concatenate(
        [latent_terms[:own_rows] + back_inputs[own_patches:], latent_terms[own_rows:]], axis=0
    )
    terms_low = latent_terms.astype(BF)
    back_latent = scatter_blocks(
        [terms_low[k * own_rows : (k + 1) * own_rows] for k in range(n_t)], n_t
    )
    features_grad = norm_backward(back_media, media_hat, media_root, media_gain)
    latents_grad = back_middle + norm_backward(
        back_latent, latent_hat[:own_rows], latent_root[:own_rows], latent_gain
    )

    grad_o = scatter_blocks(tensor_blocks([out_terms], at, n_t), n_t)[0]
    grad_kv = scatter_blocks(tensor_blocks([key_terms, value_terms], at, n_t), n_t)
    grad_q = scatter_blocks(tensor_blocks([query_terms], at, n_t), n_t)[0]

    sums = (
        gain_shift(back_media, media_hat)
        + gain_shift(latent_terms, latent_hat)
        + gain_shift(back_feed, feed_hat)
    )
    sums = jnp.stack(sums + [jnp.full((width,), penalty_part)] * 2)
    sums = all_sum(sums, [("dp", n_dp), ("tensor", n_t)])
    penalty = sums[6, 0] / count_total
    share = width // (n_dp * n_t)
    mine = lax.dynamic_index_in_dim(
        sums.reshape(8, n_dp * n_t, share), p * n_t + z, 1, keepdims=False
    )
    return (
        result.astype(BF)[None],
        penalty,
        latents_grad[None],
        features_grad[None],
        mine[0],
        mine[1],
        mine[2],
        mine[3],
        mine[4],
        mine[5],
        grad_q,
        jnp.moveaxis(grad_kv, 0, 1),
        grad_o.T,
        up_share,
        down_share.T,
    )


def solution(mesh):
    return jax.shard_map(
        local,
        mesh=mesh,
        in_specs=(
            P("dp", "tensor", None),
            P("dp", "tensor", None),
            P("dp", None),
            P("dp", None),
            P(),
            P(),
            P(),
            P(),
            P(),
            P(),
            P(None, "tensor"),
            P(None, None, "tensor"),
            P("tensor", None),
            P(None, "tensor"),
            P("tensor", None),
            P("dp", "tensor", None),
        ),
        out_specs=(
            P("dp", "tensor", None),
            P(),
            P("dp", "tensor", None),
            P("dp", "tensor", None),
            P(("dp", "tensor")),
            P(("dp", "tensor")),
            P(("dp", "tensor")),
            P(("dp", "tensor")),
            P(("dp", "tensor")),
            P(("dp", "tensor")),
            P("dp", "tensor"),
            P("dp", None, "tensor"),
            P("tensor", "dp"),
            P("dp", "tensor"),
            P("tensor", "dp"),
        ),
        check_vma=False,
    )
```

```python
from functools import partial

import jax
import jax.numpy as jnp
from jax import lax
from jax.experimental import pallas as pl
from jax.experimental.pallas import tpu as pltpu
from jax.sharding import PartitionSpec as P

HD = 96
LAT = 64
EPSILON = 1e-05
NEGATIVE = -1e30
SCALE = HD ** (-0.5)
BF = jnp.bfloat16
F32 = jnp.float32
VMEM_LIMIT = 48 * 1024 * 1024


def rotate(x, count, shift):
    return lax.ppermute(x, "tensor", [(i, (i + shift) % count) for i in range(count)])


def after(x, *done):
    many = isinstance(x, (list, tuple))
    held = lax.optimization_barrier((*x, *done) if many else (x, *done))
    return list(held[: len(x)]) if many else held[0]


def gather_blocks(x, count):
    return [x] + [rotate(x, count, k) for k in range(1, count)]


def send_blocks(blocks, count):
    return [blocks[0]] + [rotate(blocks[k], count, -k) for k in range(1, count)]


def scatter_blocks(blocks, count):
    return add_up(send_blocks(blocks, count))


def partner(x, axis, count, offset):
    return lax.ppermute(x, axis, [(i, i ^ offset) for i in range(count)])


def bits_of(count):
    return count.bit_length() - 1


def gradient_kernel(natural, n_dp, at_ref, xt_ref, y_ref, keep_ref, send_ref, total_ref):
    dims = (((1,), (0,)), ((), ())) if natural else (((1,), (1,)), ((), ()))
    total_ref[...] = lax.dot_general(xt_ref[...], y_ref[...], dims, preferred_element_type=F32)
    p, unit = at_ref[1], keep_ref.shape[1]
    for i in range(n_dp // 2):
        for odd, out in enumerate((keep_ref, send_ref)):
            first = pl.multiple_of((p ^ (2 * i + odd)) * unit, unit)
            out[i] = total_ref[pl.ds(first, unit), :].astype(BF)


def gradient(xt, y, natural, at, n_dp):
    width, rows = xt.shape
    unit = width // n_dp
    wide = y.shape[1] if natural else y.shape[0]
    step = wide // 3
    half = n_dp // 2
    if natural:
        y_spec = pl.BlockSpec((rows, step), lambda i: (0, i))
    else:
        y_spec = pl.BlockSpec((step, rows), lambda i: (i, 0))
    return pl.pallas_call(
        partial(gradient_kernel, natural, n_dp),
        grid=(3,),
        in_specs=[
            pl.BlockSpec(memory_space=pltpu.SMEM),
            pl.BlockSpec((width, rows), lambda i: (0, 0)),
            y_spec,
        ],
        out_specs=[pl.BlockSpec((half, unit, step), lambda i: (0, 0, i))] * 2,
        out_shape=[jax.ShapeDtypeStruct((half, unit, wide), BF)] * 2,
        scratch_shapes=[pltpu.VMEM((width, step), F32)],
        compiler_params=pltpu.CompilerParams(vmem_limit_bytes=VMEM_LIMIT),
    )(at, xt, y)


def bit_orders(count):
    outer = list(range(1, bits_of(count)))
    half = (len(outer) + 1) // 2
    return outer, outer[half:] + outer[:half]


def cut_kernel(widths, *refs):
    ins, (keep_ref, send_ref) = refs[:-2], refs[-2:]
    start = 0
    for i, wide in enumerate(widths):
        lanes = slice(start, start + wide)
        keep_a, got_a, keep_b, got_b = ins[4 * i : 4 * i + 4]
        keep_ref[:, :, lanes] = (keep_a[...].astype(F32) + got_a[...].astype(F32)).astype(BF)
        send_ref[:, :, lanes] = (keep_b[...].astype(F32) + got_b[...].astype(F32)).astype(BF)
        start += wide


def reduce_cut(parts, order, step, n_dp):
    left = [b for b in range(bits_of(n_dp) - 1, 0, -1) if b not in order[:step]]
    low = 1 << (len(left) - left.index(order[step]) - 1)
    count, rows, _ = parts[0][0].shape
    widths, specs, flat = [], [], []
    for keep, got, half in parts:
        wide = keep.shape[2] if half is None else keep.shape[2] // 2

        def at(bit, wide=wide, lane=half or 0):
            return pl.BlockSpec(
                (1, rows, wide), lambda i: (i // low * (2 * low) + bit * low + i % low, 0, lane)
            )

        widths.append(wide)
        specs += [at(0), at(0), at(1), at(1)]
        flat += [keep, got, keep, got]
    total = sum(widths)
    return pl.pallas_call(
        partial(cut_kernel, widths),
        grid=(count // 2,),
        in_specs=specs,
        out_specs=[pl.BlockSpec((1, rows, total), lambda i: (i, 0, 0))] * 2,
        out_shape=[jax.ShapeDtypeStruct((count // 2, rows, total), BF)] * 2,
        compiler_params=pltpu.CompilerParams(vmem_limit_bytes=VMEM_LIMIT),
    )(*flat)


def first_cut(one, two, split, orders, n_dp):
    out = []
    for h, full in enumerate((one, two)):
        parts = [(*full, None)] if full else []
        parts += [(*split, h)] if split else []
        out.append(reduce_cut(parts, orders[h], 0, n_dp))
    return out


def next_cut(pair, orders, step, n_dp):
    return [reduce_cut([(*x, None)], order, step, n_dp) for x, order in zip(pair, orders)]


def cross(pair, orders, step, n_dp):
    return [
        (keep, partner(send, "dp", n_dp, 1 << order[step])) for (keep, send), order in zip(pair, orders)
    ]


def add_up(terms):
    total = terms[0].astype(F32)
    for term in terms[1:]:
        total = total + term.astype(F32)
    return total


def blocks_kernel(n_t, weights, at_ref, *refs):
    (a_keep, a_got, b_keep, b_got), outs = refs[:4], refs[4:]
    pairs = (a_keep, a_got), (b_keep, b_got)
    z = at_ref[0]
    columns = outs[0].shape[-1]
    half = n_t // 2

    def piece(which, lane):
        lanes = pl.ds(pl.multiple_of(lane, columns), columns)
        keep, got = pairs[which]
        return keep[0, :, lanes].astype(F32) + got[0, :, lanes].astype(F32)

    for k in range(n_t):
        block = lax.rem(z - k + n_t, n_t)
        for m, which in enumerate(weights):
            if which is None:
                lane = (a_keep.shape[2] - columns * half) + lax.rem(block, half) * columns
                value = jnp.where(block >= half, piece(1, lane), piece(0, lane))
            else:
                value = piece(which, block * columns)
            outs[k][m] = value.astype(outs[k].dtype)


def tensor_blocks(pair, weights, columns, at, n_t):
    flat = [x for terms in pair for x in terms]
    rows = flat[0].shape[1]
    return pl.pallas_call(
        partial(blocks_kernel, n_t, weights),
        in_specs=[pl.BlockSpec(memory_space=pltpu.SMEM)]
        + [pl.BlockSpec(memory_space=pltpu.VMEM)] * len(flat),
        out_shape=[
            jax.ShapeDtypeStruct((len(weights), rows, columns // n_t), F32 if k == 0 else BF)
            for k in range(n_t)
        ],
        compiler_params=pltpu.CompilerParams(vmem_limit_bytes=VMEM_LIMIT),
    )(at, *flat)


def all_sum(x, axes):
    for axis, count in axes:
        for bit in range(bits_of(count)):
            x = x + partner(x, axis, count, 1 << bit)
    return x


def place_kernel(n_t, unit, z_rows, z_cols, offsets, parts, at_ref, own_ref, *refs):
    out_ref = refs[-1]
    z, p = at_ref[0], at_ref[1]
    rows, cols = own_ref.shape
    if z_rows:
        out_ref[pl.ds(pl.multiple_of(z * z_rows, z_rows), rows), :] = own_ref[...]
    else:
        out_ref[:, pl.ds(pl.multiple_of(z * z_cols, z_cols), cols)] = own_ref[...]
    for k in range(1, n_t):
        shard = lax.rem(z - k + n_t, n_t)
        for which, first, height, row_at, col_at in parts:
            for odd in range(2):
                src = refs[2 * which + odd]
                wide = src.shape[3]
                for i, off in enumerate(offsets[which]):
                    base = shard * z_rows + (p ^ (off ^ odd)) * unit + row_at
                    where = pl.ds(pl.multiple_of(base, 16), height)
                    if z_cols:
                        at = pl.ds(pl.multiple_of(shard * z_cols, z_cols), wide)
                    else:
                        at = slice(col_at, col_at + wide)
                    out_ref[where, at] = src[i, k - 1, first : first + height, :]


def reorder(x, places):
    return jnp.stack([lax.dynamic_index_in_dim(x, i, 0, keepdims=False) for i in places])


def project_kernel(place_kernel, count, at_ref, x_ref, *refs):
    place_kernel(at_ref, *refs[:-2])
    weight_ref, out_ref, turned_ref = refs[-3:]
    turned_ref[...] = x_ref[...].T
    step = weight_ref.shape[1] // count
    for c in range(count):
        cols = slice(c * step, (c + 1) * step)
        block = jnp.dot(x_ref[...], weight_ref[:, cols], preferred_element_type=F32)
        out_ref[cols, :] = block.T.astype(BF)


def place(own, pieces, offsets, parts, unit, by_rows, at, n_dp, n_t, x=None):
    rows, cols = own.shape
    shape = (n_t * rows, cols) if by_rows else (rows, n_t * cols)
    if unit % 16 or any(part[2] % 16 for part in parts):
        z, p = at[0], at[1]
        across = []
        for which, first, height, _, _ in parts:
            ordered = [None] * n_dp
            for i, off in enumerate(offsets[which]):
                for odd in range(2):
                    ordered[off ^ odd] = pieces[which][odd][i, :, first : first + height]
            across.append(reorder(jnp.stack(ordered), [p ^ d for d in range(n_dp)]))
        whole = jnp.concatenate(across, axis=3 if by_rows else 2).transpose(1, 0, 2, 3)
        whole = whole.reshape((n_t - 1, rows, cols))
        whole = jnp.concatenate([own[None], whole], axis=0)
        whole = reorder(whole, [(z - k + n_t) % n_t for k in range(n_t)])
        whole = whole.reshape(shape) if by_rows else whole.transpose(1, 0, 2).reshape(shape)
        return whole if x is None else (whole, dot("dh,rd->hr", whole, x).astype(BF), x.T)
    flat = [x for pair in pieces for x in pair]
    kernel = partial(
        place_kernel, n_t, unit, rows if by_rows else 0, 0 if by_rows else cols, offsets, parts
    )
    out = jax.ShapeDtypeStruct(shape, own.dtype)
    if x is None:
        first, outs = [], out
    else:
        kernel, first = partial(project_kernel, kernel, n_t), [x]
        outs = [out] + [jax.ShapeDtypeStruct((n, x.shape[0]), BF) for n in (shape[1], x.shape[1])]
    ins = [*first, own, *flat]
    return pl.pallas_call(
        kernel,
        out_shape=outs,
        in_specs=[pl.BlockSpec(memory_space=pltpu.SMEM)]
        + [pl.BlockSpec(memory_space=pltpu.VMEM)] * len(ins),
        compiler_params=pltpu.CompilerParams(vmem_limit_bytes=VMEM_LIMIT),
    )(at, *ins)


def rotations(x, count):
    return [rotate(x, count, k) for k in range(1, count)]


def widen(one, two, step, orders, n_dp):
    return [
        jnp.concatenate([x, partner(x, "dp", n_dp, 1 << order[step])], axis=0)
        for x, order in zip((one, two), orders)
    ]


def widen_offsets(order):
    offsets = [0]
    for bit in order:
        offsets = offsets + [o ^ (1 << bit) for o in offsets]
    return offsets


def cores(one, two, n_dp):
    return [(x, partner(x, "dp", n_dp, 1)) for x in (one, two)]


def share_of(x, axis, count):
    size = x.shape[axis] // count
    return lax.dynamic_slice_in_dim(x, lax.axis_index("dp") * size, size, axis)


def three(x):
    high = x.astype(BF)
    left = x - high.astype(F32)
    middle = left.astype(BF)
    low = (left - middle.astype(F32)).astype(BF)
    return jnp.concatenate([high, middle, low], axis=0)


def join(x, count):
    x = x.astype(F32)
    return x[:count] + x[count : 2 * count] + x[2 * count :]


def forward_kernel(heads, n_t, q_ref, k_ref, v_ref, seg_ref, img_ref, *rest):
    msgs, stat = rest[:n_t], rest[n_t]
    h = pl.program_id(0)
    rows = q_ref.shape[1] // n_t
    scores = (
        lax.dot_general(
            k_ref[...], q_ref[...], (((0,), (0,)), ((), ())), preferred_element_type=F32
        )
        * SCALE
    )
    allowed = seg_ref[...] == img_ref[...]
    masked = jnp.where(allowed, scores, NEGATIVE)
    top = jnp.max(masked, axis=0, keepdims=True)
    weight = jnp.where(allowed, jnp.exp(masked - top), 0.0)
    total = jnp.sum(weight, axis=0, keepdims=True)
    mean = jnp.sum(weight * scores, axis=0, keepdims=True)
    some = total > 0.0
    inverse = jnp.where(some, 1.0 / jnp.where(some, total, 1.0), 0.0)
    out = jnp.dot(v_ref[...], weight.astype(BF), preferred_element_type=F32) * inverse
    stat[pl.ds(h, 1)] = jnp.where(some, top + jnp.log(jnp.where(some, total, 1.0)), NEGATIVE)
    stat[pl.ds(heads + h, 1)] = mean * inverse
    at = pl.ds(pl.multiple_of(h * HD, HD), HD)
    for k in range(n_t):
        msgs[k][at, :] = out[:, k * rows : (k + 1) * rows].astype(BF)

    @pl.when(h == heads - 1)
    def _():
        for k in range(n_t):
            cols = slice(k * rows, (k + 1) * rows)
            msgs[k][heads * HD : heads * (HD + 3), :] = three(stat[:heads, cols])
            msgs[k][heads * (HD + 3) :, :] = three(stat[heads:, cols])


def attend_forward(q, k, v, seg, img, n_t):
    heads = q.shape[0] // HD
    rows, keys = q.shape[1], k.shape[1]
    one = rows // n_t
    tall = heads * (HD + 6)
    return pl.pallas_call(
        partial(forward_kernel, heads, n_t),
        grid=(heads,),
        out_shape=[jax.ShapeDtypeStruct((tall, one), BF)] * n_t,
        in_specs=[
            pl.BlockSpec((HD, rows), lambda h: (h, 0)),
            pl.BlockSpec((HD, keys), lambda h: (h, 0)),
            pl.BlockSpec((HD, keys), lambda h: (h, 0)),
            pl.BlockSpec((keys, 1), lambda h: (0, 0)),
            pl.BlockSpec((1, rows), lambda h: (0, 0)),
        ],
        out_specs=[pl.BlockSpec((tall, one), lambda h: (0, 0))] * n_t,
        scratch_shapes=[pltpu.VMEM((2 * heads, rows), F32)],
        compiler_params=pltpu.CompilerParams(vmem_limit_bytes=VMEM_LIMIT),
    )(q, k, v, seg, img)


def combine_kernel(heads, n_t, *refs):
    msgs, (out_ref, stat_ref) = refs[:n_t], refs[n_t:]
    base = heads * HD
    logs = [join(m[base : base + 3 * heads, :], heads) for m in msgs]
    means = [join(m[base + 3 * heads :, :], heads) for m in msgs]
    top = logs[0]
    for x in logs[1:]:
        top = jnp.maximum(top, x)
    shares = [jnp.exp(x - top) for x in logs]
    total = shares[0]
    for x in shares[1:]:
        total = total + x
    shares = [x / total for x in shares]
    mean = shares[0] * means[0]
    for s, x in zip(shares[1:], means[1:]):
        mean = mean + s * x
    stat_ref[:heads, :] = top + jnp.log(total)
    stat_ref[heads:, :] = mean
    for h in range(heads):
        at = slice(h * HD, (h + 1) * HD)
        acc = msgs[0][at, :].astype(F32) * shares[0][h : h + 1, :]
        for s, m in zip(shares[1:], msgs[1:]):
            acc = acc + m[at, :].astype(F32) * s[h : h + 1, :]
        out_ref[at, :] = acc.astype(BF)


def combine(msgs, heads):
    one = msgs[0].shape[1]
    return pl.pallas_call(
        partial(combine_kernel, heads, len(msgs)),
        out_shape=[
            jax.ShapeDtypeStruct((heads * HD, one), BF),
            jax.ShapeDtypeStruct((2 * heads, one), F32),
        ],
        compiler_params=pltpu.CompilerParams(vmem_limit_bytes=VMEM_LIMIT),
    )(*msgs)


def message_kernel(heads, do_ref, out_ref, stat_ref, coef_ref, msg_ref):
    base = heads * HD
    deltas = []
    for h in range(heads):
        at = slice(h * HD, (h + 1) * HD)
        grad = do_ref[at, :].astype(F32)
        deltas.append(jnp.sum(grad * out_ref[at, :].astype(F32), axis=0, keepdims=True))
    msg_ref[:base, :] = do_ref[...]
    delta = jnp.concatenate(deltas, axis=0) - coef_ref[...] * stat_ref[heads:, :]
    msg_ref[base : base + 3 * heads, :] = three(stat_ref[:heads, :])
    msg_ref[base + 3 * heads :, :] = three(delta)


def make_message(do, out, stat, coef, heads):
    return pl.pallas_call(
        partial(message_kernel, heads),
        out_shape=jax.ShapeDtypeStruct((heads * (HD + 6), do.shape[1]), BF),
        compiler_params=pltpu.CompilerParams(vmem_limit_bytes=VMEM_LIMIT),
    )(do, out, stat, coef)


def backward_kernel(heads, n_t, q_ref, k_ref, v_ref, seg_ref, img_ref, coef_ref, *rest):
    grads, stats = rest[:n_t], rest[n_t : 2 * n_t]
    dq_ref, dk_ref, dv_ref, stat = rest[2 * n_t :]
    h = pl.program_id(0)

    @pl.when(h == 0)
    def _():
        rows = q_ref.shape[1] // n_t
        for i in range(n_t):
            cols = slice(i * rows, (i + 1) * rows)
            stat[:heads, cols] = join(stats[i][: 3 * heads, :], heads)
            stat[heads:, cols] = join(stats[i][3 * heads :, :], heads)

    q, k, v = q_ref[...], k_ref[...], v_ref[...]
    grad = jnp.concatenate([g[...] for g in grads], axis=1)
    scores = (
        lax.dot_general(k, q, (((0,), (0,)), ((), ())), preferred_element_type=F32) * SCALE
    )
    allowed = seg_ref[...] == img_ref[...]
    log_total = stat[pl.ds(h, 1)]
    delta = stat[pl.ds(heads + h, 1)]
    prob = jnp.where(allowed, jnp.exp(jnp.where(allowed, scores - log_total, 0.0)), 0.0)
    back_prob = lax.dot_general(v, grad, (((0,), (0,)), ((), ())), preferred_element_type=F32)
    back = (prob * (back_prob - coef_ref[...] * scores - delta)).astype(BF)
    dq_ref[...] = (jnp.dot(k, back, preferred_element_type=F32) * SCALE).astype(BF)
    nt = (((1,), (1,)), ((), ()))
    dk_ref[...] = (lax.dot_general(q, back, nt, preferred_element_type=F32) * SCALE).astype(BF)
    dv_ref[...] = lax.dot_general(
        grad, prob.astype(BF), nt, preferred_element_type=F32
    ).astype(BF)


def attend_backward(q, k, v, seg, img, coef, msgs):
    n_t = len(msgs)
    heads = q.shape[0] // HD
    rows, keys = q.shape[1], k.shape[1]
    one = rows // n_t
    return pl.pallas_call(
        partial(backward_kernel, heads, n_t),
        grid=(heads,),
        out_shape=[
            jax.ShapeDtypeStruct(q.shape, BF),
            jax.ShapeDtypeStruct(k.shape, BF),
            jax.ShapeDtypeStruct(v.shape, BF),
        ],
        in_specs=[
            pl.BlockSpec((HD, rows), lambda h: (h, 0)),
            pl.BlockSpec((HD, keys), lambda h: (h, 0)),
            pl.BlockSpec((HD, keys), lambda h: (h, 0)),
            pl.BlockSpec((keys, 1), lambda h: (0, 0)),
            pl.BlockSpec((1, rows), lambda h: (0, 0)),
            pl.BlockSpec((1, rows), lambda h: (0, 0)),
        ]
        + [pl.BlockSpec((HD, one), lambda h: (h, 0))] * n_t
        + [pl.BlockSpec((6 * heads, one), lambda h: (HD // 6, 0))] * n_t,
        out_specs=[
            pl.BlockSpec((HD, rows), lambda h: (h, 0)),
            pl.BlockSpec((HD, keys), lambda h: (h, 0)),
            pl.BlockSpec((HD, keys), lambda h: (h, 0)),
        ],
        scratch_shapes=[pltpu.VMEM((2 * heads, rows), F32)],
        compiler_params=pltpu.CompilerParams(vmem_limit_bytes=VMEM_LIMIT),
        cost_estimate=pl.CostEstimate(
            flops=60 * heads * HD * rows * keys,
            bytes_accessed=60 * 1024 * 1024,
            transcendentals=heads * rows * keys,
        ),
    )(q, k, v, seg, img, coef, *msgs, *msgs)


def norm_parts(values):
    values = values.astype(F32)
    center = values - jnp.mean(values, axis=-1, keepdims=True)
    inv_root = lax.rsqrt(jnp.mean(center * center, axis=-1, keepdims=True) + EPSILON)
    return center * inv_root, inv_root


def norm_backward(grad_rows, normal, inv_root, gain_row):
    scaled = grad_rows * gain_row
    reduced = (
        scaled
        - jnp.mean(scaled, axis=-1, keepdims=True)
        - normal * jnp.mean(scaled * normal, axis=-1, keepdims=True)
    )
    return reduced * inv_root


def gain_shift(grad_rows, normal):
    return [jnp.sum(grad_rows * normal, axis=0), jnp.sum(grad_rows, axis=0)]


def rows_back(grads, weights):
    total = None
    for grad, weight in zip(grads, weights):
        term = lax.dot_general(grad, weight, (((0,), (1,)), ((), ())), preferred_element_type=F32)
        total = term if total is None else total + term
    return total


def media_back_kernel(dk_ref, dv_ref, wk_ref, wv_ref, x_ref, gain_ref, out_ref, sums_ref):
    back = rows_back((dk_ref[...], dv_ref[...]), (wk_ref[...], wv_ref[...]))
    normal, root = norm_parts(x_ref[...])
    out_ref[...] = norm_backward(back, normal, root, gain_ref[...])

    @pl.when(pl.program_id(0) == 0)
    def _():
        sums_ref[...] = jnp.zeros_like(sums_ref)

    sums_ref[0:1] += jnp.sum(back * normal, axis=0, keepdims=True)
    sums_ref[1:2] += jnp.sum(back, axis=0, keepdims=True)


def media_back(back_k, back_v, wk, wv, features, gain, block):
    rows, width = features.shape
    inner = back_k.shape[0]
    whole = pl.BlockSpec((width, inner), lambda i: (0, 0))
    return pl.pallas_call(
        media_back_kernel,
        grid=(rows // block,),
        in_specs=[pl.BlockSpec((inner, block), lambda i: (0, i))] * 2
        + [whole] * 2
        + [pl.BlockSpec((block, width), lambda i: (i, 0)), pl.BlockSpec((1, width), lambda i: (0, 0))],
        out_specs=[
            pl.BlockSpec((block, width), lambda i: (i, 0)),
            pl.BlockSpec((8, width), lambda i: (0, 0)),
        ],
        out_shape=[
            jax.ShapeDtypeStruct((rows, width), F32),
            jax.ShapeDtypeStruct((8, width), F32),
        ],
        compiler_params=pltpu.CompilerParams(vmem_limit_bytes=VMEM_LIMIT),
    )(back_k, back_v, wk, wv, features, gain[None])


def latent_back_kernel(n_t, dq_ref, dk_ref, dv_ref, wq_ref, wk_ref, wv_ref, *refs):
    xs, outs, sums_ref = refs[:n_t], refs[n_t:-1], refs[-1]
    rows = xs[0].shape[0]
    gain_sum = shift_sum = None
    total = rows_back((dq_ref[...],), (wq_ref[...],))
    own = rows_back((dk_ref[...], dv_ref[...]), (wk_ref[...], wv_ref[...]))
    for k in range(n_t):
        back = total[k * rows : (k + 1) * rows]
        if k == 0:
            back = back + own
        outs[k][...] = back.astype(outs[k].dtype)
        normal, _ = norm_parts(xs[k][...])
        gain_part = jnp.sum(back * normal, axis=0, keepdims=True)
        shift_part = jnp.sum(back, axis=0, keepdims=True)
        gain_sum = gain_part if gain_sum is None else gain_sum + gain_part
        shift_sum = shift_part if shift_sum is None else shift_sum + shift_part
    sums_ref[...] = jnp.zeros_like(sums_ref)
    sums_ref[0:1] = gain_sum
    sums_ref[1:2] = shift_sum


def latent_back(back_q, back_k, back_v, wq, wk, wv, blocks):
    n_t = len(blocks)
    rows, width = blocks[0].shape
    inner, keys = back_k.shape
    tail = pl.BlockSpec((inner, rows), lambda i: (0, keys // rows - 1))
    whole = pl.BlockSpec((width, inner), lambda i: (0, 0))
    return pl.pallas_call(
        partial(latent_back_kernel, n_t),
        grid=(1,),
        in_specs=[pl.BlockSpec(back_q.shape, lambda i: (0, 0)), tail, tail, whole, whole, whole]
        + [pl.BlockSpec((rows, width), lambda i: (0, 0))] * n_t,
        out_specs=[pl.BlockSpec((rows, width), lambda i: (0, 0))] * n_t
        + [pl.BlockSpec((8, width), lambda i: (0, 0))],
        out_shape=[jax.ShapeDtypeStruct((rows, width), BF if k else F32) for k in range(n_t)]
        + [jax.ShapeDtypeStruct((8, width), F32)],
        compiler_params=pltpu.CompilerParams(vmem_limit_bytes=VMEM_LIMIT),
    )(back_q, back_k, back_v, wq, wk, wv, *blocks)


def blocks_of_product_kernel(n_t, a_ref, b_ref, *outs):
    total = jnp.dot(a_ref[...], b_ref[...], preferred_element_type=F32)
    rows = outs[0].shape[0]
    for k in range(n_t):
        outs[k][...] = total[k * rows : (k + 1) * rows].astype(outs[k].dtype)


def blocks_of_product(a, b, n_t):
    shape = a.shape[0] // n_t, b.shape[1]
    return list(
        pl.pallas_call(
            partial(blocks_of_product_kernel, n_t),
            out_shape=[jax.ShapeDtypeStruct(shape, BF if k else F32) for k in range(n_t)],
            compiler_params=pltpu.CompilerParams(vmem_limit_bytes=VMEM_LIMIT),
        )(a, b)
    )


def dot(equation, a, b):
    return jnp.einsum(equation, a, b, preferred_element_type=F32)


def local(
    latents,
    features,
    lengths,
    valid_media,
    media_gain,
    media_shift,
    latent_gain,
    latent_shift,
    feed_gain,
    feed_shift,
    query_weight,
    key_value_weight,
    output_weight,
    up_weight,
    down_weight,
    cotangent,
):
    n_t = lax.axis_size("tensor")
    n_dp = lax.axis_size("dp")
    z, p = lax.axis_index("tensor"), lax.axis_index("dp")
    at = jnp.stack([z, p]).astype(jnp.int32)
    latents, features, cotangent = latents[0], features[0], cotangent[0]
    lengths, valid = lengths[0], valid_media[0]
    width = latents.shape[1]
    own_rows, own_patches = latents.shape[0], features.shape[0]
    inner = query_weight.shape[1] * n_t
    heads = inner // HD
    images = lengths.shape[0]

    count_part = jnp.full((8, 128), jnp.sum(valid).astype(F32))
    count_total = all_sum(count_part, [("dp", n_dp)])[0, 0]

    ends = jnp.sum(
        jnp.where(jnp.arange(images)[:, None] <= jnp.arange(images)[None, :], lengths[:, None], 0),
        axis=0,
    )
    positions = z * own_patches + jnp.arange(own_patches, dtype=jnp.int32)
    segment = jnp.sum((positions[:, None] >= ends[None, :]).astype(jnp.int32), axis=1)
    hit = segment[:, None] == jnp.arange(images, dtype=jnp.int32)[None, :]
    patch_valid = jnp.sum(jnp.where(hit, valid[None, :], 0), axis=1)
    patch_segment = jnp.where(patch_valid > 0, segment, -1)
    own_images = (z * own_rows + jnp.arange(own_rows, dtype=jnp.int32)) // LAT
    key_image = jnp.concatenate([patch_segment, own_images])[:, None]
    block_of = (z - jnp.arange(n_t, dtype=jnp.int32) + n_t) % n_t
    row_index = block_of[:, None] * own_rows + jnp.arange(own_rows, dtype=jnp.int32)[None, :]
    row_image = (row_index // LAT).reshape(1, -1)
    row_valid = jnp.sum(
        jnp.where(row_image.T == jnp.arange(images, dtype=jnp.int32)[None, :], valid[None, :], 0),
        axis=1,
    ).astype(F32)[None, :]

    orders = bit_orders(n_dp)
    steps = range(len(orders[0]))
    offsets = [widen_offsets(order) for order in orders]
    unit, part = width // n_dp, query_weight.shape[1]
    keyval = jnp.moveaxis(share_of(key_value_weight, 0, n_dp), 1, 0)
    kv_z = rotations(keyval, n_t)
    media_hat, media_root = norm_parts(features)
    media_normed = (media_hat * media_gain + media_shift).astype(BF)
    own_hat, own_root = norm_parts(latents)
    own_normed = (own_hat * latent_gain + latent_shift).astype(BF)
    key_input = jnp.concatenate([media_normed, own_normed], axis=0)
    kv_own = [key_value_weight[:, 0], key_value_weight[:, 1]]
    *kv_z, key_input, count_total, k_own, v_own = after([*kv_z, key_input, count_total, *kv_own])
    q_share = share_of(query_weight, 0, n_dp).reshape(2, unit // 2, part)
    o_share = share_of(output_weight, 0, n_dp)
    o_unit = o_share.shape[0]
    o_share = o_share.reshape(o_unit, 2, -1, part).transpose(1, 2, 0, 3).reshape(2, -1, part)
    qo_share = jnp.concatenate([q_share, o_share], axis=1)
    qo_z = rotations(after(qo_share, *kv_z), n_t)
    k_held, v_held = [jnp.stack([x[m] for x in kv_z])[None] for m in range(2)]
    for step in steps[:-1]:
        k_held, v_held = widen(k_held, v_held, step, orders, n_dp)
    k_held, v_held, late_latents = after([k_held, v_held, latents], *qo_z)
    latent_blocks = [latents] + rotations(late_latents, n_t)
    k_held, v_held = widen(k_held, v_held, steps[-1], orders, n_dp)
    k_pieces, v_pieces = cores(k_held, v_held, n_dp)
    qo_held = [jnp.stack([x[m] for x in qo_z])[None] for m in range(2)]
    qo_held = after(qo_held, k_held, v_held)
    for step in steps[:-1]:
        qo_held = widen(*qo_held, step, orders, n_dp)
    whole = [(0, 0, unit, 0, 0)]
    wk, keys, key_input_t = place(k_own, [k_pieces], offsets[:1], whole, unit, False, at, n_dp, n_t, key_input)
    wv, values, _ = place(v_own, [v_pieces], offsets[1:], whole, unit, False, at, n_dp, n_t, key_input)
    qo_held = widen(*after(qo_held, keys), steps[-1], orders, n_dp)
    qo_held = after(qo_held, values)
    qo_pieces = cores(*qo_held, n_dp)
    latent_all = jnp.concatenate(latent_blocks, axis=0)
    latent_hat, latent_root = norm_parts(latent_all)
    latent_normed = (latent_hat * latent_gain + latent_shift).astype(BF)
    cot_blocks = [cotangent] + rotations(after(cotangent, values, latent_normed), n_t)
    cuts = [(h, 0, unit // 2, h * unit // 2, 0) for h in range(2)]
    wq, queries, latent_t = place(
        query_weight, qo_pieces, offsets, cuts, unit, False, at, n_dp, n_t, latent_normed
    )
    cuts = [
        (h, unit // 2 + c * o_unit, o_unit, 0, h * width // 2 + c * part)
        for h in range(2)
        for c in range(width // 2 // part)
    ]
    wo = place(output_weight, qo_pieces, offsets, cuts, o_unit, True, at, n_dp, n_t)
    sent = attend_forward(queries, keys, values, key_image, row_image, n_t)
    sent = after(sent, wo, *cot_blocks[1:])
    got = [sent[0]] + [rotate(sent[k], n_t, -k) for k in range(1, n_t)]
    attended, stat = combine(got, heads)
    entropy = stat[:heads] - stat[heads:]
    own_valid = row_valid[:, :own_rows]
    penalty_part = jnp.sum(entropy * own_valid)

    latent_own = latents.astype(F32)
    middle = latent_own + dot("hr,hd->rd", attended, wo)
    feed_hat, feed_root = norm_parts(middle)
    feed_normed = (feed_hat * feed_gain + feed_shift).astype(BF)
    feed_all = jnp.concatenate(gather_blocks(feed_normed, n_t), axis=0)
    cot_all = jnp.concatenate(after(cot_blocks, feed_normed), axis=0)
    hidden = dot("rd,df->rf", feed_all, up_weight)
    cdf = 0.5 * (1.0 + lax.erf(hidden * (0.5**0.5)))
    slope = cdf + hidden * jnp.exp(-0.5 * hidden * hidden) * (0.5 / jnp.pi) ** 0.5
    activation = (hidden * cdf).astype(BF)
    back_activation = dot("rd,fd->rf", cot_all, down_weight)
    back_hidden = (back_activation * slope).astype(BF)
    back_terms = dot("rf,df->rd", back_hidden, up_weight).astype(BF)
    back_blocks = [back_terms[k * own_rows : (k + 1) * own_rows] for k in range(n_t)]
    back_arrived = send_blocks(back_blocks, n_t)
    late_activation, late_hidden = after([activation, back_hidden], back_terms)
    down_keep, down_send = gradient(cot_all.T, late_activation, True, at, n_dp)
    up_keep, up_send = gradient(feed_all.T, late_hidden, True, at, n_dp)
    result_terms = blocks_of_product(late_activation, down_weight, n_t)
    back_feed = add_up(after(back_arrived, down_send, up_send, *result_terms))
    down_got, up_got = partner(down_send, "dp", n_dp, 1), partner(up_send, "dp", n_dp, 1)

    back_middle = cotangent.astype(F32) + norm_backward(back_feed, feed_hat, feed_root, feed_gain)
    back_branch = back_middle.astype(BF)
    back_attended = dot("hd,rd->hr", wo, back_branch).astype(BF)
    own_coef = own_valid / count_total
    message = make_message(back_attended, attended, stat, own_coef, heads)
    messages = gather_blocks(message, n_t)
    out_keep, out_send = gradient(back_branch.T, attended, False, at, n_dp)
    out_got = partner(out_send, "dp", n_dp, 1)
    down_got, up_got, out_got = after([down_got, up_got, out_got], message)
    feed_pair = first_cut((down_keep, down_got), (up_keep, up_got), (out_keep, out_got), orders, n_dp)
    messages = after(messages, *[send for _, send in feed_pair])
    result_terms[1:] = after(result_terms[1:], *messages)
    result_terms = send_blocks(result_terms, n_t)
    back_q, back_k, back_v = attend_backward(
        queries, keys, values, key_image, row_image, row_valid / count_total, messages
    )
    feed_pair = cross(feed_pair, orders, 0, n_dp)
    for i in steps[1:]:
        feed_pair = next_cut(feed_pair, orders, i, n_dp)
        if i == steps[1]:
            back_q, back_k, back_v = after([back_q, back_k, back_v], *[send for _, send in feed_pair])
        feed_pair = cross(feed_pair, orders, i, n_dp)

    v_keep, v_send = gradient(key_input_t, back_v, False, at, n_dp)
    k_keep, k_send = gradient(key_input_t, after(back_k, v_send), False, at, n_dp)
    q_keep, q_send = gradient(latent_t, after(back_q, k_send, *result_terms[1:]), False, at, n_dp)
    v_send, k_send = after([v_send, k_send], q_send)
    v_got, k_got, q_got = [partner(x, "dp", n_dp, 1) for x in (v_send, k_send, q_send)]
    latent_q = after(back_q, q_send)
    *latent_terms, latent_sums = latent_back(latent_q, back_k, back_v, wq, wk, wv, latent_blocks)
    v_got, k_got, q_got = after([v_got, k_got, q_got], latent_sums)
    pair = first_cut((v_keep, v_got), (k_keep, k_got), None, orders, n_dp)
    sends = [send for _, send in pair]
    latent_terms[1:] = after(latent_terms[1:], *sends)
    latent_terms = send_blocks(latent_terms, n_t)
    pair = cross(pair, orders, 0, n_dp)
    q_pair = first_cut(None, None, (q_keep, after(q_got, *sends)), orders, n_dp)
    out_blocks = tensor_blocks(feed_pair, [None], inner, at, n_t)
    features_grad, media_sums = media_back(
        after(back_k, latent_sums, *out_blocks, *[send for _, send in q_pair]),
        back_v, wk, wv, features, media_gain, own_patches,
    )
    for i in steps[1:]:
        gots = after([got for _, got in pair], features_grad)
        pair = [(keep, got) for (keep, _), got in zip(pair, gots)]
        pair = next_cut(pair, orders, i, n_dp)
        if i == steps[1]:
            q_sends = after([send for _, send in q_pair], *[send for _, send in pair], *latent_terms[1:])
            q_pair = [(keep, send) for (keep, _), send in zip(q_pair, q_sends)]
        pair = cross(pair, orders, i, n_dp)
    q_pair = cross(q_pair, orders, 0, n_dp)
    blocks = tensor_blocks(pair, [1, 0], inner, at, n_t)
    for i in steps[1:]:
        gots = after([got for _, got in q_pair], *blocks)
        q_pair = [(keep, got) for (keep, _), got in zip(q_pair, gots)]
        q_pair = cross(next_cut(q_pair, orders, i, n_dp), orders, i, n_dp)
    blocks = send_blocks(blocks, n_t)
    q_blocks = tensor_blocks(q_pair, [None], inner, at, n_t)
    grad_kv = add_up(after(blocks, *q_blocks))
    back_latent = add_up(after(latent_terms, *q_blocks))
    late = after([x for terms in feed_pair for x in terms], *q_blocks)
    (down_keep, down_got), (up_keep, up_got) = late[:2], late[2:]
    down_share = down_keep[0, :, :inner].astype(F32) + down_got[0, :, :inner].astype(F32)
    up_share = up_keep[0, :, :inner].astype(F32) + up_got[0, :, :inner].astype(F32)
    result = middle + add_up(after(result_terms, *q_blocks))
    latents_grad = back_middle + norm_backward(
        back_latent, own_hat, own_root, latent_gain
    )

    grad_qo = scatter_blocks([jnp.concatenate(x, axis=0) for x in zip(q_blocks, out_blocks)], n_t)
    grad_q, grad_o = grad_qo[0], grad_qo[1]

    sums = [media_sums[0], media_sums[1], latent_sums[0], latent_sums[1]] + gain_shift(back_feed, feed_hat)
    sums = jnp.stack(sums + [jnp.full((width,), penalty_part)] * 2)
    sums = after(sums, features_grad)
    sums = all_sum(sums, [("dp", n_dp), ("tensor", n_t)])
    penalty = sums[6, 0] / count_total
    share = width // (n_dp * n_t)
    mine = lax.dynamic_index_in_dim(
        sums.reshape(8, n_dp * n_t, share), p * n_t + z, 1, keepdims=False
    )
    return (
        result.astype(BF)[None],
        penalty,
        latents_grad[None],
        features_grad[None],
        mine[0],
        mine[1],
        mine[2],
        mine[3],
        mine[4],
        mine[5],
        grad_q,
        jnp.moveaxis(grad_kv, 0, 1),
        grad_o.T,
        up_share,
        down_share.T,
    )


def solution(mesh):
    return jax.shard_map(
        local,
        mesh=mesh,
        in_specs=(
            P("dp", "tensor", None),
            P("dp", "tensor", None),
            P("dp", None),
            P("dp", None),
            P(),
            P(),
            P(),
            P(),
            P(),
            P(),
            P(None, "tensor"),
            P(None, None, "tensor"),
            P("tensor", None),
            P(None, "tensor"),
            P("tensor", None),
            P("dp", "tensor", None),
        ),
        out_specs=(
            P("dp", "tensor", None),
            P(),
            P("dp", "tensor", None),
            P("dp", "tensor", None),
            P(("dp", "tensor")),
            P(("dp", "tensor")),
            P(("dp", "tensor")),
            P(("dp", "tensor")),
            P(("dp", "tensor")),
            P(("dp", "tensor")),
            P("dp", "tensor"),
            P("dp", None, "tensor"),
            P("tensor", "dp"),
            P("dp", "tensor"),
            P("tensor", "dp"),
        ),
        check_vma=False,
    )
```

```python
from functools import partial

import jax
import jax.numpy as jnp
from jax import lax
from jax.experimental import pallas as pl
from jax.experimental.pallas import tpu as pltpu
from jax.sharding import PartitionSpec as P

HD = 96
LAT = 64
EPSILON = 1e-05
NEGATIVE = -1e30
SCALE = HD ** (-0.5)
BF = jnp.bfloat16
F32 = jnp.float32
VMEM_LIMIT = 48 * 1024 * 1024


def rotate(x, count, shift):
    return lax.ppermute(x, "tensor", [(i, (i + shift) % count) for i in range(count)])


def after(x, *done):
    many = isinstance(x, (list, tuple))
    held = lax.optimization_barrier((*x, *done) if many else (x, *done))
    return list(held[: len(x)]) if many else held[0]


def gather_blocks(x, count):
    return [x] + [rotate(x, count, k) for k in range(1, count)]


def send_blocks(blocks, count):
    return [blocks[0]] + [rotate(blocks[k], count, -k) for k in range(1, count)]


def scatter_blocks(blocks, count):
    return add_up(send_blocks(blocks, count))


def partner(x, axis, count, offset):
    return lax.ppermute(x, axis, [(i, i ^ offset) for i in range(count)])


def bits_of(count):
    return count.bit_length() - 1


def gradient_kernel(natural, n_dp, at_ref, xt_ref, y_ref, keep_ref, send_ref, total_ref):
    dims = (((1,), (0,)), ((), ())) if natural else (((1,), (1,)), ((), ()))
    total_ref[...] = lax.dot_general(xt_ref[...], y_ref[...], dims, preferred_element_type=F32)
    p, unit = at_ref[1], keep_ref.shape[1]
    for i in range(n_dp // 2):
        for odd, out in enumerate((keep_ref, send_ref)):
            first = pl.multiple_of((p ^ (2 * i + odd)) * unit, unit)
            out[i] = total_ref[pl.ds(first, unit), :].astype(BF)


def gradient(xt, y, natural, at, n_dp):
    width, rows = xt.shape
    unit = width // n_dp
    wide = y.shape[1] if natural else y.shape[0]
    step = wide // 3
    half = n_dp // 2
    if natural:
        y_spec = pl.BlockSpec((rows, step), lambda i: (0, i))
    else:
        y_spec = pl.BlockSpec((step, rows), lambda i: (i, 0))
    return pl.pallas_call(
        partial(gradient_kernel, natural, n_dp),
        grid=(3,),
        in_specs=[
            pl.BlockSpec(memory_space=pltpu.SMEM),
            pl.BlockSpec((width, rows), lambda i: (0, 0)),
            y_spec,
        ],
        out_specs=[pl.BlockSpec((half, unit, step), lambda i: (0, 0, i))] * 2,
        out_shape=[jax.ShapeDtypeStruct((half, unit, wide), BF)] * 2,
        scratch_shapes=[pltpu.VMEM((width, step), F32)],
        compiler_params=pltpu.CompilerParams(vmem_limit_bytes=VMEM_LIMIT),
    )(at, xt, y)


def bit_orders(count):
    outer = list(range(1, bits_of(count)))
    half = (len(outer) + 1) // 2
    return outer, outer[half:] + outer[:half]


def cut_kernel(widths, *refs):
    ins, (keep_ref, send_ref) = refs[:-2], refs[-2:]
    start = 0
    for i, wide in enumerate(widths):
        lanes = slice(start, start + wide)
        keep_a, got_a, keep_b, got_b = ins[4 * i : 4 * i + 4]
        keep_ref[:, :, lanes] = (keep_a[...].astype(F32) + got_a[...].astype(F32)).astype(BF)
        send_ref[:, :, lanes] = (keep_b[...].astype(F32) + got_b[...].astype(F32)).astype(BF)
        start += wide


def reduce_cut(parts, order, step, n_dp):
    left = [b for b in range(bits_of(n_dp) - 1, 0, -1) if b not in order[:step]]
    low = 1 << (len(left) - left.index(order[step]) - 1)
    count, rows, _ = parts[0][0].shape
    widths, specs, flat = [], [], []
    for keep, got, half in parts:
        wide = keep.shape[2] if half is None else keep.shape[2] // 2

        def at(bit, wide=wide, lane=half or 0):
            return pl.BlockSpec(
                (1, rows, wide), lambda i: (i // low * (2 * low) + bit * low + i % low, 0, lane)
            )

        widths.append(wide)
        specs += [at(0), at(0), at(1), at(1)]
        flat += [keep, got, keep, got]
    total = sum(widths)
    return pl.pallas_call(
        partial(cut_kernel, widths),
        grid=(count // 2,),
        in_specs=specs,
        out_specs=[pl.BlockSpec((1, rows, total), lambda i: (i, 0, 0))] * 2,
        out_shape=[jax.ShapeDtypeStruct((count // 2, rows, total), BF)] * 2,
        compiler_params=pltpu.CompilerParams(vmem_limit_bytes=VMEM_LIMIT),
    )(*flat)


def first_cut(one, two, split, orders, n_dp):
    out = []
    for h, full in enumerate((one, two)):
        parts = [(*full, None)] if full else []
        parts += [(*split, h)] if split else []
        out.append(reduce_cut(parts, orders[h], 0, n_dp))
    return out


def next_cut(pair, orders, step, n_dp):
    return [reduce_cut([(*x, None)], order, step, n_dp) for x, order in zip(pair, orders)]


def cross(pair, orders, step, n_dp):
    return [
        (keep, partner(send, "dp", n_dp, 1 << order[step])) for (keep, send), order in zip(pair, orders)
    ]


def add_up(terms):
    total = terms[0].astype(F32)
    for term in terms[1:]:
        total = total + term.astype(F32)
    return total


def blocks_kernel(n_t, weights, at_ref, *refs):
    (a_keep, a_got, b_keep, b_got), outs = refs[:4], refs[4:]
    pairs = (a_keep, a_got), (b_keep, b_got)
    z = at_ref[0]
    columns = outs[0].shape[-1]
    half = n_t // 2

    def piece(which, lane):
        lanes = pl.ds(pl.multiple_of(lane, columns), columns)
        keep, got = pairs[which]
        return keep[0, :, lanes].astype(F32) + got[0, :, lanes].astype(F32)

    for k in range(n_t):
        block = lax.rem(z - k + n_t, n_t)
        for m, which in enumerate(weights):
            if which is None:
                lane = (a_keep.shape[2] - columns * half) + lax.rem(block, half) * columns
                value = jnp.where(block >= half, piece(1, lane), piece(0, lane))
            else:
                value = piece(which, block * columns)
            outs[k][m] = value.astype(outs[k].dtype)


def tensor_blocks(pair, weights, columns, at, n_t):
    flat = [x for terms in pair for x in terms]
    rows = flat[0].shape[1]
    return pl.pallas_call(
        partial(blocks_kernel, n_t, weights),
        in_specs=[pl.BlockSpec(memory_space=pltpu.SMEM)]
        + [pl.BlockSpec(memory_space=pltpu.VMEM)] * len(flat),
        out_shape=[
            jax.ShapeDtypeStruct((len(weights), rows, columns // n_t), F32 if k == 0 else BF)
            for k in range(n_t)
        ],
        compiler_params=pltpu.CompilerParams(vmem_limit_bytes=VMEM_LIMIT),
    )(at, *flat)


def all_sum(x, axes):
    for axis, count in axes:
        for bit in range(bits_of(count)):
            x = x + partner(x, axis, count, 1 << bit)
    return x


def place_kernel(n_t, unit, z_rows, z_cols, offsets, parts, at_ref, own_ref, *refs):
    out_ref = refs[-1]
    z, p = at_ref[0], at_ref[1]
    rows, cols = own_ref.shape
    if z_rows:
        out_ref[pl.ds(pl.multiple_of(z * z_rows, z_rows), rows), :] = own_ref[...]
    else:
        out_ref[:, pl.ds(pl.multiple_of(z * z_cols, z_cols), cols)] = own_ref[...]
    for k in range(1, n_t):
        shard = lax.rem(z - k + n_t, n_t)
        for which, first, height, row_at, col_at in parts:
            for odd in range(2):
                src = refs[2 * which + odd]
                wide = src.shape[3]
                for i, off in enumerate(offsets[which]):
                    base = shard * z_rows + (p ^ (off ^ odd)) * unit + row_at
                    where = pl.ds(pl.multiple_of(base, 16), height)
                    if z_cols:
                        at = pl.ds(pl.multiple_of(shard * z_cols, z_cols), wide)
                    else:
                        at = slice(col_at, col_at + wide)
                    out_ref[where, at] = src[i, k - 1, first : first + height, :]


def reorder(x, places):
    return jnp.stack([lax.dynamic_index_in_dim(x, i, 0, keepdims=False) for i in places])


def project_kernel(place_kernel, count, at_ref, x_ref, *refs):
    place_kernel(at_ref, *refs[:-2])
    weight_ref, out_ref, turned_ref = refs[-3:]
    turned_ref[...] = x_ref[...].T
    step = weight_ref.shape[1] // count
    for c in range(count):
        cols = slice(c * step, (c + 1) * step)
        block = jnp.dot(x_ref[...], weight_ref[:, cols], preferred_element_type=F32)
        out_ref[cols, :] = block.T.astype(BF)


def place(own, pieces, offsets, parts, unit, by_rows, at, n_dp, n_t, x=None):
    rows, cols = own.shape
    shape = (n_t * rows, cols) if by_rows else (rows, n_t * cols)
    if unit % 16 or any(part[2] % 16 for part in parts):
        z, p = at[0], at[1]
        across = []
        for which, first, height, _, _ in parts:
            ordered = [None] * n_dp
            for i, off in enumerate(offsets[which]):
                for odd in range(2):
                    ordered[off ^ odd] = pieces[which][odd][i, :, first : first + height]
            across.append(reorder(jnp.stack(ordered), [p ^ d for d in range(n_dp)]))
        whole = jnp.concatenate(across, axis=3 if by_rows else 2).transpose(1, 0, 2, 3)
        whole = whole.reshape((n_t - 1, rows, cols))
        whole = jnp.concatenate([own[None], whole], axis=0)
        whole = reorder(whole, [(z - k + n_t) % n_t for k in range(n_t)])
        whole = whole.reshape(shape) if by_rows else whole.transpose(1, 0, 2).reshape(shape)
        return whole if x is None else (whole, dot("dh,rd->hr", whole, x).astype(BF), x.T)
    flat = [x for pair in pieces for x in pair]
    kernel = partial(
        place_kernel, n_t, unit, rows if by_rows else 0, 0 if by_rows else cols, offsets, parts
    )
    out = jax.ShapeDtypeStruct(shape, own.dtype)
    if x is None:
        first, outs = [], out
    else:
        kernel, first = partial(project_kernel, kernel, n_t), [x]
        outs = [out] + [jax.ShapeDtypeStruct((n, x.shape[0]), BF) for n in (shape[1], x.shape[1])]
    ins = [*first, own, *flat]
    return pl.pallas_call(
        kernel,
        out_shape=outs,
        in_specs=[pl.BlockSpec(memory_space=pltpu.SMEM)]
        + [pl.BlockSpec(memory_space=pltpu.VMEM)] * len(ins),
        compiler_params=pltpu.CompilerParams(vmem_limit_bytes=VMEM_LIMIT),
    )(at, *ins)


def rotations(x, count):
    return [rotate(x, count, k) for k in range(1, count)]


def widen(one, two, step, orders, n_dp, *done):
    arrived = [partner(x, "dp", n_dp, 1 << order[step]) for x, order in zip((one, two), orders)]
    if done:
        arrived = after(arrived, *done)
    return [jnp.concatenate(x, axis=0) for x in zip((one, two), arrived)]


def widen_offsets(order):
    offsets = [0]
    for bit in order:
        offsets = offsets + [o ^ (1 << bit) for o in offsets]
    return offsets


def cores(one, two, n_dp):
    return [(x, partner(x, "dp", n_dp, 1)) for x in (one, two)]


def share_of(x, axis, count):
    size = x.shape[axis] // count
    return lax.dynamic_slice_in_dim(x, lax.axis_index("dp") * size, size, axis)


def three(x):
    high = x.astype(BF)
    left = x - high.astype(F32)
    middle = left.astype(BF)
    low = (left - middle.astype(F32)).astype(BF)
    return jnp.concatenate([high, middle, low], axis=0)


def join(x, count):
    x = x.astype(F32)
    return x[:count] + x[count : 2 * count] + x[2 * count :]


GROUP = 8
CHUNK = 128
TN = (((0,), (0,)), ((), ()))
NT = (((1,), (1,)), ((), ()))


def forward_kernel(heads, n_t, span_ref, q_ref, k_ref, v_ref, seg_ref, img_ref, *rest):
    msgs, stat, acc, run = rest[:n_t], rest[n_t], rest[n_t + 1], rest[n_t + 2]
    g = pl.program_id(0)
    rows = q_ref.shape[1] // n_t
    keys = k_ref.shape[1]
    for k in range(n_t):
        cols = slice(k * rows, (k + 1) * rows)
        image = img_ref[:, cols]
        acc[...] = jnp.zeros_like(acc)
        run[...] = jnp.zeros_like(run)
        run[0] = jnp.full(run.shape[1:], NEGATIVE)

        def step(at, cols=cols, image=image):
            allowed = seg_ref[at, :] == image
            bands = [slice(h * HD, (h + 1) * HD) for h in range(GROUP)]
            scores = [
                SCALE
                * lax.dot_general(k_ref[b, at], q_ref[b, cols], TN, preferred_element_type=F32)
                for b in bands
            ]
            scores = [jnp.where(allowed, x, NEGATIVE) for x in scores]
            old = [run[0, h : h + 1] for h in range(GROUP)]
            tops = [
                jnp.maximum(m, jnp.max(x, axis=0, keepdims=True)) for m, x in zip(old, scores)
            ]
            weights = [jnp.where(allowed, jnp.exp(x - m), 0.0) for x, m in zip(scores, tops)]
            outs = [
                jnp.dot(v_ref[b, at], w.astype(BF), preferred_element_type=F32)
                for b, w in zip(bands, weights)
            ]
            fades = [jnp.exp(m - n) for m, n in zip(old, tops)]
            for h in range(GROUP):
                run[0, h : h + 1] = tops[h]
                run[1, h : h + 1] = run[1, h : h + 1] * fades[h] + jnp.sum(
                    weights[h], axis=0, keepdims=True
                )
                run[2, h : h + 1] = run[2, h : h + 1] * fades[h] + jnp.sum(
                    weights[h] * scores[h], axis=0, keepdims=True
                )
            for b, f, o in zip(bands, fades, outs):
                acc[b, :] = acc[b, :] * f + o

        if k == 0:
            step(slice(keys - rows, keys))

        @pl.loop(span_ref[0, k], span_ref[1, k])
        def _(c, step=step):
            step(pl.ds(pl.multiple_of(c * CHUNK, CHUNK), CHUNK))

        total = run[1, :GROUP]
        some = total > 0.0
        safe = jnp.where(some, total, 1.0)
        inverse = jnp.where(some, 1.0 / safe, 0.0)
        stat[0, pl.ds(g, 1), :, cols] = jnp.where(some, run[0, :GROUP] + jnp.log(safe), NEGATIVE)[None]
        stat[1, pl.ds(g, 1), :, cols] = (run[2, :GROUP] * inverse)[None]
        for h in range(GROUP):
            band = slice(h * HD, (h + 1) * HD)
            first = pl.multiple_of((g * GROUP + h) * HD, HD)
            msgs[k][pl.ds(first, HD), :] = (acc[band, :] * inverse[h : h + 1]).astype(BF)

    @pl.when(g == heads // GROUP - 1)
    def _():
        for k in range(n_t):
            cols = slice(k * rows, (k + 1) * rows)
            for i in range(2):
                first = heads * (HD + 3 * i)
                msgs[k][first : first + 3 * heads, :] = three(
                    stat[i, :, :, cols].reshape(heads, rows)
                )


def attend_forward(q, k, v, seg, img, span, n_t):
    heads = q.shape[0] // HD
    rows, keys = q.shape[1], k.shape[1]
    one = rows // n_t
    tall = heads * (HD + 6)
    band = GROUP * HD
    return pl.pallas_call(
        partial(forward_kernel, heads, n_t),
        grid_spec=pltpu.PrefetchScalarGridSpec(
            num_scalar_prefetch=1,
            grid=(heads // GROUP,),
            in_specs=[
                pl.BlockSpec((band, rows), lambda g, s: (g, 0)),
                pl.BlockSpec((band, keys), lambda g, s: (g, 0)),
                pl.BlockSpec((band, keys), lambda g, s: (g, 0)),
                pl.BlockSpec((keys, 1), lambda g, s: (0, 0)),
                pl.BlockSpec((1, rows), lambda g, s: (0, 0)),
            ],
            out_specs=[pl.BlockSpec((tall, one), lambda g, s: (0, 0))] * n_t,
            scratch_shapes=[
                pltpu.VMEM((2, heads // GROUP, GROUP, rows), F32),
                pltpu.VMEM((band, one), F32),
                pltpu.VMEM((3, 8, one), F32),
            ],
        ),
        out_shape=[jax.ShapeDtypeStruct((tall, one), BF)] * n_t,
        compiler_params=pltpu.CompilerParams(vmem_limit_bytes=VMEM_LIMIT),
    )(span, q, k, v, seg, img)


def combine_kernel(heads, n_t, *refs):
    msgs, (out_ref, stat_ref) = refs[:n_t], refs[n_t:]
    base = heads * HD
    logs = [join(m[base : base + 3 * heads, :], heads) for m in msgs]
    means = [join(m[base + 3 * heads :, :], heads) for m in msgs]
    top = logs[0]
    for x in logs[1:]:
        top = jnp.maximum(top, x)
    shares = [jnp.exp(x - top) for x in logs]
    total = shares[0]
    for x in shares[1:]:
        total = total + x
    shares = [x / total for x in shares]
    mean = shares[0] * means[0]
    for s, x in zip(shares[1:], means[1:]):
        mean = mean + s * x
    stat_ref[:heads, :] = top + jnp.log(total)
    stat_ref[heads:, :] = mean
    for h in range(heads):
        at = slice(h * HD, (h + 1) * HD)
        acc = msgs[0][at, :].astype(F32) * shares[0][h : h + 1, :]
        for s, m in zip(shares[1:], msgs[1:]):
            acc = acc + m[at, :].astype(F32) * s[h : h + 1, :]
        out_ref[at, :] = acc.astype(BF)


def combine(msgs, heads):
    one = msgs[0].shape[1]
    return pl.pallas_call(
        partial(combine_kernel, heads, len(msgs)),
        out_shape=[
            jax.ShapeDtypeStruct((heads * HD, one), BF),
            jax.ShapeDtypeStruct((2 * heads, one), F32),
        ],
        compiler_params=pltpu.CompilerParams(vmem_limit_bytes=VMEM_LIMIT),
    )(*msgs)


def message_kernel(heads, do_ref, out_ref, stat_ref, coef_ref, msg_ref):
    base = heads * HD
    deltas = []
    for h in range(heads):
        at = slice(h * HD, (h + 1) * HD)
        grad = do_ref[at, :].astype(F32)
        deltas.append(jnp.sum(grad * out_ref[at, :].astype(F32), axis=0, keepdims=True))
    msg_ref[:base, :] = do_ref[...]
    delta = jnp.concatenate(deltas, axis=0) - coef_ref[...] * stat_ref[heads:, :]
    msg_ref[base : base + 3 * heads, :] = three(stat_ref[:heads, :])
    msg_ref[base + 3 * heads :, :] = three(delta)


def make_message(do, out, stat, coef, heads):
    return pl.pallas_call(
        partial(message_kernel, heads),
        out_shape=jax.ShapeDtypeStruct((heads * (HD + 6), do.shape[1]), BF),
        compiler_params=pltpu.CompilerParams(vmem_limit_bytes=VMEM_LIMIT),
    )(do, out, stat, coef)


def backward_kernel(heads, n_t, span_ref, q_ref, k_ref, v_ref, seg_ref, img_ref, coef_ref, *rest):
    grads, stats = rest[:n_t], rest[n_t : 2 * n_t]
    dq_ref, dk_ref, dv_ref, stat, dq, dk, dv = rest[2 * n_t :]
    g = pl.program_id(0)
    rows = q_ref.shape[1] // n_t
    keys = k_ref.shape[1]

    @pl.when(g == 0)
    def _():
        for i in range(n_t):
            cols = slice(i * rows, (i + 1) * rows)
            for j in range(2):
                part = join(stats[i][3 * j * heads : 3 * (j + 1) * heads, :], heads)
                stat[j, :, :, cols] = part.reshape(heads // GROUP, GROUP, rows)

    dk[...] = jnp.zeros_like(dk)
    dv[...] = jnp.zeros_like(dv)
    for i in range(n_t):
        cols = slice(i * rows, (i + 1) * rows)
        image, coef = img_ref[:, cols], coef_ref[:, cols]
        logs = stat[0, pl.ds(g, 1), :, cols][0]
        deltas = stat[1, pl.ds(g, 1), :, cols][0]
        dq[...] = jnp.zeros_like(dq)

        def step(at, cols=cols, image=image, coef=coef, logs=logs, deltas=deltas, grad_ref=grads[i]):
            allowed = seg_ref[at, :] == image
            bands = [slice(h * HD, (h + 1) * HD) for h in range(GROUP)]
            scores = [
                SCALE
                * lax.dot_general(k_ref[b, at], q_ref[b, cols], TN, preferred_element_type=F32)
                for b in bands
            ]
            back_probs = [
                lax.dot_general(v_ref[b, at], grad_ref[b, :], TN, preferred_element_type=F32)
                for b in bands
            ]
            probs = [
                jnp.where(allowed, jnp.exp(jnp.where(allowed, x - logs[h : h + 1], 0.0)), 0.0)
                for h, x in enumerate(scores)
            ]
            backs = [
                (p * (y - coef * x - deltas[h : h + 1])).astype(BF)
                for h, (x, y, p) in enumerate(zip(scores, back_probs, probs))
            ]
            probs = [p.astype(BF) for p in probs]
            for b, p in zip(bands, probs):
                dv[b, at] += lax.dot_general(grad_ref[b, :], p, NT, preferred_element_type=F32)
            for b, x in zip(bands, backs):
                dq[b, :] += jnp.dot(k_ref[b, at], x, preferred_element_type=F32)
            for b, x in zip(bands, backs):
                dk[b, at] += lax.dot_general(q_ref[b, cols], x, NT, preferred_element_type=F32)

        if i == 0:
            step(slice(keys - rows, keys))

        @pl.loop(span_ref[0, i], span_ref[1, i])
        def _(c, step=step):
            step(pl.ds(pl.multiple_of(c * CHUNK, CHUNK), CHUNK))

        dq_ref[:, cols] = (dq[...] * SCALE).astype(BF)
    dk_ref[...] = (dk[...] * SCALE).astype(BF)
    dv_ref[...] = dv[...].astype(BF)


def attend_backward(q, k, v, seg, img, coef, span, msgs):
    n_t = len(msgs)
    heads = q.shape[0] // HD
    rows, keys = q.shape[1], k.shape[1]
    one = rows // n_t
    band = GROUP * HD
    wide = [pl.BlockSpec((band, n), lambda g, s: (g, 0)) for n in (rows, keys, keys)]
    return pl.pallas_call(
        partial(backward_kernel, heads, n_t),
        grid_spec=pltpu.PrefetchScalarGridSpec(
            num_scalar_prefetch=1,
            grid=(heads // GROUP,),
            in_specs=wide
            + [
                pl.BlockSpec((keys, 1), lambda g, s: (0, 0)),
                pl.BlockSpec((1, rows), lambda g, s: (0, 0)),
                pl.BlockSpec((1, rows), lambda g, s: (0, 0)),
            ]
            + [pl.BlockSpec((band, one), lambda g, s: (g, 0))] * n_t
            + [pl.BlockSpec((6 * heads, one), lambda g, s: (HD // 6, 0))] * n_t,
            out_specs=wide,
            scratch_shapes=[
                pltpu.VMEM((2, heads // GROUP, GROUP, rows), F32),
                pltpu.VMEM((band, one), F32),
                pltpu.VMEM((band, keys), F32),
                pltpu.VMEM((band, keys), F32),
            ],
        ),
        out_shape=[
            jax.ShapeDtypeStruct(q.shape, BF),
            jax.ShapeDtypeStruct(k.shape, BF),
            jax.ShapeDtypeStruct(v.shape, BF),
        ],
        compiler_params=pltpu.CompilerParams(vmem_limit_bytes=VMEM_LIMIT),
        cost_estimate=pl.CostEstimate(
            flops=60 * heads * HD * rows * keys,
            bytes_accessed=60 * 1024 * 1024,
            transcendentals=heads * rows * keys,
        ),
    )(span, q, k, v, seg, img, coef, *msgs, *msgs)


def norm_parts(values):
    values = values.astype(F32)
    center = values - jnp.mean(values, axis=-1, keepdims=True)
    inv_root = lax.rsqrt(jnp.mean(center * center, axis=-1, keepdims=True) + EPSILON)
    return center * inv_root, inv_root


def norm_backward(grad_rows, normal, inv_root, gain_row):
    scaled = grad_rows * gain_row
    reduced = (
        scaled
        - jnp.mean(scaled, axis=-1, keepdims=True)
        - normal * jnp.mean(scaled * normal, axis=-1, keepdims=True)
    )
    return reduced * inv_root


def gain_shift(grad_rows, normal):
    return [jnp.sum(grad_rows * normal, axis=0), jnp.sum(grad_rows, axis=0)]


def rows_back(grads, weights):
    total = None
    for grad, weight in zip(grads, weights):
        term = lax.dot_general(grad, weight, (((0,), (1,)), ((), ())), preferred_element_type=F32)
        total = term if total is None else total + term
    return total


def media_back_kernel(dk_ref, dv_ref, wk_ref, wv_ref, x_ref, gain_ref, out_ref, sums_ref):
    back = rows_back((dk_ref[...], dv_ref[...]), (wk_ref[...], wv_ref[...]))
    normal, root = norm_parts(x_ref[...])
    out_ref[...] = norm_backward(back, normal, root, gain_ref[...])

    @pl.when(pl.program_id(0) == 0)
    def _():
        sums_ref[...] = jnp.zeros_like(sums_ref)

    sums_ref[0:1] += jnp.sum(back * normal, axis=0, keepdims=True)
    sums_ref[1:2] += jnp.sum(back, axis=0, keepdims=True)


def media_back(back_k, back_v, wk, wv, features, gain, block):
    rows, width = features.shape
    inner = back_k.shape[0]
    whole = pl.BlockSpec((width, inner), lambda i: (0, 0))
    return pl.pallas_call(
        media_back_kernel,
        grid=(rows // block,),
        in_specs=[pl.BlockSpec((inner, block), lambda i: (0, i))] * 2
        + [whole] * 2
        + [pl.BlockSpec((block, width), lambda i: (i, 0)), pl.BlockSpec((1, width), lambda i: (0, 0))],
        out_specs=[
            pl.BlockSpec((block, width), lambda i: (i, 0)),
            pl.BlockSpec((8, width), lambda i: (0, 0)),
        ],
        out_shape=[
            jax.ShapeDtypeStruct((rows, width), F32),
            jax.ShapeDtypeStruct((8, width), F32),
        ],
        compiler_params=pltpu.CompilerParams(vmem_limit_bytes=VMEM_LIMIT),
    )(back_k, back_v, wk, wv, features, gain[None])


def latent_back_kernel(n_t, dq_ref, dk_ref, dv_ref, wq_ref, wk_ref, wv_ref, *refs):
    xs, outs, sums_ref = refs[:n_t], refs[n_t:-1], refs[-1]
    rows = xs[0].shape[0]
    gain_sum = shift_sum = None
    total = rows_back((dq_ref[...],), (wq_ref[...],))
    own = rows_back((dk_ref[...], dv_ref[...]), (wk_ref[...], wv_ref[...]))
    for k in range(n_t):
        back = total[k * rows : (k + 1) * rows]
        if k == 0:
            back = back + own
        outs[k][...] = back.astype(outs[k].dtype)
        normal, _ = norm_parts(xs[k][...])
        gain_part = jnp.sum(back * normal, axis=0, keepdims=True)
        shift_part = jnp.sum(back, axis=0, keepdims=True)
        gain_sum = gain_part if gain_sum is None else gain_sum + gain_part
        shift_sum = shift_part if shift_sum is None else shift_sum + shift_part
    sums_ref[...] = jnp.zeros_like(sums_ref)
    sums_ref[0:1] = gain_sum
    sums_ref[1:2] = shift_sum


def latent_back(back_q, back_k, back_v, wq, wk, wv, blocks):
    n_t = len(blocks)
    rows, width = blocks[0].shape
    inner, keys = back_k.shape
    tail = pl.BlockSpec((inner, rows), lambda i: (0, keys // rows - 1))
    whole = pl.BlockSpec((width, inner), lambda i: (0, 0))
    return pl.pallas_call(
        partial(latent_back_kernel, n_t),
        grid=(1,),
        in_specs=[pl.BlockSpec(back_q.shape, lambda i: (0, 0)), tail, tail, whole, whole, whole]
        + [pl.BlockSpec((rows, width), lambda i: (0, 0))] * n_t,
        out_specs=[pl.BlockSpec((rows, width), lambda i: (0, 0))] * n_t
        + [pl.BlockSpec((8, width), lambda i: (0, 0))],
        out_shape=[jax.ShapeDtypeStruct((rows, width), BF if k else F32) for k in range(n_t)]
        + [jax.ShapeDtypeStruct((8, width), F32)],
        compiler_params=pltpu.CompilerParams(vmem_limit_bytes=VMEM_LIMIT),
    )(back_q, back_k, back_v, wq, wk, wv, *blocks)


def blocks_of_product_kernel(n_t, a_ref, b_ref, *outs):
    total = jnp.dot(a_ref[...], b_ref[...], preferred_element_type=F32)
    rows = outs[0].shape[0]
    for k in range(n_t):
        outs[k][...] = total[k * rows : (k + 1) * rows].astype(outs[k].dtype)


def blocks_of_product(a, b, n_t):
    shape = a.shape[0] // n_t, b.shape[1]
    return list(
        pl.pallas_call(
            partial(blocks_of_product_kernel, n_t),
            out_shape=[jax.ShapeDtypeStruct(shape, BF if k else F32) for k in range(n_t)],
            compiler_params=pltpu.CompilerParams(vmem_limit_bytes=VMEM_LIMIT),
        )(a, b)
    )


def finish_kernel(n_t, columns, *refs):
    results, latent_terms, feeds = refs[:n_t], refs[n_t : 2 * n_t], refs[2 * n_t : 2 * n_t + 4]
    middle_ref, back_ref, x_ref, gain_ref, *outs = refs[2 * n_t + 4 :]
    outs[0][...] = (middle_ref[...] + add_up([r[...] for r in results])).astype(BF)
    normal, root = norm_parts(x_ref[...])
    back = add_up([r[...] for r in latent_terms])
    outs[1][...] = back_ref[...] + norm_backward(back, normal, root, gain_ref[...])
    for m in range(2):
        keep, got = feeds[2 * m], feeds[2 * m + 1]
        outs[2 + m][...] = keep[0, :, :columns].astype(F32) + got[0, :, :columns].astype(F32)


def finish(result_terms, latent_terms, feed_pair, middle, back_middle, latents, gain, columns):
    feeds = [x for pair in feed_pair for x in pair]
    unit, width = feeds[0].shape[1], middle.shape[1]
    return pl.pallas_call(
        partial(finish_kernel, len(result_terms), columns),
        out_shape=[
            jax.ShapeDtypeStruct(middle.shape, BF),
            jax.ShapeDtypeStruct(middle.shape, F32),
            jax.ShapeDtypeStruct((unit, columns), F32),
            jax.ShapeDtypeStruct((unit, columns), F32),
        ],
        compiler_params=pltpu.CompilerParams(vmem_limit_bytes=VMEM_LIMIT),
    )(*result_terms, *latent_terms, *feeds, middle, back_middle, latents, gain[None])


def dot(equation, a, b):
    return jnp.einsum(equation, a, b, preferred_element_type=F32)


def local(
    latents,
    features,
    lengths,
    valid_media,
    media_gain,
    media_shift,
    latent_gain,
    latent_shift,
    feed_gain,
    feed_shift,
    query_weight,
    key_value_weight,
    output_weight,
    up_weight,
    down_weight,
    cotangent,
):
    n_t = lax.axis_size("tensor")
    n_dp = lax.axis_size("dp")
    z, p = lax.axis_index("tensor"), lax.axis_index("dp")
    at = jnp.stack([z, p]).astype(jnp.int32)
    latents, features, cotangent = latents[0], features[0], cotangent[0]
    lengths, valid = lengths[0], valid_media[0]
    width = latents.shape[1]
    own_rows, own_patches = latents.shape[0], features.shape[0]
    inner = query_weight.shape[1] * n_t
    heads = inner // HD
    images = lengths.shape[0]

    count_part = jnp.full((8, 128), jnp.sum(valid).astype(F32))
    count_total = all_sum(count_part, [("dp", n_dp)])[0, 0]

    ends = jnp.sum(
        jnp.where(jnp.arange(images)[:, None] <= jnp.arange(images)[None, :], lengths[:, None], 0),
        axis=0,
    )
    positions = z * own_patches + jnp.arange(own_patches, dtype=jnp.int32)
    segment = jnp.sum((positions[:, None] >= ends[None, :]).astype(jnp.int32), axis=1)
    hit = segment[:, None] == jnp.arange(images, dtype=jnp.int32)[None, :]
    patch_valid = jnp.sum(jnp.where(hit, valid[None, :], 0), axis=1)
    patch_segment = jnp.where(patch_valid > 0, segment, -1)
    own_images = (z * own_rows + jnp.arange(own_rows, dtype=jnp.int32)) // LAT
    key_image = jnp.concatenate([patch_segment, own_images])[:, None]
    block_of = (z - jnp.arange(n_t, dtype=jnp.int32) + n_t) % n_t
    row_index = block_of[:, None] * own_rows + jnp.arange(own_rows, dtype=jnp.int32)[None, :]
    row_image = (row_index // LAT).reshape(1, -1)
    rows_each = own_rows // LAT
    local_ends = jnp.clip(ends - z * own_patches, 0, own_patches)
    local_starts = jnp.clip(ends - lengths - z * own_patches, 0, own_patches)
    block_image = block_of * rows_each
    at_image = jnp.arange(images, dtype=jnp.int32)[None, :]
    low = jnp.sum(jnp.where(at_image == block_image[:, None], local_starts[None, :], 0), axis=1)
    high = jnp.sum(
        jnp.where(at_image == block_image[:, None] + rows_each - 1, local_ends[None, :], 0), axis=1
    )
    span = jnp.stack([low // CHUNK, (high + CHUNK - 1) // CHUNK]).astype(jnp.int32)
    row_valid = jnp.sum(
        jnp.where(row_image.T == jnp.arange(images, dtype=jnp.int32)[None, :], valid[None, :], 0),
        axis=1,
    ).astype(F32)[None, :]

    orders = bit_orders(n_dp)
    steps = range(len(orders[0]))
    offsets = [widen_offsets(order) for order in orders]
    unit, part = width // n_dp, query_weight.shape[1]
    keyval = jnp.moveaxis(share_of(key_value_weight, 0, n_dp), 1, 0)
    kv_z = rotations(keyval, n_t)
    media_hat, media_root = norm_parts(features)
    media_normed = (media_hat * media_gain + media_shift).astype(BF)
    own_hat, own_root = norm_parts(latents)
    own_normed = (own_hat * latent_gain + latent_shift).astype(BF)
    key_input = jnp.concatenate([media_normed, own_normed], axis=0)
    kv_own = [key_value_weight[:, 0], key_value_weight[:, 1]]
    *kv_z, key_input, count_total, k_own, v_own = after([*kv_z, key_input, count_total, *kv_own])
    q_share = share_of(query_weight, 0, n_dp).reshape(2, unit // 2, part)
    o_share = share_of(output_weight, 0, n_dp)
    o_unit = o_share.shape[0]
    o_share = o_share.reshape(o_unit, 2, -1, part).transpose(1, 2, 0, 3).reshape(2, -1, part)
    qo_share = jnp.concatenate([q_share, o_share], axis=1)
    qo_z = rotations(after(qo_share, *kv_z), n_t)
    k_held, v_held = [jnp.stack([x[m] for x in kv_z])[None] for m in range(2)]
    for step in steps[:-1]:
        k_held, v_held = widen(k_held, v_held, step, orders, n_dp)
    k_held, v_held = after([k_held, v_held], *qo_z)
    gathered = lax.all_gather(jnp.stack(after([latents, cotangent], *qo_z)), "tensor", axis=0)
    others = [
        lax.dynamic_index_in_dim(gathered, (z - k + n_t) % n_t, 0, keepdims=False)
        for k in range(1, n_t)
    ]
    latent_blocks = [latents] + [x[0] for x in others]
    cot_blocks = [cotangent] + [x[1] for x in others]
    k_held, v_held = widen(k_held, v_held, steps[-1], orders, n_dp)
    k_pieces, v_pieces = cores(k_held, v_held, n_dp)
    qo_held = [jnp.stack([x[m] for x in qo_z])[None] for m in range(2)]
    qo_held = after(qo_held, k_held, v_held)
    whole = [(0, 0, unit, 0, 0)]
    wk, keys, key_input_t = place(k_own, [k_pieces], offsets[:1], whole, unit, False, at, n_dp, n_t, key_input)
    wv, values, _ = place(v_own, [v_pieces], offsets[1:], whole, unit, False, at, n_dp, n_t, key_input)
    for step in steps[:-1]:
        qo_held = widen(*qo_held, step, orders, n_dp, keys)
    qo_held = widen(*qo_held, steps[-1], orders, n_dp, values)
    qo_pieces = cores(*qo_held, n_dp)
    latent_all = jnp.concatenate(latent_blocks, axis=0)
    latent_hat, latent_root = norm_parts(latent_all)
    latent_normed = (latent_hat * latent_gain + latent_shift).astype(BF)
    cuts = [(h, 0, unit // 2, h * unit // 2, 0) for h in range(2)]
    wq, queries, latent_t = place(
        query_weight, qo_pieces, offsets, cuts, unit, False, at, n_dp, n_t, latent_normed
    )
    cuts = [
        (h, unit // 2 + c * o_unit, o_unit, 0, h * width // 2 + c * part)
        for h in range(2)
        for c in range(width // 2 // part)
    ]
    wo = place(output_weight, qo_pieces, offsets, cuts, o_unit, True, at, n_dp, n_t)
    sent = attend_forward(queries, keys, values, key_image, row_image, span, n_t)
    sent = after(sent, wo)
    got = [sent[0]] + [rotate(sent[k], n_t, -k) for k in range(1, n_t)]
    attended, stat = combine(got, heads)
    entropy = stat[:heads] - stat[heads:]
    own_valid = row_valid[:, :own_rows]
    penalty_part = jnp.sum(entropy * own_valid)

    latent_own = latents.astype(F32)
    middle = latent_own + dot("hr,hd->rd", attended, wo)
    feed_hat, feed_root = norm_parts(middle)
    feed_normed = (feed_hat * feed_gain + feed_shift).astype(BF)
    feed_all = jnp.concatenate(gather_blocks(feed_normed, n_t), axis=0)
    cot_all = jnp.concatenate(after(cot_blocks, feed_normed), axis=0)
    hidden = dot("rd,df->rf", feed_all, up_weight)
    cdf = 0.5 * (1.0 + lax.erf(hidden * (0.5**0.5)))
    slope = cdf + hidden * jnp.exp(-0.5 * hidden * hidden) * (0.5 / jnp.pi) ** 0.5
    activation = (hidden * cdf).astype(BF)
    back_activation = dot("rd,fd->rf", cot_all, down_weight)
    back_hidden = (back_activation * slope).astype(BF)
    back_terms = dot("rf,df->rd", back_hidden, up_weight).astype(BF)
    back_blocks = [back_terms[k * own_rows : (k + 1) * own_rows] for k in range(n_t)]
    back_arrived = send_blocks(back_blocks, n_t)
    late_activation, late_hidden = after([activation, back_hidden], back_terms)
    down_keep, down_send = gradient(cot_all.T, late_activation, True, at, n_dp)
    up_keep, up_send = gradient(feed_all.T, late_hidden, True, at, n_dp)
    result_terms = blocks_of_product(late_activation, down_weight, n_t)
    back_feed = add_up(after(back_arrived, down_send, up_send, *result_terms))
    down_got, up_got = partner(down_send, "dp", n_dp, 1), partner(up_send, "dp", n_dp, 1)

    back_middle = cotangent.astype(F32) + norm_backward(back_feed, feed_hat, feed_root, feed_gain)
    back_branch = back_middle.astype(BF)
    back_attended = dot("hd,rd->hr", wo, back_branch).astype(BF)
    own_coef = own_valid / count_total
    message = make_message(back_attended, attended, stat, own_coef, heads)
    messages = gather_blocks(message, n_t)
    out_keep, out_send = gradient(back_branch.T, attended, False, at, n_dp)
    out_got = partner(out_send, "dp", n_dp, 1)
    down_got, up_got, out_got = after([down_got, up_got, out_got], message)
    feed_pair = first_cut((down_keep, down_got), (up_keep, up_got), (out_keep, out_got), orders, n_dp)
    messages = after(messages, *[send for _, send in feed_pair])
    result_terms[1:] = after(result_terms[1:], *messages)
    result_terms = send_blocks(result_terms, n_t)
    back_q, back_k, back_v = attend_backward(
        queries, keys, values, key_image, row_image, row_valid / count_total, span, messages
    )
    feed_pair = cross(feed_pair, orders, 0, n_dp)
    for i in steps[1:]:
        feed_pair = next_cut(feed_pair, orders, i, n_dp)
        if i == steps[1]:
            back_q, back_k, back_v = after([back_q, back_k, back_v], *[send for _, send in feed_pair])
        feed_pair = cross(feed_pair, orders, i, n_dp)

    v_keep, v_send = gradient(key_input_t, back_v, False, at, n_dp)
    k_keep, k_send = gradient(key_input_t, after(back_k, v_send), False, at, n_dp)
    q_keep, q_send = gradient(latent_t, after(back_q, k_send, *result_terms[1:]), False, at, n_dp)
    v_send, k_send = after([v_send, k_send], q_send)
    v_got, k_got, q_got = [partner(x, "dp", n_dp, 1) for x in (v_send, k_send, q_send)]
    latent_q = after(back_q, q_send)
    *latent_terms, latent_sums = latent_back(latent_q, back_k, back_v, wq, wk, wv, latent_blocks)
    v_got, k_got, q_got = after([v_got, k_got, q_got], latent_sums)
    k_got = after(k_got, *[got for _, got in feed_pair])
    pair = first_cut((v_keep, v_got), (k_keep, k_got), None, orders, n_dp)
    sends = [send for _, send in pair]
    latent_terms[1:] = after(latent_terms[1:], *sends)
    latent_terms = send_blocks(latent_terms, n_t)
    pair = cross(pair, orders, 0, n_dp)
    q_pair = first_cut(None, None, (q_keep, after(q_got, *sends)), orders, n_dp)
    out_blocks = tensor_blocks(feed_pair, [None], inner, at, n_t)
    features_grad, media_sums = media_back(
        after(back_k, latent_sums, *out_blocks, *[send for _, send in q_pair]),
        back_v, wk, wv, features, media_gain, own_patches,
    )
    for i in steps[1:]:
        gots = after([got for _, got in pair], features_grad)
        pair = [(keep, got) for (keep, _), got in zip(pair, gots)]
        pair = next_cut(pair, orders, i, n_dp)
        if i == steps[1]:
            q_sends = after([send for _, send in q_pair], *[send for _, send in pair], *latent_terms[1:])
            q_pair = [(keep, send) for (keep, _), send in zip(q_pair, q_sends)]
        pair = cross(pair, orders, i, n_dp)
    q_pair = cross(q_pair, orders, 0, n_dp)
    blocks = send_blocks(tensor_blocks(pair, [1, 0], inner, at, n_t), n_t)
    for i in steps[1:]:
        gots = after([got for _, got in q_pair], blocks[1], blocks[-1])
        q_pair = [(keep, got) for (keep, _), got in zip(q_pair, gots)]
        q_pair = cross(next_cut(q_pair, orders, i, n_dp), orders, i, n_dp)
    q_blocks = tensor_blocks(q_pair, [None], inner, at, n_t)
    grad_kv = add_up(after(blocks, *q_blocks))
    result, latents_grad, down_share, up_share = finish(
        after(result_terms, *q_blocks), latent_terms, feed_pair, middle, back_middle, latents, latent_gain, inner
    )

    qo_blocks = [jnp.concatenate(x, axis=0) for x in zip(q_blocks, out_blocks)]
    grad_qo = add_up(after(send_blocks(qo_blocks, n_t), result))
    grad_q, grad_o = grad_qo[0], grad_qo[1]

    sums = [media_sums[0], media_sums[1], latent_sums[0], latent_sums[1]] + gain_shift(back_feed, feed_hat)
    sums = jnp.stack(sums + [jnp.full((width,), penalty_part)] * 2)
    sums = after(sums, features_grad)
    sums = all_sum(sums, [("dp", n_dp), ("tensor", n_t)])
    penalty = sums[6, 0] / count_total
    share = width // (n_dp * n_t)
    mine = lax.dynamic_index_in_dim(
        sums.reshape(8, n_dp * n_t, share), p * n_t + z, 1, keepdims=False
    )
    return (
        result[None],
        penalty,
        latents_grad[None],
        features_grad[None],
        mine[0],
        mine[1],
        mine[2],
        mine[3],
        mine[4],
        mine[5],
        grad_q,
        jnp.moveaxis(grad_kv, 0, 1),
        grad_o.T,
        up_share,
        down_share.T,
    )


def solution(mesh):
    return jax.shard_map(
        local,
        mesh=mesh,
        in_specs=(
            P("dp", "tensor", None),
            P("dp", "tensor", None),
            P("dp", None),
            P("dp", None),
            P(),
            P(),
            P(),
            P(),
            P(),
            P(),
            P(None, "tensor"),
            P(None, None, "tensor"),
            P("tensor", None),
            P(None, "tensor"),
            P("tensor", None),
            P("dp", "tensor", None),
        ),
        out_specs=(
            P("dp", "tensor", None),
            P(),
            P("dp", "tensor", None),
            P("dp", "tensor", None),
            P(("dp", "tensor")),
            P(("dp", "tensor")),
            P(("dp", "tensor")),
            P(("dp", "tensor")),
            P(("dp", "tensor")),
            P(("dp", "tensor")),
            P("dp", "tensor"),
            P("dp", None, "tensor"),
            P("tensor", "dp"),
            P("dp", "tensor"),
            P("tensor", "dp"),
        ),
        check_vma=False,
    )
```

```python
from functools import partial

import jax
import jax.numpy as jnp
from jax import lax
from jax.experimental import pallas as pl
from jax.experimental.pallas import tpu as pltpu
from jax.sharding import PartitionSpec as P

HD = 96
LAT = 64
EPSILON = 1e-05
NEGATIVE = -1e30
SCALE = HD ** (-0.5)
BF = jnp.bfloat16
F32 = jnp.float32
VMEM_LIMIT = 48 * 1024 * 1024


def rotate(x, count, shift):
    return lax.ppermute(x, "tensor", [(i, (i + shift) % count) for i in range(count)])


def after(x, *done):
    many = isinstance(x, (list, tuple))
    held = lax.optimization_barrier((*x, *done) if many else (x, *done))
    return list(held[: len(x)]) if many else held[0]


def gather_blocks(x, count):
    return [x] + [rotate(x, count, k) for k in range(1, count)]


def send_blocks(blocks, count):
    return [blocks[0]] + [rotate(blocks[k], count, -k) for k in range(1, count)]


def scatter_blocks(blocks, count):
    return add_up(send_blocks(blocks, count))


def partner(x, axis, count, offset):
    return lax.ppermute(x, axis, [(i, i ^ offset) for i in range(count)])


def bits_of(count):
    return count.bit_length() - 1


def gradient_kernel(natural, turned, n_dp, at_ref, xt_ref, y_ref, keep_ref, send_ref, total_ref):
    dims = (((1,), (0,)), ((), ())) if natural else (((1,), (1,)), ((), ()))
    xt = xt_ref[...].T if turned else xt_ref[...]
    total_ref[...] = lax.dot_general(xt, y_ref[...], dims, preferred_element_type=F32)
    p, unit = at_ref[1], keep_ref.shape[1]
    for i in range(n_dp // 2):
        for odd, out in enumerate((keep_ref, send_ref)):
            first = pl.multiple_of((p ^ (2 * i + odd)) * unit, unit)
            out[i] = total_ref[pl.ds(first, unit), :].astype(BF)


def gradient(xt, y, natural, at, n_dp, turned=False):
    width, rows = xt.shape[::-1] if turned else xt.shape
    unit = width // n_dp
    wide = y.shape[1] if natural else y.shape[0]
    step = wide // 3
    half = n_dp // 2
    if natural:
        y_spec = pl.BlockSpec((rows, step), lambda i: (0, i))
    else:
        y_spec = pl.BlockSpec((step, rows), lambda i: (i, 0))
    return pl.pallas_call(
        partial(gradient_kernel, natural, turned, n_dp),
        grid=(3,),
        in_specs=[
            pl.BlockSpec(memory_space=pltpu.SMEM),
            pl.BlockSpec(xt.shape, lambda i: (0, 0)),
            y_spec,
        ],
        out_specs=[pl.BlockSpec((half, unit, step), lambda i: (0, 0, i))] * 2,
        out_shape=[pltpu.HBM((half, unit, wide), BF)] * 2,
        scratch_shapes=[pltpu.VMEM((width, step), F32)],
        compiler_params=pltpu.CompilerParams(vmem_limit_bytes=24 * 1024 * 1024),
    )(at, xt, y)


def bit_orders(count):
    outer = list(range(1, bits_of(count)))
    half = (len(outer) + 1) // 2
    return outer, outer[half:] + outer[:half]


def cut_kernel(widths, *refs):
    ins, (keep_ref, send_ref) = refs[:-2], refs[-2:]
    start = 0
    for i, wide in enumerate(widths):
        lanes = slice(start, start + wide)
        keep_a, got_a, keep_b, got_b = ins[4 * i : 4 * i + 4]
        keep_ref[:, :, lanes] = (keep_a[...].astype(F32) + got_a[...].astype(F32)).astype(BF)
        send_ref[:, :, lanes] = (keep_b[...].astype(F32) + got_b[...].astype(F32)).astype(BF)
        start += wide


def reduce_cut(parts, order, step, n_dp):
    left = [b for b in range(bits_of(n_dp) - 1, 0, -1) if b not in order[:step]]
    low = 1 << (len(left) - left.index(order[step]) - 1)
    count, rows, _ = parts[0][0].shape
    widths, specs, flat = [], [], []
    for keep, got, half in parts:
        wide = keep.shape[2] if half is None else keep.shape[2] // 2

        def at(bit, wide=wide, lane=half or 0):
            return pl.BlockSpec(
                (1, rows, wide), lambda i: (i // low * (2 * low) + bit * low + i % low, 0, lane)
            )

        widths.append(wide)
        specs += [at(0), at(0), at(1), at(1)]
        flat += [keep, got, keep, got]
    total = sum(widths)
    return pl.pallas_call(
        partial(cut_kernel, widths),
        grid=(count // 2,),
        in_specs=specs,
        out_specs=[pl.BlockSpec((1, rows, total), lambda i: (i, 0, 0))] * 2,
        out_shape=[pltpu.HBM((count // 2, rows, total), BF)] * 2,
        compiler_params=pltpu.CompilerParams(vmem_limit_bytes=20 * 1024 * 1024),
    )(*flat)


def first_cut(one, two, split, orders, n_dp):
    out = []
    for h, full in enumerate((one, two)):
        parts = [(*full, None)] if full else []
        parts += [(*split, h)] if split else []
        out.append(reduce_cut(parts, orders[h], 0, n_dp))
    return out


def next_cut(pair, orders, step, n_dp):
    return [reduce_cut([(*x, None)], order, step, n_dp) for x, order in zip(pair, orders)]


def cross(pair, orders, step, n_dp):
    return [
        (keep, partner(send, "dp", n_dp, 1 << order[step])) for (keep, send), order in zip(pair, orders)
    ]


def add_up(terms):
    total = terms[0].astype(F32)
    for term in terms[1:]:
        total = total + term.astype(F32)
    return total


def blocks_kernel(n_t, weights, at_ref, *refs):
    (a_keep, a_got, b_keep, b_got), outs = refs[:4], refs[4:]
    pairs = (a_keep, a_got), (b_keep, b_got)
    z = at_ref[0]
    columns = outs[0].shape[-1]
    half = n_t // 2

    def piece(which, lane):
        lanes = pl.ds(pl.multiple_of(lane, columns), columns)
        keep, got = pairs[which]
        return keep[0, :, lanes].astype(F32) + got[0, :, lanes].astype(F32)

    for k in range(n_t):
        block = lax.rem(z - k + n_t, n_t)
        for m, which in enumerate(weights):
            if which is None:
                lane = (a_keep.shape[2] - columns * half) + lax.rem(block, half) * columns
                value = jnp.where(block >= half, piece(1, lane), piece(0, lane))
            else:
                value = piece(which, block * columns)
            outs[k][m] = value.astype(outs[k].dtype)


def tensor_blocks(pair, weights, columns, at, n_t):
    flat = [x for terms in pair for x in terms]
    rows = flat[0].shape[1]
    return pl.pallas_call(
        partial(blocks_kernel, n_t, weights),
        in_specs=[pl.BlockSpec(memory_space=pltpu.SMEM)]
        + [pl.BlockSpec(memory_space=pltpu.VMEM)] * len(flat),
        out_shape=[
            jax.ShapeDtypeStruct((len(weights), rows, columns // n_t), F32 if k == 0 else BF)
            for k in range(n_t)
        ],
        compiler_params=pltpu.CompilerParams(vmem_limit_bytes=14 * 1024 * 1024),
    )(at, *flat)


def all_sum(x, axes):
    for axis, count in axes:
        for bit in range(bits_of(count)):
            x = x + partner(x, axis, count, 1 << bit)
    return x


def place_kernel(n_t, unit, z_rows, z_cols, offsets, parts, at_ref, own_ref, *refs):
    out_ref = refs[-1]
    z, p = at_ref[0], at_ref[1]
    rows, cols = own_ref.shape
    if z_rows:
        out_ref[pl.ds(pl.multiple_of(z * z_rows, z_rows), rows), :] = own_ref[...]
    else:
        out_ref[:, pl.ds(pl.multiple_of(z * z_cols, z_cols), cols)] = own_ref[...]
    for k in range(1, n_t):
        shard = lax.rem(z - k + n_t, n_t)
        for which, first, height, row_at, col_at in parts:
            for odd in range(2):
                src = refs[2 * which + odd]
                wide = src.shape[3]
                for i, off in enumerate(offsets[which]):
                    base = shard * z_rows + (p ^ (off ^ odd)) * unit + row_at
                    where = pl.ds(pl.multiple_of(base, 16), height)
                    if z_cols:
                        at = pl.ds(pl.multiple_of(shard * z_cols, z_cols), wide)
                    else:
                        at = slice(col_at, col_at + wide)
                    out_ref[where, at] = src[i, k - 1, first : first + height, :]


def reorder(x, places):
    return jnp.stack([lax.dynamic_index_in_dim(x, i, 0, keepdims=False) for i in places])


def project_kernel(place_kernel, count, at_ref, x_ref, *refs):
    place_kernel(at_ref, *refs[:-2])
    weight_ref, out_ref, turned_ref = refs[-3:]
    turned_ref[...] = x_ref[...].T
    step = weight_ref.shape[1] // count
    for c in range(count):
        cols = slice(c * step, (c + 1) * step)
        block = jnp.dot(x_ref[...], weight_ref[:, cols], preferred_element_type=F32)
        out_ref[cols, :] = block.T.astype(BF)


def place(own, pieces, offsets, parts, unit, by_rows, at, n_dp, n_t, x=None):
    rows, cols = own.shape
    shape = (n_t * rows, cols) if by_rows else (rows, n_t * cols)
    if unit % 16 or any(part[2] % 16 for part in parts):
        z, p = at[0], at[1]
        across = []
        for which, first, height, _, _ in parts:
            ordered = [None] * n_dp
            for i, off in enumerate(offsets[which]):
                for odd in range(2):
                    ordered[off ^ odd] = pieces[which][odd][i, :, first : first + height]
            across.append(reorder(jnp.stack(ordered), [p ^ d for d in range(n_dp)]))
        whole = jnp.concatenate(across, axis=3 if by_rows else 2).transpose(1, 0, 2, 3)
        whole = whole.reshape((n_t - 1, rows, cols))
        whole = jnp.concatenate([own[None], whole], axis=0)
        whole = reorder(whole, [(z - k + n_t) % n_t for k in range(n_t)])
        whole = whole.reshape(shape) if by_rows else whole.transpose(1, 0, 2).reshape(shape)
        return whole if x is None else (whole, dot("dh,rd->hr", whole, x).astype(BF), x.T)
    flat = [x for pair in pieces for x in pair]
    kernel = partial(
        place_kernel, n_t, unit, rows if by_rows else 0, 0 if by_rows else cols, offsets, parts
    )
    out = jax.ShapeDtypeStruct(shape, own.dtype)
    if x is None:
        first, outs = [], out
    else:
        kernel, first = partial(project_kernel, kernel, n_t), [x]
        outs = [out] + [jax.ShapeDtypeStruct((n, x.shape[0]), BF) for n in (shape[1], x.shape[1])]
    ins = [*first, own, *flat]
    return pl.pallas_call(
        kernel,
        out_shape=outs,
        in_specs=[pl.BlockSpec(memory_space=pltpu.SMEM)]
        + [pl.BlockSpec(memory_space=pltpu.VMEM)] * len(ins),
        compiler_params=pltpu.CompilerParams(vmem_limit_bytes=28 * 1024 * 1024),
    )(at, *ins)


def rotations(x, count):
    return [rotate(x, count, k) for k in range(1, count)]


def widen(one, two, step, orders, n_dp, *done):
    arrived = [partner(x, "dp", n_dp, 1 << order[step]) for x, order in zip((one, two), orders)]
    if done:
        arrived = after(arrived, *done)
    return [jnp.concatenate(x, axis=0) for x in zip((one, two), arrived)]


def widen_offsets(order):
    offsets = [0]
    for bit in order:
        offsets = offsets + [o ^ (1 << bit) for o in offsets]
    return offsets


def cores(one, two, n_dp):
    return [(x, partner(x, "dp", n_dp, 1)) for x in (one, two)]


def share_of(x, axis, count):
    size = x.shape[axis] // count
    return lax.dynamic_slice_in_dim(x, lax.axis_index("dp") * size, size, axis)


def three(x):
    high = x.astype(BF)
    left = x - high.astype(F32)
    middle = left.astype(BF)
    low = (left - middle.astype(F32)).astype(BF)
    return jnp.concatenate([high, middle, low], axis=0)


def join(x, count):
    x = x.astype(F32)
    return x[:count] + x[count : 2 * count] + x[2 * count :]


GROUP = 8
CHUNK = 128
TN = (((0,), (0,)), ((), ()))
NT = (((1,), (1,)), ((), ()))


def forward_kernel(heads, n_t, span_ref, q_ref, k_ref, v_ref, seg_ref, img_ref, *rest):
    msgs, stat, acc, run = rest[:n_t], rest[n_t], rest[n_t + 1], rest[n_t + 2]
    g = pl.program_id(0)
    rows = q_ref.shape[1] // n_t
    keys = k_ref.shape[1]
    for k in range(n_t):
        cols = slice(k * rows, (k + 1) * rows)
        image = img_ref[:, cols]
        acc[...] = jnp.zeros_like(acc)
        run[...] = jnp.zeros_like(run)
        run[0] = jnp.full(run.shape[1:], NEGATIVE)

        def step(at, cols=cols, image=image):
            allowed = seg_ref[at, :] == image
            bands = [slice(h * HD, (h + 1) * HD) for h in range(GROUP)]
            scores = [
                SCALE
                * lax.dot_general(k_ref[b, at], q_ref[b, cols], TN, preferred_element_type=F32)
                for b in bands
            ]
            scores = [jnp.where(allowed, x, NEGATIVE) for x in scores]
            old = [run[0, h : h + 1] for h in range(GROUP)]
            tops = [
                jnp.maximum(m, jnp.max(x, axis=0, keepdims=True)) for m, x in zip(old, scores)
            ]
            weights = [jnp.where(allowed, jnp.exp(x - m), 0.0) for x, m in zip(scores, tops)]
            outs = [
                jnp.dot(v_ref[b, at], w.astype(BF), preferred_element_type=F32)
                for b, w in zip(bands, weights)
            ]
            fades = [jnp.exp(m - n) for m, n in zip(old, tops)]
            for h in range(GROUP):
                run[0, h : h + 1] = tops[h]
                run[1, h : h + 1] = run[1, h : h + 1] * fades[h] + jnp.sum(
                    weights[h], axis=0, keepdims=True
                )
                run[2, h : h + 1] = run[2, h : h + 1] * fades[h] + jnp.sum(
                    weights[h] * scores[h], axis=0, keepdims=True
                )
            for b, f, o in zip(bands, fades, outs):
                acc[b, :] = acc[b, :] * f + o

        if k == 0:
            step(slice(keys - rows, keys))

        @pl.loop(span_ref[0, k], span_ref[1, k])
        def _(c, step=step):
            step(pl.ds(pl.multiple_of(c * CHUNK, CHUNK), CHUNK))

        total = run[1, :GROUP]
        some = total > 0.0
        safe = jnp.where(some, total, 1.0)
        inverse = jnp.where(some, 1.0 / safe, 0.0)
        stat[0, pl.ds(g, 1), :, cols] = jnp.where(some, run[0, :GROUP] + jnp.log(safe), NEGATIVE)[None]
        stat[1, pl.ds(g, 1), :, cols] = (run[2, :GROUP] * inverse)[None]
        for h in range(GROUP):
            band = slice(h * HD, (h + 1) * HD)
            first = pl.multiple_of((g * GROUP + h) * HD, HD)
            msgs[k][pl.ds(first, HD), :] = (acc[band, :] * inverse[h : h + 1]).astype(BF)

    @pl.when(g == heads // GROUP - 1)
    def _():
        for k in range(n_t):
            cols = slice(k * rows, (k + 1) * rows)
            for i in range(2):
                first = heads * (HD + 3 * i)
                msgs[k][first : first + 3 * heads, :] = three(
                    stat[i, :, :, cols].reshape(heads, rows)
                )


def attend_forward(q, k, v, seg, img, span, n_t):
    heads = q.shape[0] // HD
    rows, keys = q.shape[1], k.shape[1]
    one = rows // n_t
    tall = heads * (HD + 6)
    band = GROUP * HD
    return pl.pallas_call(
        partial(forward_kernel, heads, n_t),
        grid_spec=pltpu.PrefetchScalarGridSpec(
            num_scalar_prefetch=1,
            grid=(heads // GROUP,),
            in_specs=[
                pl.BlockSpec((band, rows), lambda g, s: (g, 0)),
                pl.BlockSpec((band, keys), lambda g, s: (g, 0)),
                pl.BlockSpec((band, keys), lambda g, s: (g, 0)),
                pl.BlockSpec((keys, 1), lambda g, s: (0, 0)),
                pl.BlockSpec((1, rows), lambda g, s: (0, 0)),
            ],
            out_specs=[pl.BlockSpec((tall, one), lambda g, s: (0, 0))] * n_t,
            scratch_shapes=[
                pltpu.VMEM((2, heads // GROUP, GROUP, rows), F32),
                pltpu.VMEM((band, one), F32),
                pltpu.VMEM((3, 8, one), F32),
            ],
        ),
        out_shape=[jax.ShapeDtypeStruct((tall, one), BF)] * n_t,
        compiler_params=pltpu.CompilerParams(vmem_limit_bytes=20 * 1024 * 1024),
    )(span, q, k, v, seg, img)


def combine_kernel(heads, n_t, *refs):
    msgs, (out_ref, stat_ref) = refs[:n_t], refs[n_t:]
    base = heads * HD
    logs = [join(m[base : base + 3 * heads, :], heads) for m in msgs]
    means = [join(m[base + 3 * heads :, :], heads) for m in msgs]
    top = logs[0]
    for x in logs[1:]:
        top = jnp.maximum(top, x)
    shares = [jnp.exp(x - top) for x in logs]
    total = shares[0]
    for x in shares[1:]:
        total = total + x
    shares = [x / total for x in shares]
    mean = shares[0] * means[0]
    for s, x in zip(shares[1:], means[1:]):
        mean = mean + s * x
    stat_ref[:heads, :] = top + jnp.log(total)
    stat_ref[heads:, :] = mean
    for h in range(heads):
        at = slice(h * HD, (h + 1) * HD)
        acc = msgs[0][at, :].astype(F32) * shares[0][h : h + 1, :]
        for s, m in zip(shares[1:], msgs[1:]):
            acc = acc + m[at, :].astype(F32) * s[h : h + 1, :]
        out_ref[at, :] = acc.astype(BF)


def combine(msgs, heads):
    one = msgs[0].shape[1]
    return pl.pallas_call(
        partial(combine_kernel, heads, len(msgs)),
        out_shape=[
            jax.ShapeDtypeStruct((heads * HD, one), BF),
            jax.ShapeDtypeStruct((2 * heads, one), F32),
        ],
        compiler_params=pltpu.CompilerParams(vmem_limit_bytes=8 * 1024 * 1024),
    )(*msgs)


def message_kernel(heads, do_ref, out_ref, stat_ref, coef_ref, msg_ref):
    base = heads * HD
    deltas = []
    for h in range(heads):
        at = slice(h * HD, (h + 1) * HD)
        grad = do_ref[at, :].astype(F32)
        deltas.append(jnp.sum(grad * out_ref[at, :].astype(F32), axis=0, keepdims=True))
    msg_ref[:base, :] = do_ref[...]
    delta = jnp.concatenate(deltas, axis=0) - coef_ref[...] * stat_ref[heads:, :]
    msg_ref[base : base + 3 * heads, :] = three(stat_ref[:heads, :])
    msg_ref[base + 3 * heads :, :] = three(delta)


def make_message(do, out, stat, coef, heads):
    return pl.pallas_call(
        partial(message_kernel, heads),
        out_shape=jax.ShapeDtypeStruct((heads * (HD + 6), do.shape[1]), BF),
        compiler_params=pltpu.CompilerParams(vmem_limit_bytes=6 * 1024 * 1024),
    )(do, out, stat, coef)


def backward_kernel(heads, n_t, span_ref, q_ref, k_ref, v_ref, seg_ref, img_ref, coef_ref, *rest):
    grads, stats = rest[:n_t], rest[n_t : 2 * n_t]
    dq_ref, dk_ref, dv_ref, stat, dq, dk, dv = rest[2 * n_t :]
    g = pl.program_id(0)
    rows = q_ref.shape[1] // n_t
    keys = k_ref.shape[1]

    @pl.when(g == 0)
    def _():
        for i in range(n_t):
            cols = slice(i * rows, (i + 1) * rows)
            for j in range(2):
                part = join(stats[i][3 * j * heads : 3 * (j + 1) * heads, :], heads)
                stat[j, :, :, cols] = part.reshape(heads // GROUP, GROUP, rows)

    dk[...] = jnp.zeros_like(dk)
    dv[...] = jnp.zeros_like(dv)
    for i in range(n_t):
        cols = slice(i * rows, (i + 1) * rows)
        image, coef = img_ref[:, cols], coef_ref[:, cols]
        logs = stat[0, pl.ds(g, 1), :, cols][0]
        deltas = stat[1, pl.ds(g, 1), :, cols][0]
        dq[...] = jnp.zeros_like(dq)

        def step(at, cols=cols, image=image, coef=coef, logs=logs, deltas=deltas, grad_ref=grads[i]):
            allowed = seg_ref[at, :] == image
            bands = [slice(h * HD, (h + 1) * HD) for h in range(GROUP)]
            scores = [
                SCALE
                * lax.dot_general(k_ref[b, at], q_ref[b, cols], TN, preferred_element_type=F32)
                for b in bands
            ]
            back_probs = [
                lax.dot_general(v_ref[b, at], grad_ref[b, :], TN, preferred_element_type=F32)
                for b in bands
            ]
            probs = [
                jnp.where(allowed, jnp.exp(jnp.where(allowed, x - logs[h : h + 1], 0.0)), 0.0)
                for h, x in enumerate(scores)
            ]
            backs = [
                (p * (y - coef * x - deltas[h : h + 1])).astype(BF)
                for h, (x, y, p) in enumerate(zip(scores, back_probs, probs))
            ]
            probs = [p.astype(BF) for p in probs]
            for b, p in zip(bands, probs):
                dv[b, at] += lax.dot_general(grad_ref[b, :], p, NT, preferred_element_type=F32)
            for b, x in zip(bands, backs):
                dq[b, :] += jnp.dot(k_ref[b, at], x, preferred_element_type=F32)
            for b, x in zip(bands, backs):
                dk[b, at] += lax.dot_general(q_ref[b, cols], x, NT, preferred_element_type=F32)

        if i == 0:
            step(slice(keys - rows, keys))

        @pl.loop(span_ref[0, i], span_ref[1, i])
        def _(c, step=step):
            step(pl.ds(pl.multiple_of(c * CHUNK, CHUNK), CHUNK))

        dq_ref[:, cols] = (dq[...] * SCALE).astype(BF)
    dk_ref[...] = (dk[...] * SCALE).astype(BF)
    dv_ref[...] = dv[...].astype(BF)


def attend_backward(q, k, v, seg, img, coef, span, msgs):
    n_t = len(msgs)
    heads = q.shape[0] // HD
    rows, keys = q.shape[1], k.shape[1]
    one = rows // n_t
    band = GROUP * HD
    wide = [pl.BlockSpec((band, n), lambda g, s: (g, 0)) for n in (rows, keys, keys)]
    return pl.pallas_call(
        partial(backward_kernel, heads, n_t),
        grid_spec=pltpu.PrefetchScalarGridSpec(
            num_scalar_prefetch=1,
            grid=(heads // GROUP,),
            in_specs=wide
            + [
                pl.BlockSpec((keys, 1), lambda g, s: (0, 0)),
                pl.BlockSpec((1, rows), lambda g, s: (0, 0)),
                pl.BlockSpec((1, rows), lambda g, s: (0, 0)),
            ]
            + [pl.BlockSpec((band, one), lambda g, s: (g, 0))] * n_t
            + [pl.BlockSpec((6 * heads, one), lambda g, s: (HD // 6, 0))] * n_t,
            out_specs=wide,
            scratch_shapes=[
                pltpu.VMEM((2, heads // GROUP, GROUP, rows), F32),
                pltpu.VMEM((band, one), F32),
                pltpu.VMEM((band, keys), F32),
                pltpu.VMEM((band, keys), F32),
            ],
        ),
        out_shape=[
            jax.ShapeDtypeStruct(q.shape, BF),
            jax.ShapeDtypeStruct(k.shape, BF),
            jax.ShapeDtypeStruct(v.shape, BF),
        ],
        compiler_params=pltpu.CompilerParams(vmem_limit_bytes=36 * 1024 * 1024),
        cost_estimate=pl.CostEstimate(
            flops=60 * heads * HD * rows * keys,
            bytes_accessed=60 * 1024 * 1024,
            transcendentals=heads * rows * keys,
        ),
    )(span, q, k, v, seg, img, coef, *msgs, *msgs)


def norm_parts(values):
    values = values.astype(F32)
    center = values - jnp.mean(values, axis=-1, keepdims=True)
    inv_root = lax.rsqrt(jnp.mean(center * center, axis=-1, keepdims=True) + EPSILON)
    return center * inv_root, inv_root


def norm_backward(grad_rows, normal, inv_root, gain_row):
    scaled = grad_rows * gain_row
    reduced = (
        scaled
        - jnp.mean(scaled, axis=-1, keepdims=True)
        - normal * jnp.mean(scaled * normal, axis=-1, keepdims=True)
    )
    return reduced * inv_root


def gain_shift(grad_rows, normal):
    return [jnp.sum(grad_rows * normal, axis=0), jnp.sum(grad_rows, axis=0)]


def rows_back(grads, weights):
    total = None
    for grad, weight in zip(grads, weights):
        term = lax.dot_general(grad, weight, (((0,), (1,)), ((), ())), preferred_element_type=F32)
        total = term if total is None else total + term
    return total


def media_back_kernel(dk_ref, dv_ref, wk_ref, wv_ref, x_ref, gain_ref, out_ref, sums_ref):
    back = rows_back((dk_ref[...], dv_ref[...]), (wk_ref[...], wv_ref[...]))
    normal, root = norm_parts(x_ref[...])
    out_ref[...] = norm_backward(back, normal, root, gain_ref[...])

    @pl.when(pl.program_id(0) == 0)
    def _():
        sums_ref[...] = jnp.zeros_like(sums_ref)

    sums_ref[0:1] += jnp.sum(back * normal, axis=0, keepdims=True)
    sums_ref[1:2] += jnp.sum(back, axis=0, keepdims=True)


def media_back(back_k, back_v, wk, wv, features, gain, block):
    rows, width = features.shape
    inner = back_k.shape[0]
    whole = pl.BlockSpec((width, inner), lambda i: (0, 0))
    return pl.pallas_call(
        media_back_kernel,
        grid=(rows // block,),
        in_specs=[pl.BlockSpec((inner, block), lambda i: (0, i))] * 2
        + [whole] * 2
        + [pl.BlockSpec((block, width), lambda i: (i, 0)), pl.BlockSpec((1, width), lambda i: (0, 0))],
        out_specs=[
            pl.BlockSpec((block, width), lambda i: (i, 0)),
            pl.BlockSpec((8, width), lambda i: (0, 0)),
        ],
        out_shape=[
            jax.ShapeDtypeStruct((rows, width), F32),
            jax.ShapeDtypeStruct((8, width), F32),
        ],
        compiler_params=pltpu.CompilerParams(vmem_limit_bytes=VMEM_LIMIT),
    )(back_k, back_v, wk, wv, features, gain[None])


def latent_back_kernel(n_t, dq_ref, dk_ref, dv_ref, wq_ref, wk_ref, wv_ref, *refs):
    xs, outs, sums_ref = refs[:n_t], refs[n_t:-1], refs[-1]
    rows = xs[0].shape[0]
    gain_sum = shift_sum = None
    total = rows_back((dq_ref[...],), (wq_ref[...],))
    own = rows_back((dk_ref[...], dv_ref[...]), (wk_ref[...], wv_ref[...]))
    for k in range(n_t):
        back = total[k * rows : (k + 1) * rows]
        if k == 0:
            back = back + own
        outs[k][...] = back.astype(outs[k].dtype)
        normal, _ = norm_parts(xs[k][...])
        gain_part = jnp.sum(back * normal, axis=0, keepdims=True)
        shift_part = jnp.sum(back, axis=0, keepdims=True)
        gain_sum = gain_part if gain_sum is None else gain_sum + gain_part
        shift_sum = shift_part if shift_sum is None else shift_sum + shift_part
    sums_ref[...] = jnp.zeros_like(sums_ref)
    sums_ref[0:1] = gain_sum
    sums_ref[1:2] = shift_sum


def latent_back(back_q, back_k, back_v, wq, wk, wv, blocks):
    n_t = len(blocks)
    rows, width = blocks[0].shape
    inner, keys = back_k.shape
    tail = pl.BlockSpec((inner, rows), lambda i: (0, keys // rows - 1))
    whole = pl.BlockSpec((width, inner), lambda i: (0, 0))
    return pl.pallas_call(
        partial(latent_back_kernel, n_t),
        grid=(1,),
        in_specs=[pl.BlockSpec(back_q.shape, lambda i: (0, 0)), tail, tail, whole, whole, whole]
        + [pl.BlockSpec((rows, width), lambda i: (0, 0))] * n_t,
        out_specs=[pl.BlockSpec((rows, width), lambda i: (0, 0))] * n_t
        + [pl.BlockSpec((8, width), lambda i: (0, 0))],
        out_shape=[jax.ShapeDtypeStruct((rows, width), BF if k else F32) for k in range(n_t)]
        + [jax.ShapeDtypeStruct((8, width), F32)],
        compiler_params=pltpu.CompilerParams(vmem_limit_bytes=50 * 1024 * 1024),
    )(back_q, back_k, back_v, wq, wk, wv, *blocks)


def blocks_of_product_kernel(n_t, a_ref, b_ref, *outs):
    total = jnp.dot(a_ref[...], b_ref[...], preferred_element_type=F32)
    rows = outs[0].shape[0]
    for k in range(n_t):
        outs[k][...] = total[k * rows : (k + 1) * rows].astype(outs[k].dtype)


def blocks_of_product(a, b, n_t):
    shape = a.shape[0] // n_t, b.shape[1]
    return list(
        pl.pallas_call(
            partial(blocks_of_product_kernel, n_t),
            out_shape=[jax.ShapeDtypeStruct(shape, BF if k else F32) for k in range(n_t)],
            compiler_params=pltpu.CompilerParams(vmem_limit_bytes=VMEM_LIMIT),
        )(a, b)
    )


def finish_kernel(n_t, columns, *refs):
    results, latent_terms, feeds = refs[:n_t], refs[n_t : 2 * n_t], refs[2 * n_t : 2 * n_t + 4]
    middle_ref, back_ref, x_ref, gain_ref, *outs = refs[2 * n_t + 4 :]
    outs[0][...] = (middle_ref[...] + add_up([r[...] for r in results])).astype(BF)
    normal, root = norm_parts(x_ref[...])
    back = add_up([r[...] for r in latent_terms])
    outs[1][...] = back_ref[...] + norm_backward(back, normal, root, gain_ref[...])
    for m in range(2):
        keep, got = feeds[2 * m], feeds[2 * m + 1]
        outs[2 + m][...] = keep[0, :, :columns].astype(F32) + got[0, :, :columns].astype(F32)


def finish(result_terms, latent_terms, feed_pair, middle, back_middle, latents, gain, columns):
    feeds = [x for pair in feed_pair for x in pair]
    unit, width = feeds[0].shape[1], middle.shape[1]
    return pl.pallas_call(
        partial(finish_kernel, len(result_terms), columns),
        out_shape=[
            jax.ShapeDtypeStruct(middle.shape, BF),
            jax.ShapeDtypeStruct(middle.shape, F32),
            jax.ShapeDtypeStruct((unit, columns), F32),
            jax.ShapeDtypeStruct((unit, columns), F32),
        ],
        compiler_params=pltpu.CompilerParams(vmem_limit_bytes=20 * 1024 * 1024),
    )(*result_terms, *latent_terms, *feeds, middle, back_middle, latents, gain[None])


def dot(equation, a, b):
    return jnp.einsum(equation, a, b, preferred_element_type=F32)


def local(
    latents,
    features,
    lengths,
    valid_media,
    media_gain,
    media_shift,
    latent_gain,
    latent_shift,
    feed_gain,
    feed_shift,
    query_weight,
    key_value_weight,
    output_weight,
    up_weight,
    down_weight,
    cotangent,
):
    n_t = lax.axis_size("tensor")
    n_dp = lax.axis_size("dp")
    z, p = lax.axis_index("tensor"), lax.axis_index("dp")
    at = jnp.stack([z, p]).astype(jnp.int32)
    latents, features, cotangent = latents[0], features[0], cotangent[0]
    lengths, valid = lengths[0], valid_media[0]
    width = latents.shape[1]
    own_rows, own_patches = latents.shape[0], features.shape[0]
    inner = query_weight.shape[1] * n_t
    heads = inner // HD
    images = lengths.shape[0]


    ends = jnp.sum(
        jnp.where(jnp.arange(images)[:, None] <= jnp.arange(images)[None, :], lengths[:, None], 0),
        axis=0,
    )
    positions = z * own_patches + jnp.arange(own_patches, dtype=jnp.int32)
    segment = jnp.sum((positions[:, None] >= ends[None, :]).astype(jnp.int32), axis=1)
    hit = segment[:, None] == jnp.arange(images, dtype=jnp.int32)[None, :]
    patch_valid = jnp.sum(jnp.where(hit, valid[None, :], 0), axis=1)
    patch_segment = jnp.where(patch_valid > 0, segment, -1)
    own_images = (z * own_rows + jnp.arange(own_rows, dtype=jnp.int32)) // LAT
    key_image = jnp.concatenate([patch_segment, own_images])[:, None]
    block_of = (z - jnp.arange(n_t, dtype=jnp.int32) + n_t) % n_t
    row_index = block_of[:, None] * own_rows + jnp.arange(own_rows, dtype=jnp.int32)[None, :]
    row_image = (row_index // LAT).reshape(1, -1)
    rows_each = own_rows // LAT
    local_ends = jnp.clip(ends - z * own_patches, 0, own_patches)
    local_starts = jnp.clip(ends - lengths - z * own_patches, 0, own_patches)
    block_image = block_of * rows_each
    at_image = jnp.arange(images, dtype=jnp.int32)[None, :]
    low = jnp.sum(jnp.where(at_image == block_image[:, None], local_starts[None, :], 0), axis=1)
    high = jnp.sum(
        jnp.where(at_image == block_image[:, None] + rows_each - 1, local_ends[None, :], 0), axis=1
    )
    span = jnp.stack([low // CHUNK, (high + CHUNK - 1) // CHUNK]).astype(jnp.int32)
    row_valid = jnp.sum(
        jnp.where(row_image.T == jnp.arange(images, dtype=jnp.int32)[None, :], valid[None, :], 0),
        axis=1,
    ).astype(F32)[None, :]

    orders = bit_orders(n_dp)
    steps = range(len(orders[0]))
    offsets = [widen_offsets(order) for order in orders]
    unit, part = width // n_dp, query_weight.shape[1]
    keyval = jnp.moveaxis(share_of(key_value_weight, 0, n_dp), 1, 0)
    kv_z = rotations(keyval, n_t)
    media_hat, media_root = norm_parts(features)
    media_normed = (media_hat * media_gain + media_shift).astype(BF)
    own_hat, own_root = norm_parts(latents)
    own_normed = (own_hat * latent_gain + latent_shift).astype(BF)
    key_input = jnp.concatenate([media_normed, own_normed], axis=0)
    kv_own = [key_value_weight[:, 0], key_value_weight[:, 1]]
    *kv_z, key_input, k_own, v_own = after([*kv_z, key_input, *kv_own])
    q_share = share_of(query_weight, 0, n_dp).reshape(2, unit // 2, part)
    o_share = share_of(output_weight, 0, n_dp)
    o_unit = o_share.shape[0]
    o_share = o_share.reshape(o_unit, 2, -1, part).transpose(1, 2, 0, 3).reshape(2, -1, part)
    qo_share = jnp.concatenate([q_share, o_share], axis=1)
    qo_z = rotations(after(qo_share, *kv_z), n_t)
    k_held, v_held = [jnp.stack([x[m] for x in kv_z])[None] for m in range(2)]
    for step in steps[:-1]:
        k_held, v_held = widen(k_held, v_held, step, orders, n_dp)
    k_held, v_held = after([k_held, v_held], *qo_z)
    gathered = lax.all_gather(jnp.stack(after([latents, cotangent], *qo_z)), "tensor", axis=0)
    others = [
        lax.dynamic_index_in_dim(gathered, (z - k + n_t) % n_t, 0, keepdims=False)
        for k in range(1, n_t)
    ]
    latent_blocks = [latents] + [x[0] for x in others]
    cot_blocks = [cotangent] + [x[1] for x in others]
    k_held, v_held = widen(k_held, v_held, steps[-1], orders, n_dp)
    k_pieces, v_pieces = cores(k_held, v_held, n_dp)
    qo_held = [jnp.stack([x[m] for x in qo_z])[None] for m in range(2)]
    qo_held = after(qo_held, k_held, v_held)
    whole = [(0, 0, unit, 0, 0)]
    wk, keys, key_input_t = place(k_own, [k_pieces], offsets[:1], whole, unit, False, at, n_dp, n_t, key_input)
    wv, values, _ = place(v_own, [v_pieces], offsets[1:], whole, unit, False, at, n_dp, n_t, key_input)
    for step in steps[:-1]:
        qo_held = widen(*qo_held, step, orders, n_dp, keys)
    qo_held = widen(*qo_held, steps[-1], orders, n_dp, values)
    qo_pieces = cores(*qo_held, n_dp)
    latent_all = jnp.concatenate(latent_blocks, axis=0)
    latent_hat, latent_root = norm_parts(latent_all)
    latent_normed = (latent_hat * latent_gain + latent_shift).astype(BF)
    cuts = [(h, 0, unit // 2, h * unit // 2, 0) for h in range(2)]
    wq, queries, latent_t = place(
        query_weight, qo_pieces, offsets, cuts, unit, False, at, n_dp, n_t, latent_normed
    )
    cuts = [
        (h, unit // 2 + c * o_unit, o_unit, 0, h * width // 2 + c * part)
        for h in range(2)
        for c in range(width // 2 // part)
    ]
    wo = place(output_weight, qo_pieces, offsets, cuts, o_unit, True, at, n_dp, n_t)
    sent = attend_forward(queries, keys, values, key_image, row_image, span, n_t)
    sent = after(sent, wo)
    got = [sent[0]] + [rotate(sent[k], n_t, -k) for k in range(1, n_t)]
    count_part = after(jnp.full((8, 128), jnp.sum(valid).astype(F32)), *sent[1:])
    count_total = all_sum(count_part, [("dp", n_dp)])[0, 0]
    got = after(got, count_total)
    attended, stat = combine(got, heads)
    entropy = stat[:heads] - stat[heads:]
    own_valid = row_valid[:, :own_rows]
    penalty_part = jnp.sum(entropy * own_valid)

    latent_own = latents.astype(F32)
    middle = latent_own + dot("hr,hd->rd", attended, wo)
    feed_hat, feed_root = norm_parts(middle)
    feed_normed = (feed_hat * feed_gain + feed_shift).astype(BF)
    feed_all = jnp.concatenate(gather_blocks(feed_normed, n_t), axis=0)
    cot_all = jnp.concatenate(after(cot_blocks, feed_normed), axis=0)
    hidden = dot("rd,df->rf", feed_all, up_weight)
    cdf = 0.5 * (1.0 + lax.erf(hidden * (0.5**0.5)))
    slope = cdf + hidden * jnp.exp(-0.5 * hidden * hidden) * (0.5 / jnp.pi) ** 0.5
    activation = (hidden * cdf).astype(BF)
    back_activation = dot("rd,fd->rf", cot_all, down_weight)
    back_hidden = (back_activation * slope).astype(BF)
    back_terms = dot("rf,df->rd", back_hidden, up_weight).astype(BF)
    back_blocks = [back_terms[k * own_rows : (k + 1) * own_rows] for k in range(n_t)]
    back_arrived = send_blocks(back_blocks, n_t)
    late_activation, late_hidden = after([activation, back_hidden], back_terms)
    down_keep, down_send = gradient(cot_all.T, late_activation, True, at, n_dp)
    up_keep, up_send = gradient(feed_all.T, late_hidden, True, at, n_dp)
    result_terms = blocks_of_product(late_activation, down_weight, n_t)
    back_feed = add_up(after(back_arrived, down_send, up_send, *result_terms))
    down_got, up_got = partner(down_send, "dp", n_dp, 1), partner(up_send, "dp", n_dp, 1)

    back_middle = cotangent.astype(F32) + norm_backward(back_feed, feed_hat, feed_root, feed_gain)
    back_branch = back_middle.astype(BF)
    back_attended = dot("hd,rd->hr", wo, back_branch).astype(BF)
    own_coef = own_valid / count_total
    message = make_message(back_attended, attended, stat, own_coef, heads)
    messages = gather_blocks(message, n_t)
    out_keep, out_send = gradient(back_branch, attended, False, at, n_dp, True)
    out_got = partner(out_send, "dp", n_dp, 1)
    down_got, up_got, out_got = after([down_got, up_got, out_got], message)
    feed_pair = first_cut((down_keep, down_got), (up_keep, up_got), (out_keep, out_got), orders, n_dp)
    messages = after(messages, *[send for _, send in feed_pair])
    result_terms[1:] = after(result_terms[1:], *messages)
    result_terms = send_blocks(result_terms, n_t)
    back_q, back_k, back_v = attend_backward(
        queries, keys, values, key_image, row_image, row_valid / count_total, span, messages
    )
    feed_pair = cross(feed_pair, orders, 0, n_dp)
    for i in steps[1:]:
        feed_pair = next_cut(feed_pair, orders, i, n_dp)
        if i == steps[1]:
            back_q, back_k, back_v = after([back_q, back_k, back_v], *[send for _, send in feed_pair])
        feed_pair = cross(feed_pair, orders, i, n_dp)

    v_keep, v_send = gradient(key_input_t, back_v, False, at, n_dp)
    k_keep, k_send = gradient(key_input_t, after(back_k, v_send), False, at, n_dp)
    q_keep, q_send = gradient(latent_t, after(back_q, k_send, *result_terms[1:]), False, at, n_dp)
    v_send, k_send = after([v_send, k_send], q_send)
    v_got, k_got, q_got = [partner(x, "dp", n_dp, 1) for x in (v_send, k_send, q_send)]
    latent_q = after(back_q, q_send)
    *latent_terms, latent_sums = latent_back(latent_q, back_k, back_v, wq, wk, wv, latent_blocks)
    v_got, k_got, q_got = after([v_got, k_got, q_got], latent_sums)
    k_got = after(k_got, *[got for _, got in feed_pair])
    pair = first_cut((v_keep, v_got), (k_keep, k_got), None, orders, n_dp)
    sends = [send for _, send in pair]
    latent_terms[1:] = after(latent_terms[1:], *sends)
    latent_terms = send_blocks(latent_terms, n_t)
    pair = cross(pair, orders, 0, n_dp)
    q_pair = first_cut(None, None, (q_keep, after(q_got, *sends)), orders, n_dp)
    out_blocks = tensor_blocks(feed_pair, [None], inner, at, n_t)
    features_grad, media_sums = media_back(
        after(back_k, latent_sums, *out_blocks, *[send for _, send in q_pair]),
        back_v, wk, wv, features, media_gain, own_patches,
    )
    for i in steps[1:]:
        gots = after([got for _, got in pair], features_grad)
        pair = [(keep, got) for (keep, _), got in zip(pair, gots)]
        pair = next_cut(pair, orders, i, n_dp)
        if i == steps[1]:
            q_sends = after([send for _, send in q_pair], *[send for _, send in pair], *latent_terms[1:])
            q_pair = [(keep, send) for (keep, _), send in zip(q_pair, q_sends)]
        pair = cross(pair, orders, i, n_dp)
    q_pair = cross(q_pair, orders, 0, n_dp)
    blocks = send_blocks(tensor_blocks(pair, [1, 0], inner, at, n_t), n_t)
    for i in steps[1:]:
        gots = after([got for _, got in q_pair], blocks[1], blocks[-1])
        q_pair = [(keep, got) for (keep, _), got in zip(q_pair, gots)]
        q_pair = cross(next_cut(q_pair, orders, i, n_dp), orders, i, n_dp)
    q_blocks = tensor_blocks(q_pair, [None], inner, at, n_t)
    grad_kv = add_up(after(blocks, *q_blocks))
    result, latents_grad, down_share, up_share = finish(
        after(result_terms, *q_blocks), latent_terms, feed_pair, middle, back_middle, latents, latent_gain, inner
    )

    qo_blocks = [jnp.concatenate(x, axis=0) for x in zip(q_blocks, out_blocks)]
    grad_qo = add_up(after(send_blocks(qo_blocks, n_t), result))
    grad_q, grad_o = grad_qo[0], grad_qo[1]

    sums = [media_sums[0], media_sums[1], latent_sums[0], latent_sums[1]] + gain_shift(back_feed, feed_hat)
    sums = jnp.stack(sums + [jnp.full((width,), penalty_part)] * 2)
    sums = after(sums, features_grad)
    sums = after(all_sum(sums, [("dp", n_dp)]), *q_blocks)
    sums = all_sum(sums, [("tensor", n_t)])
    penalty = sums[6, 0] / count_total
    share = width // (n_dp * n_t)
    mine = lax.dynamic_index_in_dim(
        sums.reshape(8, n_dp * n_t, share), p * n_t + z, 1, keepdims=False
    )
    return (
        result[None],
        penalty,
        latents_grad[None],
        features_grad[None],
        mine[0],
        mine[1],
        mine[2],
        mine[3],
        mine[4],
        mine[5],
        grad_q,
        jnp.moveaxis(grad_kv, 0, 1),
        grad_o.T,
        up_share,
        down_share.T,
    )


def solution(mesh):
    return jax.shard_map(
        local,
        mesh=mesh,
        in_specs=(
            P("dp", "tensor", None),
            P("dp", "tensor", None),
            P("dp", None),
            P("dp", None),
            P(),
            P(),
            P(),
            P(),
            P(),
            P(),
            P(None, "tensor"),
            P(None, None, "tensor"),
            P("tensor", None),
            P(None, "tensor"),
            P("tensor", None),
            P("dp", "tensor", None),
        ),
        out_specs=(
            P("dp", "tensor", None),
            P(),
            P("dp", "tensor", None),
            P("dp", "tensor", None),
            P(("dp", "tensor")),
            P(("dp", "tensor")),
            P(("dp", "tensor")),
            P(("dp", "tensor")),
            P(("dp", "tensor")),
            P(("dp", "tensor")),
            P("dp", "tensor"),
            P("dp", None, "tensor"),
            P("tensor", "dp"),
            P("dp", "tensor"),
            P("tensor", "dp"),
        ),
        check_vma=False,
    )
```

```python
from functools import partial

import jax
import jax.numpy as jnp
from jax import lax
from jax.experimental import pallas as pl
from jax.experimental.pallas import tpu as pltpu
from jax.sharding import PartitionSpec as P

HD = 96
LAT = 64
EPSILON = 1e-05
NEGATIVE = -1e30
SCALE = HD ** (-0.5)
BF = jnp.bfloat16
F32 = jnp.float32
VMEM_LIMIT = 48 * 1024 * 1024


def rotate(x, count, shift):
    return lax.ppermute(x, "tensor", [(i, (i + shift) % count) for i in range(count)])


def after(x, *done):
    many = isinstance(x, (list, tuple))
    held = lax.optimization_barrier((*x, *done) if many else (x, *done))
    return list(held[: len(x)]) if many else held[0]


def gather_blocks(x, count):
    return [x] + [rotate(x, count, k) for k in range(1, count)]


def send_blocks(blocks, count):
    return [blocks[0]] + [rotate(blocks[k], count, -k) for k in range(1, count)]


def scatter_blocks(blocks, count):
    return add_up(send_blocks(blocks, count))


def partner(x, axis, count, offset):
    return lax.ppermute(x, axis, [(i, i ^ offset) for i in range(count)])


def bits_of(count):
    return count.bit_length() - 1


def gradient_kernel(natural, turned, n_dp, at_ref, xt_ref, y_ref, keep_ref, send_ref, total_ref):
    dims = (((1,), (0,)), ((), ())) if natural else (((1,), (1,)), ((), ()))
    xt = xt_ref[...].T if turned else xt_ref[...]
    total_ref[...] = lax.dot_general(xt, y_ref[...], dims, preferred_element_type=F32)
    p, unit = at_ref[1], keep_ref.shape[1]
    for i in range(n_dp // 2):
        for odd, out in enumerate((keep_ref, send_ref)):
            first = pl.multiple_of((p ^ (2 * i + odd)) * unit, unit)
            out[i] = total_ref[pl.ds(first, unit), :].astype(BF)


def gradient(xt, y, natural, at, n_dp, turned=False):
    width, rows = xt.shape[::-1] if turned else xt.shape
    unit = width // n_dp
    wide = y.shape[1] if natural else y.shape[0]
    step = wide // 3
    half = n_dp // 2
    if natural:
        y_spec = pl.BlockSpec((rows, step), lambda i: (0, i))
    else:
        y_spec = pl.BlockSpec((step, rows), lambda i: (i, 0))
    return pl.pallas_call(
        partial(gradient_kernel, natural, turned, n_dp),
        grid=(3,),
        in_specs=[
            pl.BlockSpec(memory_space=pltpu.SMEM),
            pl.BlockSpec(xt.shape, lambda i: (0, 0)),
            y_spec,
        ],
        out_specs=[pl.BlockSpec((half, unit, step), lambda i: (0, 0, i))] * 2,
        out_shape=[pltpu.HBM((half, unit, wide), BF)] * 2,
        scratch_shapes=[pltpu.VMEM((width, step), F32)],
        compiler_params=pltpu.CompilerParams(vmem_limit_bytes=24 * 1024 * 1024),
    )(at, xt, y)


def bit_orders(count):
    outer = list(range(1, bits_of(count)))
    half = (len(outer) + 1) // 2
    return outer, outer[half:] + outer[:half]


def cut_kernel(widths, *refs):
    ins, (keep_ref, send_ref) = refs[:-2], refs[-2:]
    start = 0
    for i, wide in enumerate(widths):
        lanes = slice(start, start + wide)
        keep_a, got_a, keep_b, got_b = ins[4 * i : 4 * i + 4]
        keep_ref[:, :, lanes] = (keep_a[...].astype(F32) + got_a[...].astype(F32)).astype(BF)
        send_ref[:, :, lanes] = (keep_b[...].astype(F32) + got_b[...].astype(F32)).astype(BF)
        start += wide


def reduce_cut(parts, order, step, n_dp):
    left = [b for b in range(bits_of(n_dp) - 1, 0, -1) if b not in order[:step]]
    low = 1 << (len(left) - left.index(order[step]) - 1)
    count, rows, _ = parts[0][0].shape
    widths, specs, flat = [], [], []
    for keep, got, half in parts:
        wide = keep.shape[2] if half is None else keep.shape[2] // 2

        def at(bit, wide=wide, lane=half or 0):
            return pl.BlockSpec(
                (1, rows, wide), lambda i: (i // low * (2 * low) + bit * low + i % low, 0, lane)
            )

        widths.append(wide)
        specs += [at(0), at(0), at(1), at(1)]
        flat += [keep, got, keep, got]
    total = sum(widths)
    return pl.pallas_call(
        partial(cut_kernel, widths),
        grid=(count // 2,),
        in_specs=specs,
        out_specs=[pl.BlockSpec((1, rows, total), lambda i: (i, 0, 0))] * 2,
        out_shape=[pltpu.HBM((count // 2, rows, total), BF)] * 2,
        compiler_params=pltpu.CompilerParams(vmem_limit_bytes=20 * 1024 * 1024),
    )(*flat)


def first_cut(one, two, split, orders, n_dp):
    out = []
    for h, full in enumerate((one, two)):
        parts = [(*full, None)] if full else []
        parts += [(*split, h)] if split else []
        out.append(reduce_cut(parts, orders[h], 0, n_dp))
    return out


def next_cut(pair, orders, step, n_dp):
    return [reduce_cut([(*x, None)], order, step, n_dp) for x, order in zip(pair, orders)]


def cross(pair, orders, step, n_dp):
    return [
        (keep, partner(send, "dp", n_dp, 1 << order[step])) for (keep, send), order in zip(pair, orders)
    ]


def add_up(terms):
    total = terms[0].astype(F32)
    for term in terms[1:]:
        total = total + term.astype(F32)
    return total


def blocks_kernel(n_t, weights, at_ref, *refs):
    (a_keep, a_got, b_keep, b_got), outs = refs[:4], refs[4:]
    pairs = (a_keep, a_got), (b_keep, b_got)
    z = at_ref[0]
    columns = outs[0].shape[-1]
    half = n_t // 2

    def piece(which, lane):
        lanes = pl.ds(pl.multiple_of(lane, columns), columns)
        keep, got = pairs[which]
        return keep[0, :, lanes].astype(F32) + got[0, :, lanes].astype(F32)

    for k in range(n_t):
        block = lax.rem(z - k + n_t, n_t)
        for m, which in enumerate(weights):
            if which is None:
                lane = (a_keep.shape[2] - columns * half) + lax.rem(block, half) * columns
                value = jnp.where(block >= half, piece(1, lane), piece(0, lane))
            else:
                value = piece(which, block * columns)
            outs[k][m] = value.astype(outs[k].dtype)


def tensor_blocks(pair, weights, columns, at, n_t):
    flat = [x for terms in pair for x in terms]
    rows = flat[0].shape[1]
    return pl.pallas_call(
        partial(blocks_kernel, n_t, weights),
        in_specs=[pl.BlockSpec(memory_space=pltpu.SMEM)]
        + [pl.BlockSpec(memory_space=pltpu.VMEM)] * len(flat),
        out_shape=[
            jax.ShapeDtypeStruct((len(weights), rows, columns // n_t), F32 if k == 0 else BF)
            for k in range(n_t)
        ],
        compiler_params=pltpu.CompilerParams(vmem_limit_bytes=14 * 1024 * 1024),
    )(at, *flat)


def all_sum(x, axes):
    for axis, count in axes:
        for bit in range(bits_of(count)):
            x = x + partner(x, axis, count, 1 << bit)
    return x


def place_kernel(n_t, unit, z_rows, z_cols, offsets, parts, at_ref, own_ref, *refs):
    out_ref = refs[-1]
    z, p = at_ref[0], at_ref[1]
    rows, cols = own_ref.shape
    if z_rows:
        out_ref[pl.ds(pl.multiple_of(z * z_rows, z_rows), rows), :] = own_ref[...]
    else:
        out_ref[:, pl.ds(pl.multiple_of(z * z_cols, z_cols), cols)] = own_ref[...]
    for k in range(1, n_t):
        shard = lax.rem(z - k + n_t, n_t)
        for which, first, height, row_at, col_at in parts:
            for odd in range(2):
                src = refs[2 * which + odd]
                wide = src.shape[3]
                for i, off in enumerate(offsets[which]):
                    base = shard * z_rows + (p ^ (off ^ odd)) * unit + row_at
                    where = pl.ds(pl.multiple_of(base, 16), height)
                    if z_cols:
                        at = pl.ds(pl.multiple_of(shard * z_cols, z_cols), wide)
                    else:
                        at = slice(col_at, col_at + wide)
                    out_ref[where, at] = src[i, k - 1, first : first + height, :]


def reorder(x, places):
    return jnp.stack([lax.dynamic_index_in_dim(x, i, 0, keepdims=False) for i in places])


def project_kernel(place_kernel, count, at_ref, x_ref, *refs):
    place_kernel(at_ref, *refs[:-2])
    weight_ref, out_ref, turned_ref = refs[-3:]
    turned_ref[...] = x_ref[...].T
    step = weight_ref.shape[1] // count
    for c in range(count):
        cols = slice(c * step, (c + 1) * step)
        block = jnp.dot(x_ref[...], weight_ref[:, cols], preferred_element_type=F32)
        out_ref[cols, :] = block.T.astype(BF)


def place(own, pieces, offsets, parts, unit, by_rows, at, n_dp, n_t, x=None):
    rows, cols = own.shape
    shape = (n_t * rows, cols) if by_rows else (rows, n_t * cols)
    if unit % 16 or any(part[2] % 16 for part in parts):
        z, p = at[0], at[1]
        across = []
        for which, first, height, _, _ in parts:
            ordered = [None] * n_dp
            for i, off in enumerate(offsets[which]):
                for odd in range(2):
                    ordered[off ^ odd] = pieces[which][odd][i, :, first : first + height]
            across.append(reorder(jnp.stack(ordered), [p ^ d for d in range(n_dp)]))
        whole = jnp.concatenate(across, axis=3 if by_rows else 2).transpose(1, 0, 2, 3)
        whole = whole.reshape((n_t - 1, rows, cols))
        whole = jnp.concatenate([own[None], whole], axis=0)
        whole = reorder(whole, [(z - k + n_t) % n_t for k in range(n_t)])
        whole = whole.reshape(shape) if by_rows else whole.transpose(1, 0, 2).reshape(shape)
        return whole if x is None else (whole, dot("dh,rd->hr", whole, x).astype(BF), x.T)
    flat = [x for pair in pieces for x in pair]
    kernel = partial(
        place_kernel, n_t, unit, rows if by_rows else 0, 0 if by_rows else cols, offsets, parts
    )
    out = jax.ShapeDtypeStruct(shape, own.dtype)
    if x is None:
        first, outs = [], out
    else:
        kernel, first = partial(project_kernel, kernel, n_t), [x]
        outs = [out] + [jax.ShapeDtypeStruct((n, x.shape[0]), BF) for n in (shape[1], x.shape[1])]
    ins = [*first, own, *flat]
    return pl.pallas_call(
        kernel,
        out_shape=outs,
        in_specs=[pl.BlockSpec(memory_space=pltpu.SMEM)]
        + [pl.BlockSpec(memory_space=pltpu.VMEM)] * len(ins),
        compiler_params=pltpu.CompilerParams(vmem_limit_bytes=28 * 1024 * 1024),
    )(at, *ins)


def rotations(x, count):
    return [rotate(x, count, k) for k in range(1, count)]


def widen(one, two, step, orders, n_dp, *done):
    arrived = [partner(x, "dp", n_dp, 1 << order[step]) for x, order in zip((one, two), orders)]
    if done:
        arrived = after(arrived, *done)
    return [jnp.concatenate(x, axis=0) for x in zip((one, two), arrived)]


def widen_offsets(order):
    offsets = [0]
    for bit in order:
        offsets = offsets + [o ^ (1 << bit) for o in offsets]
    return offsets


def cores(one, two, n_dp):
    return [(x, partner(x, "dp", n_dp, 1)) for x in (one, two)]


def share_of(x, axis, count):
    size = x.shape[axis] // count
    return lax.dynamic_slice_in_dim(x, lax.axis_index("dp") * size, size, axis)


def three(x):
    high = x.astype(BF)
    left = x - high.astype(F32)
    middle = left.astype(BF)
    low = (left - middle.astype(F32)).astype(BF)
    return jnp.concatenate([high, middle, low], axis=0)


def join(x, count):
    x = x.astype(F32)
    return x[:count] + x[count : 2 * count] + x[2 * count :]


GROUP = 8
CHUNK = 128
TN = (((0,), (0,)), ((), ()))
NT = (((1,), (1,)), ((), ()))


def forward_kernel(heads, n_t, span_ref, q_ref, k_ref, v_ref, seg_ref, img_ref, *rest):
    msgs, stat, acc, run = rest[:n_t], rest[n_t], rest[n_t + 1], rest[n_t + 2]
    g = pl.program_id(0)
    rows = q_ref.shape[1] // n_t
    keys = k_ref.shape[1]
    for k in range(n_t):
        cols = slice(k * rows, (k + 1) * rows)
        image = img_ref[:, cols]
        acc[...] = jnp.zeros_like(acc)
        run[...] = jnp.zeros_like(run)
        run[0] = jnp.full(run.shape[1:], NEGATIVE)

        def step(at, cols=cols, image=image):
            allowed = seg_ref[at, :] == image
            bands = [slice(h * HD, (h + 1) * HD) for h in range(GROUP)]
            scores = [
                SCALE
                * lax.dot_general(k_ref[b, at], q_ref[b, cols], TN, preferred_element_type=F32)
                for b in bands
            ]
            scores = [jnp.where(allowed, x, NEGATIVE) for x in scores]
            old = [run[0, h : h + 1] for h in range(GROUP)]
            tops = [
                jnp.maximum(m, jnp.max(x, axis=0, keepdims=True)) for m, x in zip(old, scores)
            ]
            weights = [jnp.where(allowed, jnp.exp(x - m), 0.0) for x, m in zip(scores, tops)]
            outs = [
                jnp.dot(v_ref[b, at], w.astype(BF), preferred_element_type=F32)
                for b, w in zip(bands, weights)
            ]
            fades = [jnp.exp(m - n) for m, n in zip(old, tops)]
            for h in range(GROUP):
                run[0, h : h + 1] = tops[h]
                run[1, h : h + 1] = run[1, h : h + 1] * fades[h] + jnp.sum(
                    weights[h], axis=0, keepdims=True
                )
                run[2, h : h + 1] = run[2, h : h + 1] * fades[h] + jnp.sum(
                    weights[h] * scores[h], axis=0, keepdims=True
                )
            for b, f, o in zip(bands, fades, outs):
                acc[b, :] = acc[b, :] * f + o

        if k == 0:
            step(slice(keys - rows, keys))

        @pl.loop(span_ref[0, k], span_ref[1, k])
        def _(c, step=step):
            step(pl.ds(pl.multiple_of(c * CHUNK, CHUNK), CHUNK))

        total = run[1, :GROUP]
        some = total > 0.0
        safe = jnp.where(some, total, 1.0)
        inverse = jnp.where(some, 1.0 / safe, 0.0)
        stat[0, pl.ds(g, 1), :, cols] = jnp.where(some, run[0, :GROUP] + jnp.log(safe), NEGATIVE)[None]
        stat[1, pl.ds(g, 1), :, cols] = (run[2, :GROUP] * inverse)[None]
        for h in range(GROUP):
            band = slice(h * HD, (h + 1) * HD)
            first = pl.multiple_of((g * GROUP + h) * HD, HD)
            msgs[k][pl.ds(first, HD), :] = (acc[band, :] * inverse[h : h + 1]).astype(BF)

    @pl.when(g == heads // GROUP - 1)
    def _():
        for k in range(n_t):
            cols = slice(k * rows, (k + 1) * rows)
            for i in range(2):
                first = heads * (HD + 3 * i)
                msgs[k][first : first + 3 * heads, :] = three(
                    stat[i, :, :, cols].reshape(heads, rows)
                )


def attend_forward(q, k, v, seg, img, span, n_t):
    heads = q.shape[0] // HD
    rows, keys = q.shape[1], k.shape[1]
    one = rows // n_t
    tall = heads * (HD + 6)
    band = GROUP * HD
    return pl.pallas_call(
        partial(forward_kernel, heads, n_t),
        grid_spec=pltpu.PrefetchScalarGridSpec(
            num_scalar_prefetch=1,
            grid=(heads // GROUP,),
            in_specs=[
                pl.BlockSpec((band, rows), lambda g, s: (g, 0)),
                pl.BlockSpec((band, keys), lambda g, s: (g, 0)),
                pl.BlockSpec((band, keys), lambda g, s: (g, 0)),
                pl.BlockSpec((keys, 1), lambda g, s: (0, 0)),
                pl.BlockSpec((1, rows), lambda g, s: (0, 0)),
            ],
            out_specs=[pl.BlockSpec((tall, one), lambda g, s: (0, 0))] * n_t,
            scratch_shapes=[
                pltpu.VMEM((2, heads // GROUP, GROUP, rows), F32),
                pltpu.VMEM((band, one), F32),
                pltpu.VMEM((3, 8, one), F32),
            ],
        ),
        out_shape=[jax.ShapeDtypeStruct((tall, one), BF)] * n_t,
        compiler_params=pltpu.CompilerParams(vmem_limit_bytes=20 * 1024 * 1024),
    )(span, q, k, v, seg, img)


def combine_kernel(heads, n_t, *refs):
    msgs, (out_ref, stat_ref) = refs[:n_t], refs[n_t:]
    base = heads * HD
    logs = [join(m[base : base + 3 * heads, :], heads) for m in msgs]
    means = [join(m[base + 3 * heads :, :], heads) for m in msgs]
    top = logs[0]
    for x in logs[1:]:
        top = jnp.maximum(top, x)
    shares = [jnp.exp(x - top) for x in logs]
    total = shares[0]
    for x in shares[1:]:
        total = total + x
    shares = [x / total for x in shares]
    mean = shares[0] * means[0]
    for s, x in zip(shares[1:], means[1:]):
        mean = mean + s * x
    stat_ref[:heads, :] = top + jnp.log(total)
    stat_ref[heads:, :] = mean
    for h in range(heads):
        at = slice(h * HD, (h + 1) * HD)
        acc = msgs[0][at, :].astype(F32) * shares[0][h : h + 1, :]
        for s, m in zip(shares[1:], msgs[1:]):
            acc = acc + m[at, :].astype(F32) * s[h : h + 1, :]
        out_ref[at, :] = acc.astype(BF)


def combine(msgs, heads):
    one = msgs[0].shape[1]
    return pl.pallas_call(
        partial(combine_kernel, heads, len(msgs)),
        out_shape=[
            jax.ShapeDtypeStruct((heads * HD, one), BF),
            jax.ShapeDtypeStruct((2 * heads, one), F32),
        ],
        compiler_params=pltpu.CompilerParams(vmem_limit_bytes=8 * 1024 * 1024),
    )(*msgs)


def message_kernel(heads, do_ref, out_ref, stat_ref, coef_ref, msg_ref):
    base = heads * HD
    deltas = []
    for h in range(heads):
        at = slice(h * HD, (h + 1) * HD)
        grad = do_ref[at, :].astype(F32)
        deltas.append(jnp.sum(grad * out_ref[at, :].astype(F32), axis=0, keepdims=True))
    msg_ref[:base, :] = do_ref[...]
    delta = jnp.concatenate(deltas, axis=0) - coef_ref[...] * stat_ref[heads:, :]
    msg_ref[base : base + 3 * heads, :] = three(stat_ref[:heads, :])
    msg_ref[base + 3 * heads :, :] = three(delta)


def make_message(do, out, stat, coef, heads):
    return pl.pallas_call(
        partial(message_kernel, heads),
        out_shape=jax.ShapeDtypeStruct((heads * (HD + 6), do.shape[1]), BF),
        compiler_params=pltpu.CompilerParams(vmem_limit_bytes=6 * 1024 * 1024),
    )(do, out, stat, coef)


def backward_kernel(heads, n_t, span_ref, q_ref, k_ref, v_ref, seg_ref, img_ref, coef_ref, *rest):
    grads, stats = rest[:n_t], rest[n_t : 2 * n_t]
    dq_ref, dk_ref, dv_ref, stat, dq, dk, dv = rest[2 * n_t :]
    g = pl.program_id(0)
    rows = q_ref.shape[1] // n_t
    keys = k_ref.shape[1]

    @pl.when(g == 0)
    def _():
        for i in range(n_t):
            cols = slice(i * rows, (i + 1) * rows)
            for j in range(2):
                part = join(stats[i][3 * j * heads : 3 * (j + 1) * heads, :], heads)
                stat[j, :, :, cols] = part.reshape(heads // GROUP, GROUP, rows)

    dk[...] = jnp.zeros_like(dk)
    dv[...] = jnp.zeros_like(dv)
    for i in range(n_t):
        cols = slice(i * rows, (i + 1) * rows)
        image, coef = img_ref[:, cols], coef_ref[:, cols]
        logs = stat[0, pl.ds(g, 1), :, cols][0]
        deltas = stat[1, pl.ds(g, 1), :, cols][0]
        dq[...] = jnp.zeros_like(dq)

        def step(at, cols=cols, image=image, coef=coef, logs=logs, deltas=deltas, grad_ref=grads[i]):
            allowed = seg_ref[at, :] == image
            bands = [slice(h * HD, (h + 1) * HD) for h in range(GROUP)]
            scores = [
                SCALE
                * lax.dot_general(k_ref[b, at], q_ref[b, cols], TN, preferred_element_type=F32)
                for b in bands
            ]
            back_probs = [
                lax.dot_general(v_ref[b, at], grad_ref[b, :], TN, preferred_element_type=F32)
                for b in bands
            ]
            probs = [
                jnp.where(allowed, jnp.exp(jnp.where(allowed, x - logs[h : h + 1], 0.0)), 0.0)
                for h, x in enumerate(scores)
            ]
            backs = [
                (p * (y - coef * x - deltas[h : h + 1])).astype(BF)
                for h, (x, y, p) in enumerate(zip(scores, back_probs, probs))
            ]
            probs = [p.astype(BF) for p in probs]
            for b, p in zip(bands, probs):
                dv[b, at] += lax.dot_general(grad_ref[b, :], p, NT, preferred_element_type=F32)
            for b, x in zip(bands, backs):
                dq[b, :] += jnp.dot(k_ref[b, at], x, preferred_element_type=F32)
            for b, x in zip(bands, backs):
                dk[b, at] += lax.dot_general(q_ref[b, cols], x, NT, preferred_element_type=F32)

        if i == 0:
            step(slice(keys - rows, keys))

        @pl.loop(span_ref[0, i], span_ref[1, i])
        def _(c, step=step):
            step(pl.ds(pl.multiple_of(c * CHUNK, CHUNK), CHUNK))

        dq_ref[:, cols] = (dq[...] * SCALE).astype(BF)
    dk_ref[...] = (dk[...] * SCALE).astype(BF)
    dv_ref[...] = dv[...].astype(BF)


def attend_backward(q, k, v, seg, img, coef, span, msgs):
    n_t = len(msgs)
    heads = q.shape[0] // HD
    rows, keys = q.shape[1], k.shape[1]
    one = rows // n_t
    band = GROUP * HD
    wide = [pl.BlockSpec((band, n), lambda g, s: (g, 0)) for n in (rows, keys, keys)]
    return pl.pallas_call(
        partial(backward_kernel, heads, n_t),
        grid_spec=pltpu.PrefetchScalarGridSpec(
            num_scalar_prefetch=1,
            grid=(heads // GROUP,),
            in_specs=wide
            + [
                pl.BlockSpec((keys, 1), lambda g, s: (0, 0)),
                pl.BlockSpec((1, rows), lambda g, s: (0, 0)),
                pl.BlockSpec((1, rows), lambda g, s: (0, 0)),
            ]
            + [pl.BlockSpec((band, one), lambda g, s: (g, 0))] * n_t
            + [pl.BlockSpec((6 * heads, one), lambda g, s: (HD // 6, 0))] * n_t,
            out_specs=wide,
            scratch_shapes=[
                pltpu.VMEM((2, heads // GROUP, GROUP, rows), F32),
                pltpu.VMEM((band, one), F32),
                pltpu.VMEM((band, keys), F32),
                pltpu.VMEM((band, keys), F32),
            ],
        ),
        out_shape=[
            jax.ShapeDtypeStruct(q.shape, BF),
            jax.ShapeDtypeStruct(k.shape, BF),
            jax.ShapeDtypeStruct(v.shape, BF),
        ],
        compiler_params=pltpu.CompilerParams(vmem_limit_bytes=36 * 1024 * 1024),
        cost_estimate=pl.CostEstimate(
            flops=60 * heads * HD * rows * keys,
            bytes_accessed=60 * 1024 * 1024,
            transcendentals=heads * rows * keys,
        ),
    )(span, q, k, v, seg, img, coef, *msgs, *msgs)


def norm_parts(values):
    values = values.astype(F32)
    center = values - jnp.mean(values, axis=-1, keepdims=True)
    inv_root = lax.rsqrt(jnp.mean(center * center, axis=-1, keepdims=True) + EPSILON)
    return center * inv_root, inv_root


def norm_backward(grad_rows, normal, inv_root, gain_row):
    scaled = grad_rows * gain_row
    reduced = (
        scaled
        - jnp.mean(scaled, axis=-1, keepdims=True)
        - normal * jnp.mean(scaled * normal, axis=-1, keepdims=True)
    )
    return reduced * inv_root


def gain_shift(grad_rows, normal):
    return [jnp.sum(grad_rows * normal, axis=0), jnp.sum(grad_rows, axis=0)]


def rows_back(grads, weights):
    total = None
    for grad, weight in zip(grads, weights):
        term = lax.dot_general(grad, weight, (((0,), (1,)), ((), ())), preferred_element_type=F32)
        total = term if total is None else total + term
    return total


def media_back_kernel(dk_ref, dv_ref, wk_ref, wv_ref, x_ref, gain_ref, out_ref, sums_ref):
    back = rows_back((dk_ref[...], dv_ref[...]), (wk_ref[...], wv_ref[...]))
    normal, root = norm_parts(x_ref[...])
    out_ref[...] = norm_backward(back, normal, root, gain_ref[...])

    @pl.when(pl.program_id(0) == 0)
    def _():
        sums_ref[...] = jnp.zeros_like(sums_ref)

    sums_ref[0:1] += jnp.sum(back * normal, axis=0, keepdims=True)
    sums_ref[1:2] += jnp.sum(back, axis=0, keepdims=True)


def media_back(back_k, back_v, wk, wv, features, gain, block):
    rows, width = features.shape
    inner = back_k.shape[0]
    whole = pl.BlockSpec((width, inner), lambda i: (0, 0))
    return pl.pallas_call(
        media_back_kernel,
        grid=(rows // block,),
        in_specs=[pl.BlockSpec((inner, block), lambda i: (0, i))] * 2
        + [whole] * 2
        + [pl.BlockSpec((block, width), lambda i: (i, 0)), pl.BlockSpec((1, width), lambda i: (0, 0))],
        out_specs=[
            pl.BlockSpec((block, width), lambda i: (i, 0)),
            pl.BlockSpec((8, width), lambda i: (0, 0)),
        ],
        out_shape=[
            jax.ShapeDtypeStruct((rows, width), F32),
            jax.ShapeDtypeStruct((8, width), F32),
        ],
        compiler_params=pltpu.CompilerParams(vmem_limit_bytes=VMEM_LIMIT),
    )(back_k, back_v, wk, wv, features, gain[None])


def latent_back_kernel(n_t, dq_ref, dk_ref, dv_ref, wq_ref, wk_ref, wv_ref, *refs):
    xs, outs, sums_ref = refs[:n_t], refs[n_t:-1], refs[-1]
    rows = xs[0].shape[0]
    gain_sum = shift_sum = None
    total = rows_back((dq_ref[...],), (wq_ref[...],))
    own = rows_back((dk_ref[...], dv_ref[...]), (wk_ref[...], wv_ref[...]))
    for k in range(n_t):
        back = total[k * rows : (k + 1) * rows]
        if k == 0:
            back = back + own
        outs[k][...] = back.astype(outs[k].dtype)
        normal, _ = norm_parts(xs[k][...])
        gain_part = jnp.sum(back * normal, axis=0, keepdims=True)
        shift_part = jnp.sum(back, axis=0, keepdims=True)
        gain_sum = gain_part if gain_sum is None else gain_sum + gain_part
        shift_sum = shift_part if shift_sum is None else shift_sum + shift_part
    sums_ref[...] = jnp.zeros_like(sums_ref)
    sums_ref[0:1] = gain_sum
    sums_ref[1:2] = shift_sum


def latent_back(back_q, back_k, back_v, wq, wk, wv, blocks):
    n_t = len(blocks)
    rows, width = blocks[0].shape
    inner, keys = back_k.shape
    tail = pl.BlockSpec((inner, rows), lambda i: (0, keys // rows - 1))
    whole = pl.BlockSpec((width, inner), lambda i: (0, 0))
    return pl.pallas_call(
        partial(latent_back_kernel, n_t),
        grid=(1,),
        in_specs=[pl.BlockSpec(back_q.shape, lambda i: (0, 0)), tail, tail, whole, whole, whole]
        + [pl.BlockSpec((rows, width), lambda i: (0, 0))] * n_t,
        out_specs=[pl.BlockSpec((rows, width), lambda i: (0, 0))] * n_t
        + [pl.BlockSpec((8, width), lambda i: (0, 0))],
        out_shape=[jax.ShapeDtypeStruct((rows, width), BF if k else F32) for k in range(n_t)]
        + [jax.ShapeDtypeStruct((8, width), F32)],
        compiler_params=pltpu.CompilerParams(vmem_limit_bytes=50 * 1024 * 1024),
    )(back_q, back_k, back_v, wq, wk, wv, *blocks)


def blocks_of_product_kernel(n_t, a_ref, b_ref, *outs):
    total = jnp.dot(a_ref[...], b_ref[...], preferred_element_type=F32)
    rows = outs[0].shape[0]
    for k in range(n_t):
        outs[k][...] = total[k * rows : (k + 1) * rows].astype(outs[k].dtype)


def blocks_of_product(a, b, n_t):
    shape = a.shape[0] // n_t, b.shape[1]
    return list(
        pl.pallas_call(
            partial(blocks_of_product_kernel, n_t),
            out_shape=[jax.ShapeDtypeStruct(shape, BF if k else F32) for k in range(n_t)],
            compiler_params=pltpu.CompilerParams(vmem_limit_bytes=VMEM_LIMIT),
        )(a, b)
    )


def finish_kernel(n_t, columns, *refs):
    results, latent_terms, feeds = refs[:n_t], refs[n_t : 2 * n_t], refs[2 * n_t : 2 * n_t + 4]
    middle_ref, back_ref, x_ref, gain_ref, *outs = refs[2 * n_t + 4 :]
    outs[0][...] = (middle_ref[...] + add_up([r[...] for r in results])).astype(BF)
    normal, root = norm_parts(x_ref[...])
    back = add_up([r[...] for r in latent_terms])
    outs[1][...] = back_ref[...] + norm_backward(back, normal, root, gain_ref[...])
    for m in range(2):
        keep, got = feeds[2 * m], feeds[2 * m + 1]
        outs[2 + m][...] = keep[0, :, :columns].astype(F32) + got[0, :, :columns].astype(F32)


def finish(result_terms, latent_terms, feed_pair, middle, back_middle, latents, gain, columns):
    feeds = [x for pair in feed_pair for x in pair]
    unit, width = feeds[0].shape[1], middle.shape[1]
    return pl.pallas_call(
        partial(finish_kernel, len(result_terms), columns),
        out_shape=[
            jax.ShapeDtypeStruct(middle.shape, BF),
            jax.ShapeDtypeStruct(middle.shape, F32),
            jax.ShapeDtypeStruct((unit, columns), F32),
            jax.ShapeDtypeStruct((unit, columns), F32),
        ],
        compiler_params=pltpu.CompilerParams(vmem_limit_bytes=20 * 1024 * 1024),
    )(*result_terms, *latent_terms, *feeds, middle, back_middle, latents, gain[None])


def dot(equation, a, b):
    return jnp.einsum(equation, a, b, preferred_element_type=F32)


def local(
    latents,
    features,
    lengths,
    valid_media,
    media_gain,
    media_shift,
    latent_gain,
    latent_shift,
    feed_gain,
    feed_shift,
    query_weight,
    key_value_weight,
    output_weight,
    up_weight,
    down_weight,
    cotangent,
):
    n_t = lax.axis_size("tensor")
    n_dp = lax.axis_size("dp")
    z, p = lax.axis_index("tensor"), lax.axis_index("dp")
    at = jnp.stack([z, p]).astype(jnp.int32)
    latents, features, cotangent = latents[0], features[0], cotangent[0]
    lengths, valid = lengths[0], valid_media[0]
    width = latents.shape[1]
    own_rows, own_patches = latents.shape[0], features.shape[0]
    inner = query_weight.shape[1] * n_t
    heads = inner // HD
    images = lengths.shape[0]


    ends = jnp.sum(
        jnp.where(jnp.arange(images)[:, None] <= jnp.arange(images)[None, :], lengths[:, None], 0),
        axis=0,
    )
    positions = z * own_patches + jnp.arange(own_patches, dtype=jnp.int32)
    segment = jnp.sum((positions[:, None] >= ends[None, :]).astype(jnp.int32), axis=1)
    hit = segment[:, None] == jnp.arange(images, dtype=jnp.int32)[None, :]
    patch_valid = jnp.sum(jnp.where(hit, valid[None, :], 0), axis=1)
    patch_segment = jnp.where(patch_valid > 0, segment, -1)
    own_images = (z * own_rows + jnp.arange(own_rows, dtype=jnp.int32)) // LAT
    key_image = jnp.concatenate([patch_segment, own_images])[:, None]
    block_of = (z - jnp.arange(n_t, dtype=jnp.int32) + n_t) % n_t
    row_index = block_of[:, None] * own_rows + jnp.arange(own_rows, dtype=jnp.int32)[None, :]
    row_image = (row_index // LAT).reshape(1, -1)
    rows_each = own_rows // LAT
    local_ends = jnp.clip(ends - z * own_patches, 0, own_patches)
    local_starts = jnp.clip(ends - lengths - z * own_patches, 0, own_patches)
    block_image = block_of * rows_each
    at_image = jnp.arange(images, dtype=jnp.int32)[None, :]
    low = jnp.sum(jnp.where(at_image == block_image[:, None], local_starts[None, :], 0), axis=1)
    high = jnp.sum(
        jnp.where(at_image == block_image[:, None] + rows_each - 1, local_ends[None, :], 0), axis=1
    )
    span = jnp.stack([low // CHUNK, (high + CHUNK - 1) // CHUNK]).astype(jnp.int32)
    row_valid = jnp.sum(
        jnp.where(row_image.T == jnp.arange(images, dtype=jnp.int32)[None, :], valid[None, :], 0),
        axis=1,
    ).astype(F32)[None, :]

    orders = bit_orders(n_dp)
    steps = range(len(orders[0]))
    offsets = [widen_offsets(order) for order in orders]
    unit, part = width // n_dp, query_weight.shape[1]
    keyval = jnp.moveaxis(share_of(key_value_weight, 0, n_dp), 1, 0)
    kv_z = rotations(keyval, n_t)
    media_hat, media_root = norm_parts(features)
    media_normed = (media_hat * media_gain + media_shift).astype(BF)
    own_hat, own_root = norm_parts(latents)
    own_normed = (own_hat * latent_gain + latent_shift).astype(BF)
    key_input = jnp.concatenate([media_normed, own_normed], axis=0)
    kv_own = [key_value_weight[:, 0], key_value_weight[:, 1]]
    *kv_z, key_input, k_own, v_own = after([*kv_z, key_input, *kv_own])
    q_share = share_of(query_weight, 0, n_dp).reshape(2, unit // 2, part)
    o_share = share_of(output_weight, 0, n_dp)
    o_unit = o_share.shape[0]
    o_share = o_share.reshape(o_unit, 2, -1, part).transpose(1, 2, 0, 3).reshape(2, -1, part)
    qo_share = jnp.concatenate([q_share, o_share], axis=1)
    qo_z = rotations(after(qo_share, *kv_z), n_t)
    k_held, v_held = [jnp.stack([x[m] for x in kv_z])[None] for m in range(2)]
    for step in steps[:-1]:
        k_held, v_held = widen(k_held, v_held, step, orders, n_dp)
    k_held, v_held = after([k_held, v_held], *qo_z)
    gathered = lax.all_gather(jnp.stack(after([latents, cotangent], *qo_z)), "tensor", axis=0)
    others = [
        lax.dynamic_index_in_dim(gathered, (z - k + n_t) % n_t, 0, keepdims=False)
        for k in range(1, n_t)
    ]
    latent_blocks = [latents] + [x[0] for x in others]
    cot_blocks = [cotangent] + [x[1] for x in others]
    k_held, v_held = widen(k_held, v_held, steps[-1], orders, n_dp)
    k_pieces, v_pieces = cores(k_held, v_held, n_dp)
    qo_held = [jnp.stack([x[m] for x in qo_z])[None] for m in range(2)]
    qo_held = after(qo_held, k_held, v_held)
    whole = [(0, 0, unit, 0, 0)]
    wk, keys, key_input_t = place(k_own, [k_pieces], offsets[:1], whole, unit, False, at, n_dp, n_t, key_input)
    wv, values, _ = place(v_own, [v_pieces], offsets[1:], whole, unit, False, at, n_dp, n_t, key_input)
    for step in steps[:-1]:
        qo_held = widen(*qo_held, step, orders, n_dp, keys)
    qo_held = widen(*qo_held, steps[-1], orders, n_dp, values)
    qo_pieces = cores(*qo_held, n_dp)
    latent_all = jnp.concatenate(latent_blocks, axis=0)
    latent_hat, latent_root = norm_parts(latent_all)
    latent_normed = (latent_hat * latent_gain + latent_shift).astype(BF)
    cuts = [(h, 0, unit // 2, h * unit // 2, 0) for h in range(2)]
    wq, queries, latent_t = place(
        query_weight, qo_pieces, offsets, cuts, unit, False, at, n_dp, n_t, latent_normed
    )
    cuts = [
        (h, unit // 2 + c * o_unit, o_unit, 0, h * width // 2 + c * part)
        for h in range(2)
        for c in range(width // 2 // part)
    ]
    wo = place(output_weight, qo_pieces, offsets, cuts, o_unit, True, at, n_dp, n_t)
    sent = attend_forward(queries, keys, values, key_image, row_image, span, n_t)
    got = [sent[0]] + [rotate(sent[k], n_t, -k) for k in range(1, n_t)]
    count_part = after(jnp.full((8, 128), jnp.sum(valid).astype(F32)), *sent[1:])
    count_total = all_sum(count_part, [("dp", n_dp)])[0, 0]
    got = after(got, count_total, wo)
    attended, stat = combine(got, heads)
    entropy = stat[:heads] - stat[heads:]
    own_valid = row_valid[:, :own_rows]
    penalty_part = jnp.sum(entropy * own_valid)

    latent_own = latents.astype(F32)
    middle = latent_own + dot("hr,hd->rd", attended, wo)
    feed_hat, feed_root = norm_parts(middle)
    feed_normed = (feed_hat * feed_gain + feed_shift).astype(BF)
    feed_all = jnp.concatenate(gather_blocks(feed_normed, n_t), axis=0)
    cot_all = jnp.concatenate(after(cot_blocks, feed_normed), axis=0)
    hidden = dot("rd,df->rf", feed_all, up_weight)
    cdf = 0.5 * (1.0 + lax.erf(hidden * (0.5**0.5)))
    slope = cdf + hidden * jnp.exp(-0.5 * hidden * hidden) * (0.5 / jnp.pi) ** 0.5
    activation = (hidden * cdf).astype(BF)
    back_activation = dot("rd,fd->rf", cot_all, down_weight)
    back_hidden = (back_activation * slope).astype(BF)
    back_terms = dot("rf,df->rd", back_hidden, up_weight).astype(BF)
    back_blocks = [back_terms[k * own_rows : (k + 1) * own_rows] for k in range(n_t)]
    back_arrived = send_blocks(back_blocks, n_t)
    late_activation, late_hidden = after([activation, back_hidden], back_terms)
    down_keep, down_send = gradient(cot_all.T, late_activation, True, at, n_dp)
    up_keep, up_send = gradient(feed_all.T, late_hidden, True, at, n_dp)
    result_terms = blocks_of_product(late_activation, down_weight, n_t)
    back_feed = add_up(after(back_arrived, down_send, up_send, *result_terms))
    down_got, up_got = partner(down_send, "dp", n_dp, 1), partner(up_send, "dp", n_dp, 1)

    back_middle = cotangent.astype(F32) + norm_backward(back_feed, feed_hat, feed_root, feed_gain)
    back_branch = back_middle.astype(BF)
    back_attended = dot("hd,rd->hr", wo, back_branch).astype(BF)
    own_coef = own_valid / count_total
    message = make_message(back_attended, attended, stat, own_coef, heads)
    messages = gather_blocks(message, n_t)
    out_keep, out_send = gradient(back_branch, attended, False, at, n_dp, True)
    out_got = partner(out_send, "dp", n_dp, 1)
    down_got, up_got, out_got = after([down_got, up_got, out_got], message)
    feed_pair = first_cut((down_keep, down_got), (up_keep, up_got), (out_keep, out_got), orders, n_dp)
    messages = after(messages, *[send for _, send in feed_pair])
    result_terms[1:] = after(result_terms[1:], *messages)
    result_terms = send_blocks(result_terms, n_t)
    back_q, back_k, back_v = attend_backward(
        queries, keys, values, key_image, row_image, row_valid / count_total, span, messages
    )
    feed_pair = cross(feed_pair, orders, 0, n_dp)
    for i in steps[1:]:
        feed_pair = next_cut(feed_pair, orders, i, n_dp)
        if i == steps[1]:
            back_q, back_k, back_v = after([back_q, back_k, back_v], *[send for _, send in feed_pair])
        feed_pair = cross(feed_pair, orders, i, n_dp)

    v_keep, v_send = gradient(key_input_t, back_v, False, at, n_dp)
    k_keep, k_send = gradient(key_input_t, after(back_k, v_send), False, at, n_dp)
    q_keep, q_send = gradient(latent_t, after(back_q, k_send, *result_terms[1:]), False, at, n_dp)
    v_send, k_send = after([v_send, k_send], q_send)
    v_got, k_got, q_got = [partner(x, "dp", n_dp, 1) for x in (v_send, k_send, q_send)]
    latent_q = after(back_q, q_send)
    *latent_terms, latent_sums = latent_back(latent_q, back_k, back_v, wq, wk, wv, latent_blocks)
    v_got, k_got, q_got = after([v_got, k_got, q_got], latent_sums)
    k_got = after(k_got, *[got for _, got in feed_pair])
    pair = first_cut((v_keep, v_got), (k_keep, k_got), None, orders, n_dp)
    sends = [send for _, send in pair]
    latent_terms[1:] = after(latent_terms[1:], *sends)
    latent_terms = send_blocks(latent_terms, n_t)
    pair = cross(pair, orders, 0, n_dp)
    q_pair = first_cut(None, None, (q_keep, after(q_got, *sends)), orders, n_dp)
    out_blocks = tensor_blocks(feed_pair, [None], inner, at, n_t)
    features_grad, media_sums = media_back(
        after(back_k, latent_sums, *out_blocks, *[send for _, send in q_pair]),
        back_v, wk, wv, features, media_gain, own_patches,
    )
    for i in steps[1:]:
        gots = after([got for _, got in pair], features_grad)
        pair = [(keep, got) for (keep, _), got in zip(pair, gots)]
        pair = next_cut(pair, orders, i, n_dp)
        if i == steps[1]:
            q_sends = after([send for _, send in q_pair], *[send for _, send in pair], *latent_terms[1:])
            q_pair = [(keep, send) for (keep, _), send in zip(q_pair, q_sends)]
        pair = cross(pair, orders, i, n_dp)
    q_pair = cross(q_pair, orders, 0, n_dp)
    blocks = send_blocks(tensor_blocks(pair, [1, 0], inner, at, n_t), n_t)
    for i in steps[1:]:
        gots = after([got for _, got in q_pair], blocks[1], blocks[-1])
        q_pair = [(keep, got) for (keep, _), got in zip(q_pair, gots)]
        q_pair = cross(next_cut(q_pair, orders, i, n_dp), orders, i, n_dp)
    q_blocks = tensor_blocks(q_pair, [None], inner, at, n_t)
    grad_kv = add_up(after(blocks, *q_blocks))
    result, latents_grad, down_share, up_share = finish(
        after(result_terms, *q_blocks), latent_terms, feed_pair, middle, back_middle, latents, latent_gain, inner
    )

    qo_blocks = [jnp.concatenate(x, axis=0) for x in zip(q_blocks, out_blocks)]
    grad_qo = add_up(after(send_blocks(qo_blocks, n_t), result))
    grad_q, grad_o = grad_qo[0], grad_qo[1]

    sums = [media_sums[0], media_sums[1], latent_sums[0], latent_sums[1]] + gain_shift(back_feed, feed_hat)
    sums = jnp.stack(sums + [jnp.full((width,), penalty_part)] * 2)
    sums = after(sums, features_grad)
    sums = after(all_sum(sums, [("dp", n_dp)]), *q_blocks)
    sums = all_sum(sums, [("tensor", n_t)])
    penalty = sums[6, 0] / count_total
    share = width // (n_dp * n_t)
    mine = lax.dynamic_index_in_dim(
        sums.reshape(8, n_dp * n_t, share), p * n_t + z, 1, keepdims=False
    )
    return (
        result[None],
        penalty,
        latents_grad[None],
        features_grad[None],
        mine[0],
        mine[1],
        mine[2],
        mine[3],
        mine[4],
        mine[5],
        grad_q,
        jnp.moveaxis(grad_kv, 0, 1),
        grad_o.T,
        up_share,
        down_share.T,
    )


def solution(mesh):
    return jax.shard_map(
        local,
        mesh=mesh,
        in_specs=(
            P("dp", "tensor", None),
            P("dp", "tensor", None),
            P("dp", None),
            P("dp", None),
            P(),
            P(),
            P(),
            P(),
            P(),
            P(),
            P(None, "tensor"),
            P(None, None, "tensor"),
            P("tensor", None),
            P(None, "tensor"),
            P("tensor", None),
            P("dp", "tensor", None),
        ),
        out_specs=(
            P("dp", "tensor", None),
            P(),
            P("dp", "tensor", None),
            P("dp", "tensor", None),
            P(("dp", "tensor")),
            P(("dp", "tensor")),
            P(("dp", "tensor")),
            P(("dp", "tensor")),
            P(("dp", "tensor")),
            P(("dp", "tensor")),
            P("dp", "tensor"),
            P("dp", None, "tensor"),
            P("tensor", "dp"),
            P("dp", "tensor"),
            P("tensor", "dp"),
        ),
        check_vma=False,
    )
```

```python
from functools import partial

import jax
import jax.numpy as jnp
from jax import lax
from jax.experimental import pallas as pl
from jax.experimental.pallas import tpu as pltpu
from jax.sharding import PartitionSpec as P

HD = 96
LAT = 64
EPSILON = 1e-05
NEGATIVE = -1e30
SCALE = HD ** (-0.5)
BF = jnp.bfloat16
F32 = jnp.float32
VMEM_LIMIT = 48 * 1024 * 1024


def rotate(x, count, shift):
    return lax.ppermute(x, "tensor", [(i, (i + shift) % count) for i in range(count)])


def after(x, *done):
    many = isinstance(x, (list, tuple))
    held = lax.optimization_barrier((*x, *done) if many else (x, *done))
    return list(held[: len(x)]) if many else held[0]


def gather_blocks(x, count):
    return [x] + [rotate(x, count, k) for k in range(1, count)]


def send_blocks(blocks, count):
    return [blocks[0]] + [rotate(blocks[k], count, -k) for k in range(1, count)]


def scatter_blocks(blocks, count):
    return add_up(send_blocks(blocks, count))


def partner(x, axis, count, offset):
    return lax.ppermute(x, axis, [(i, i ^ offset) for i in range(count)])


def bits_of(count):
    return count.bit_length() - 1


def gradient_kernel(natural, turned, n_dp, at_ref, xt_ref, y_ref, keep_ref, send_ref, total_ref):
    dims = (((1,), (0,)), ((), ())) if natural else (((1,), (1,)), ((), ()))
    xt = xt_ref[...].T if turned else xt_ref[...]
    total_ref[...] = lax.dot_general(xt, y_ref[...], dims, preferred_element_type=F32)
    p, unit = at_ref[1], keep_ref.shape[1]
    for i in range(n_dp // 2):
        for odd, out in enumerate((keep_ref, send_ref)):
            first = pl.multiple_of((p ^ (2 * i + odd)) * unit, unit)
            out[i] = total_ref[pl.ds(first, unit), :].astype(BF)


def gradient(xt, y, natural, at, n_dp, turned=False):
    width, rows = xt.shape[::-1] if turned else xt.shape
    unit = width // n_dp
    wide = y.shape[1] if natural else y.shape[0]
    step = wide // 3
    half = n_dp // 2
    if natural:
        y_spec = pl.BlockSpec((rows, step), lambda i: (0, i))
    else:
        y_spec = pl.BlockSpec((step, rows), lambda i: (i, 0))
    return pl.pallas_call(
        partial(gradient_kernel, natural, turned, n_dp),
        grid=(3,),
        in_specs=[
            pl.BlockSpec(memory_space=pltpu.SMEM),
            pl.BlockSpec(xt.shape, lambda i: (0, 0)),
            y_spec,
        ],
        out_specs=[pl.BlockSpec((half, unit, step), lambda i: (0, 0, i))] * 2,
        out_shape=[pltpu.HBM((half, unit, wide), BF)] * 2,
        scratch_shapes=[pltpu.VMEM((width, step), F32)],
        compiler_params=pltpu.CompilerParams(vmem_limit_bytes=24 * 1024 * 1024),
    )(at, xt, y)


def bit_orders(count):
    outer = list(range(1, bits_of(count)))
    half = (len(outer) + 1) // 2
    return outer, outer[half:] + outer[:half]


def cut_kernel(widths, *refs):
    ins, (keep_ref, send_ref) = refs[:-2], refs[-2:]
    start = 0
    for i, wide in enumerate(widths):
        lanes = slice(start, start + wide)
        keep_a, got_a, keep_b, got_b = ins[4 * i : 4 * i + 4]
        keep_ref[:, :, lanes] = (keep_a[...].astype(F32) + got_a[...].astype(F32)).astype(BF)
        send_ref[:, :, lanes] = (keep_b[...].astype(F32) + got_b[...].astype(F32)).astype(BF)
        start += wide


def reduce_cut(parts, order, step, n_dp):
    left = [b for b in range(bits_of(n_dp) - 1, 0, -1) if b not in order[:step]]
    low = 1 << (len(left) - left.index(order[step]) - 1)
    count, rows, _ = parts[0][0].shape
    widths, specs, flat = [], [], []
    for keep, got, half in parts:
        wide = keep.shape[2] if half is None else keep.shape[2] // 2

        def at(bit, wide=wide, lane=half or 0):
            return pl.BlockSpec(
                (1, rows, wide), lambda i: (i // low * (2 * low) + bit * low + i % low, 0, lane)
            )

        widths.append(wide)
        specs += [at(0), at(0), at(1), at(1)]
        flat += [keep, got, keep, got]
    total = sum(widths)
    return pl.pallas_call(
        partial(cut_kernel, widths),
        grid=(count // 2,),
        in_specs=specs,
        out_specs=[pl.BlockSpec((1, rows, total), lambda i: (i, 0, 0))] * 2,
        out_shape=[pltpu.HBM((count // 2, rows, total), BF)] * 2,
        compiler_params=pltpu.CompilerParams(vmem_limit_bytes=20 * 1024 * 1024),
    )(*flat)


def first_cut(one, two, split, orders, n_dp):
    out = []
    for h, full in enumerate((one, two)):
        parts = [(*full, None)] if full else []
        parts += [(*split, h)] if split else []
        out.append(reduce_cut(parts, orders[h], 0, n_dp))
    return out


def next_cut(pair, orders, step, n_dp):
    return [reduce_cut([(*x, None)], order, step, n_dp) for x, order in zip(pair, orders)]


def cross(pair, orders, step, n_dp):
    return [
        (keep, partner(send, "dp", n_dp, 1 << order[step])) for (keep, send), order in zip(pair, orders)
    ]


def add_up(terms):
    total = terms[0].astype(F32)
    for term in terms[1:]:
        total = total + term.astype(F32)
    return total


def blocks_kernel(n_t, weights, at_ref, *refs):
    (a_keep, a_got, b_keep, b_got), outs = refs[:4], refs[4:]
    pairs = (a_keep, a_got), (b_keep, b_got)
    z = at_ref[0]
    columns = outs[0].shape[-1]
    half = n_t // 2

    def piece(which, lane):
        lanes = pl.ds(pl.multiple_of(lane, columns), columns)
        keep, got = pairs[which]
        return keep[0, :, lanes].astype(F32) + got[0, :, lanes].astype(F32)

    for k in range(n_t):
        block = lax.rem(z - k + n_t, n_t)
        for m, which in enumerate(weights):
            if which is None:
                lane = (a_keep.shape[2] - columns * half) + lax.rem(block, half) * columns
                value = jnp.where(block >= half, piece(1, lane), piece(0, lane))
            else:
                value = piece(which, block * columns)
            outs[k][m] = value.astype(outs[k].dtype)


def tensor_blocks(pair, weights, columns, at, n_t):
    flat = [x for terms in pair for x in terms]
    rows = flat[0].shape[1]
    return pl.pallas_call(
        partial(blocks_kernel, n_t, weights),
        in_specs=[pl.BlockSpec(memory_space=pltpu.SMEM)]
        + [pl.BlockSpec(memory_space=pltpu.VMEM)] * len(flat),
        out_shape=[
            jax.ShapeDtypeStruct((len(weights), rows, columns // n_t), F32 if k == 0 else BF)
            for k in range(n_t)
        ],
        compiler_params=pltpu.CompilerParams(vmem_limit_bytes=14 * 1024 * 1024),
    )(at, *flat)


def all_sum(x, axes):
    for axis, count in axes:
        for bit in range(bits_of(count)):
            x = x + partner(x, axis, count, 1 << bit)
    return x


def place_kernel(n_t, unit, z_rows, z_cols, offsets, parts, at_ref, own_ref, *refs):
    out_ref = refs[-1]
    z, p = at_ref[0], at_ref[1]
    rows, cols = own_ref.shape
    if z_rows:
        out_ref[pl.ds(pl.multiple_of(z * z_rows, z_rows), rows), :] = own_ref[...]
    else:
        out_ref[:, pl.ds(pl.multiple_of(z * z_cols, z_cols), cols)] = own_ref[...]
    for k in range(1, n_t):
        shard = lax.rem(z - k + n_t, n_t)
        for which, first, height, row_at, col_at in parts:
            for odd in range(2):
                src = refs[2 * which + odd]
                wide = src.shape[3]
                for i, off in enumerate(offsets[which]):
                    base = shard * z_rows + (p ^ (off ^ odd)) * unit + row_at
                    where = pl.ds(pl.multiple_of(base, 16), height)
                    if z_cols:
                        at = pl.ds(pl.multiple_of(shard * z_cols, z_cols), wide)
                    else:
                        at = slice(col_at, col_at + wide)
                    out_ref[where, at] = src[i, k - 1, first : first + height, :]


def reorder(x, places):
    return jnp.stack([lax.dynamic_index_in_dim(x, i, 0, keepdims=False) for i in places])


def project_kernel(place_kernel, count, at_ref, x_ref, *refs):
    place_kernel(at_ref, *refs[:-2])
    weight_ref, out_ref, turned_ref = refs[-3:]
    turned_ref[...] = x_ref[...].T
    step = weight_ref.shape[1] // count
    for c in range(count):
        cols = slice(c * step, (c + 1) * step)
        block = jnp.dot(x_ref[...], weight_ref[:, cols], preferred_element_type=F32)
        out_ref[cols, :] = block.T.astype(BF)


def place(own, pieces, offsets, parts, unit, by_rows, at, n_dp, n_t, x=None):
    rows, cols = own.shape
    shape = (n_t * rows, cols) if by_rows else (rows, n_t * cols)
    if unit % 16 or any(part[2] % 16 for part in parts):
        z, p = at[0], at[1]
        across = []
        for which, first, height, _, _ in parts:
            ordered = [None] * n_dp
            for i, off in enumerate(offsets[which]):
                for odd in range(2):
                    ordered[off ^ odd] = pieces[which][odd][i, :, first : first + height]
            across.append(reorder(jnp.stack(ordered), [p ^ d for d in range(n_dp)]))
        whole = jnp.concatenate(across, axis=3 if by_rows else 2).transpose(1, 0, 2, 3)
        whole = whole.reshape((n_t - 1, rows, cols))
        whole = jnp.concatenate([own[None], whole], axis=0)
        whole = reorder(whole, [(z - k + n_t) % n_t for k in range(n_t)])
        whole = whole.reshape(shape) if by_rows else whole.transpose(1, 0, 2).reshape(shape)
        return whole if x is None else (whole, dot("dh,rd->hr", whole, x).astype(BF), x.T)
    flat = [x for pair in pieces for x in pair]
    kernel = partial(
        place_kernel, n_t, unit, rows if by_rows else 0, 0 if by_rows else cols, offsets, parts
    )
    out = jax.ShapeDtypeStruct(shape, own.dtype)
    if x is None:
        first, outs = [], out
    else:
        kernel, first = partial(project_kernel, kernel, n_t), [x]
        outs = [out] + [jax.ShapeDtypeStruct((n, x.shape[0]), BF) for n in (shape[1], x.shape[1])]
    ins = [*first, own, *flat]
    return pl.pallas_call(
        kernel,
        out_shape=outs,
        in_specs=[pl.BlockSpec(memory_space=pltpu.SMEM)]
        + [pl.BlockSpec(memory_space=pltpu.VMEM)] * len(ins),
        compiler_params=pltpu.CompilerParams(vmem_limit_bytes=28 * 1024 * 1024),
    )(at, *ins)


def rotations(x, count):
    return [rotate(x, count, k) for k in range(1, count)]


def widen(one, two, step, orders, n_dp, *done):
    arrived = [partner(x, "dp", n_dp, 1 << order[step]) for x, order in zip((one, two), orders)]
    if done:
        arrived = after(arrived, *done)
    return [jnp.concatenate(x, axis=0) for x in zip((one, two), arrived)]


def widen_offsets(order):
    offsets = [0]
    for bit in order:
        offsets = offsets + [o ^ (1 << bit) for o in offsets]
    return offsets


def cores(one, two, n_dp):
    return [(x, partner(x, "dp", n_dp, 1)) for x in (one, two)]


def share_of(x, axis, count):
    size = x.shape[axis] // count
    return lax.dynamic_slice_in_dim(x, lax.axis_index("dp") * size, size, axis)


def three(x):
    high = x.astype(BF)
    left = x - high.astype(F32)
    middle = left.astype(BF)
    low = (left - middle.astype(F32)).astype(BF)
    return jnp.concatenate([high, middle, low], axis=0)


def join(x, count):
    x = x.astype(F32)
    return x[:count] + x[count : 2 * count] + x[2 * count :]


GROUP = 8
CHUNK = 128
TN = (((0,), (0,)), ((), ()))
NT = (((1,), (1,)), ((), ()))


def forward_kernel(heads, n_t, span_ref, q_ref, k_ref, v_ref, seg_ref, img_ref, *rest):
    msgs, stat, acc, run = rest[:n_t], rest[n_t], rest[n_t + 1], rest[n_t + 2]
    g = pl.program_id(0)
    rows = q_ref.shape[1] // n_t
    keys = k_ref.shape[1]
    for k in range(n_t):
        cols = slice(k * rows, (k + 1) * rows)
        image = img_ref[:, cols]
        acc[...] = jnp.zeros_like(acc)
        run[...] = jnp.zeros_like(run)
        run[0] = jnp.full(run.shape[1:], NEGATIVE)

        def step(at, cols=cols, image=image):
            allowed = seg_ref[at, :] == image
            bands = [slice(h * HD, (h + 1) * HD) for h in range(GROUP)]
            scores = [
                SCALE
                * lax.dot_general(k_ref[b, at], q_ref[b, cols], TN, preferred_element_type=F32)
                for b in bands
            ]
            scores = [jnp.where(allowed, x, NEGATIVE) for x in scores]
            old = [run[0, h : h + 1] for h in range(GROUP)]
            tops = [
                jnp.maximum(m, jnp.max(x, axis=0, keepdims=True)) for m, x in zip(old, scores)
            ]
            weights = [jnp.where(allowed, jnp.exp(x - m), 0.0) for x, m in zip(scores, tops)]
            outs = [
                jnp.dot(v_ref[b, at], w.astype(BF), preferred_element_type=F32)
                for b, w in zip(bands, weights)
            ]
            fades = [jnp.exp(m - n) for m, n in zip(old, tops)]
            for h in range(GROUP):
                run[0, h : h + 1] = tops[h]
                run[1, h : h + 1] = run[1, h : h + 1] * fades[h] + jnp.sum(
                    weights[h], axis=0, keepdims=True
                )
                run[2, h : h + 1] = run[2, h : h + 1] * fades[h] + jnp.sum(
                    weights[h] * scores[h], axis=0, keepdims=True
                )
            for b, f, o in zip(bands, fades, outs):
                acc[b, :] = acc[b, :] * f + o

        if k == 0:
            step(slice(keys - rows, keys))

        @pl.loop(span_ref[0, k], span_ref[1, k])
        def _(c, step=step):
            step(pl.ds(pl.multiple_of(c * CHUNK, CHUNK), CHUNK))

        total = run[1, :GROUP]
        some = total > 0.0
        safe = jnp.where(some, total, 1.0)
        inverse = jnp.where(some, 1.0 / safe, 0.0)
        stat[0, pl.ds(g, 1), :, cols] = jnp.where(some, run[0, :GROUP] + jnp.log(safe), NEGATIVE)[None]
        stat[1, pl.ds(g, 1), :, cols] = (run[2, :GROUP] * inverse)[None]
        for h in range(GROUP):
            band = slice(h * HD, (h + 1) * HD)
            first = pl.multiple_of((g * GROUP + h) * HD, HD)
            msgs[k][pl.ds(first, HD), :] = (acc[band, :] * inverse[h : h + 1]).astype(BF)

    @pl.when(g == heads // GROUP - 1)
    def _():
        for k in range(n_t):
            cols = slice(k * rows, (k + 1) * rows)
            for i in range(2):
                first = heads * (HD + 3 * i)
                msgs[k][first : first + 3 * heads, :] = three(
                    stat[i, :, :, cols].reshape(heads, rows)
                )


def attend_forward(q, k, v, seg, img, span, n_t):
    heads = q.shape[0] // HD
    rows, keys = q.shape[1], k.shape[1]
    one = rows // n_t
    tall = heads * (HD + 6)
    band = GROUP * HD
    return pl.pallas_call(
        partial(forward_kernel, heads, n_t),
        grid_spec=pltpu.PrefetchScalarGridSpec(
            num_scalar_prefetch=1,
            grid=(heads // GROUP,),
            in_specs=[
                pl.BlockSpec((band, rows), lambda g, s: (g, 0)),
                pl.BlockSpec((band, keys), lambda g, s: (g, 0)),
                pl.BlockSpec((band, keys), lambda g, s: (g, 0)),
                pl.BlockSpec((keys, 1), lambda g, s: (0, 0)),
                pl.BlockSpec((1, rows), lambda g, s: (0, 0)),
            ],
            out_specs=[pl.BlockSpec((tall, one), lambda g, s: (0, 0))] * n_t,
            scratch_shapes=[
                pltpu.VMEM((2, heads // GROUP, GROUP, rows), F32),
                pltpu.VMEM((band, one), F32),
                pltpu.VMEM((3, 8, one), F32),
            ],
        ),
        out_shape=[jax.ShapeDtypeStruct((tall, one), BF)] * n_t,
        compiler_params=pltpu.CompilerParams(vmem_limit_bytes=20 * 1024 * 1024),
    )(span, q, k, v, seg, img)


def combine_kernel(heads, n_t, *refs):
    msgs, (out_ref, stat_ref) = refs[:n_t], refs[n_t:]
    base = heads * HD
    logs = [join(m[base : base + 3 * heads, :], heads) for m in msgs]
    means = [join(m[base + 3 * heads :, :], heads) for m in msgs]
    top = logs[0]
    for x in logs[1:]:
        top = jnp.maximum(top, x)
    shares = [jnp.exp(x - top) for x in logs]
    total = shares[0]
    for x in shares[1:]:
        total = total + x
    shares = [x / total for x in shares]
    mean = shares[0] * means[0]
    for s, x in zip(shares[1:], means[1:]):
        mean = mean + s * x
    stat_ref[:heads, :] = top + jnp.log(total)
    stat_ref[heads:, :] = mean
    for h in range(heads):
        at = slice(h * HD, (h + 1) * HD)
        acc = msgs[0][at, :].astype(F32) * shares[0][h : h + 1, :]
        for s, m in zip(shares[1:], msgs[1:]):
            acc = acc + m[at, :].astype(F32) * s[h : h + 1, :]
        out_ref[at, :] = acc.astype(BF)


def combine(msgs, heads):
    one = msgs[0].shape[1]
    return pl.pallas_call(
        partial(combine_kernel, heads, len(msgs)),
        out_shape=[
            jax.ShapeDtypeStruct((heads * HD, one), BF),
            jax.ShapeDtypeStruct((2 * heads, one), F32),
        ],
        compiler_params=pltpu.CompilerParams(vmem_limit_bytes=8 * 1024 * 1024),
    )(*msgs)


def message_kernel(heads, do_ref, out_ref, stat_ref, coef_ref, msg_ref):
    base = heads * HD
    deltas = []
    for h in range(heads):
        at = slice(h * HD, (h + 1) * HD)
        grad = do_ref[at, :].astype(F32)
        deltas.append(jnp.sum(grad * out_ref[at, :].astype(F32), axis=0, keepdims=True))
    msg_ref[:base, :] = do_ref[...]
    delta = jnp.concatenate(deltas, axis=0) - coef_ref[...] * stat_ref[heads:, :]
    msg_ref[base : base + 3 * heads, :] = three(stat_ref[:heads, :])
    msg_ref[base + 3 * heads :, :] = three(delta)


def make_message(do, out, stat, coef, heads):
    return pl.pallas_call(
        partial(message_kernel, heads),
        out_shape=jax.ShapeDtypeStruct((heads * (HD + 6), do.shape[1]), BF),
        compiler_params=pltpu.CompilerParams(vmem_limit_bytes=6 * 1024 * 1024),
    )(do, out, stat, coef)


def backward_kernel(heads, n_t, span_ref, q_ref, k_ref, v_ref, seg_ref, img_ref, coef_ref, *rest):
    grads, stats = rest[:n_t], rest[n_t : 2 * n_t]
    dq_ref, dk_ref, dv_ref, stat, dq, dk, dv = rest[2 * n_t :]
    g = pl.program_id(0)
    rows = q_ref.shape[1] // n_t
    keys = k_ref.shape[1]

    @pl.when(g == 0)
    def _():
        for i in range(n_t):
            cols = slice(i * rows, (i + 1) * rows)
            for j in range(2):
                part = join(stats[i][3 * j * heads : 3 * (j + 1) * heads, :], heads)
                stat[j, :, :, cols] = part.reshape(heads // GROUP, GROUP, rows)

    dk[...] = jnp.zeros_like(dk)
    dv[...] = jnp.zeros_like(dv)
    for i in range(n_t):
        cols = slice(i * rows, (i + 1) * rows)
        image, coef = img_ref[:, cols], coef_ref[:, cols]
        logs = stat[0, pl.ds(g, 1), :, cols][0]
        deltas = stat[1, pl.ds(g, 1), :, cols][0]
        dq[...] = jnp.zeros_like(dq)

        def step(at, cols=cols, image=image, coef=coef, logs=logs, deltas=deltas, grad_ref=grads[i]):
            allowed = seg_ref[at, :] == image
            bands = [slice(h * HD, (h + 1) * HD) for h in range(GROUP)]
            scores = [
                SCALE
                * lax.dot_general(k_ref[b, at], q_ref[b, cols], TN, preferred_element_type=F32)
                for b in bands
            ]
            back_probs = [
                lax.dot_general(v_ref[b, at], grad_ref[b, :], TN, preferred_element_type=F32)
                for b in bands
            ]
            probs = [
                jnp.where(allowed, jnp.exp(jnp.where(allowed, x - logs[h : h + 1], 0.0)), 0.0)
                for h, x in enumerate(scores)
            ]
            backs = [
                (p * (y - coef * x - deltas[h : h + 1])).astype(BF)
                for h, (x, y, p) in enumerate(zip(scores, back_probs, probs))
            ]
            probs = [p.astype(BF) for p in probs]
            for b, p in zip(bands, probs):
                dv[b, at] += lax.dot_general(grad_ref[b, :], p, NT, preferred_element_type=F32)
            for b, x in zip(bands, backs):
                dq[b, :] += jnp.dot(k_ref[b, at], x, preferred_element_type=F32)
            for b, x in zip(bands, backs):
                dk[b, at] += lax.dot_general(q_ref[b, cols], x, NT, preferred_element_type=F32)

        if i == 0:
            step(slice(keys - rows, keys))

        @pl.loop(span_ref[0, i], span_ref[1, i])
        def _(c, step=step):
            step(pl.ds(pl.multiple_of(c * CHUNK, CHUNK), CHUNK))

        dq_ref[:, cols] = (dq[...] * SCALE).astype(BF)
    dk_ref[...] = (dk[...] * SCALE).astype(BF)
    dv_ref[...] = dv[...].astype(BF)


def attend_backward(q, k, v, seg, img, coef, span, msgs):
    n_t = len(msgs)
    heads = q.shape[0] // HD
    rows, keys = q.shape[1], k.shape[1]
    one = rows // n_t
    band = GROUP * HD
    wide = [pl.BlockSpec((band, n), lambda g, s: (g, 0)) for n in (rows, keys, keys)]
    return pl.pallas_call(
        partial(backward_kernel, heads, n_t),
        grid_spec=pltpu.PrefetchScalarGridSpec(
            num_scalar_prefetch=1,
            grid=(heads // GROUP,),
            in_specs=wide
            + [
                pl.BlockSpec((keys, 1), lambda g, s: (0, 0)),
                pl.BlockSpec((1, rows), lambda g, s: (0, 0)),
                pl.BlockSpec((1, rows), lambda g, s: (0, 0)),
            ]
            + [pl.BlockSpec((band, one), lambda g, s: (g, 0))] * n_t
            + [pl.BlockSpec((6 * heads, one), lambda g, s: (HD // 6, 0))] * n_t,
            out_specs=wide,
            scratch_shapes=[
                pltpu.VMEM((2, heads // GROUP, GROUP, rows), F32),
                pltpu.VMEM((band, one), F32),
                pltpu.VMEM((band, keys), F32),
                pltpu.VMEM((band, keys), F32),
            ],
        ),
        out_shape=[
            jax.ShapeDtypeStruct(q.shape, BF),
            jax.ShapeDtypeStruct(k.shape, BF),
            jax.ShapeDtypeStruct(v.shape, BF),
        ],
        compiler_params=pltpu.CompilerParams(vmem_limit_bytes=36 * 1024 * 1024),
        cost_estimate=pl.CostEstimate(
            flops=60 * heads * HD * rows * keys,
            bytes_accessed=60 * 1024 * 1024,
            transcendentals=heads * rows * keys,
        ),
    )(span, q, k, v, seg, img, coef, *msgs, *msgs)


def norm_parts(values):
    values = values.astype(F32)
    center = values - jnp.mean(values, axis=-1, keepdims=True)
    inv_root = lax.rsqrt(jnp.mean(center * center, axis=-1, keepdims=True) + EPSILON)
    return center * inv_root, inv_root


def norm_backward(grad_rows, normal, inv_root, gain_row):
    scaled = grad_rows * gain_row
    reduced = (
        scaled
        - jnp.mean(scaled, axis=-1, keepdims=True)
        - normal * jnp.mean(scaled * normal, axis=-1, keepdims=True)
    )
    return reduced * inv_root


def gain_shift(grad_rows, normal):
    return [jnp.sum(grad_rows * normal, axis=0), jnp.sum(grad_rows, axis=0)]


def rows_back(grads, weights):
    total = None
    for grad, weight in zip(grads, weights):
        term = lax.dot_general(grad, weight, (((0,), (1,)), ((), ())), preferred_element_type=F32)
        total = term if total is None else total + term
    return total


def media_back_kernel(dk_ref, dv_ref, wk_ref, wv_ref, x_ref, gain_ref, out_ref, sums_ref):
    back = rows_back((dk_ref[...], dv_ref[...]), (wk_ref[...], wv_ref[...]))
    normal, root = norm_parts(x_ref[...])
    out_ref[...] = norm_backward(back, normal, root, gain_ref[...])

    @pl.when(pl.program_id(0) == 0)
    def _():
        sums_ref[...] = jnp.zeros_like(sums_ref)

    sums_ref[0:1] += jnp.sum(back * normal, axis=0, keepdims=True)
    sums_ref[1:2] += jnp.sum(back, axis=0, keepdims=True)


def media_back(back_k, back_v, wk, wv, features, gain, block):
    rows, width = features.shape
    inner = back_k.shape[0]
    whole = pl.BlockSpec((width, inner), lambda i: (0, 0))
    return pl.pallas_call(
        media_back_kernel,
        grid=(rows // block,),
        in_specs=[pl.BlockSpec((inner, block), lambda i: (0, i))] * 2
        + [whole] * 2
        + [pl.BlockSpec((block, width), lambda i: (i, 0)), pl.BlockSpec((1, width), lambda i: (0, 0))],
        out_specs=[
            pl.BlockSpec((block, width), lambda i: (i, 0)),
            pl.BlockSpec((8, width), lambda i: (0, 0)),
        ],
        out_shape=[
            jax.ShapeDtypeStruct((rows, width), F32),
            jax.ShapeDtypeStruct((8, width), F32),
        ],
        compiler_params=pltpu.CompilerParams(vmem_limit_bytes=VMEM_LIMIT),
    )(back_k, back_v, wk, wv, features, gain[None])


def latent_back_kernel(n_t, dq_ref, dk_ref, dv_ref, wq_ref, wk_ref, wv_ref, *refs):
    xs, outs, sums_ref = refs[:n_t], refs[n_t:-1], refs[-1]
    rows = xs[0].shape[0]
    gain_sum = shift_sum = None
    total = rows_back((dq_ref[...],), (wq_ref[...],))
    own = rows_back((dk_ref[...], dv_ref[...]), (wk_ref[...], wv_ref[...]))
    for k in range(n_t):
        back = total[k * rows : (k + 1) * rows]
        if k == 0:
            back = back + own
        outs[k][...] = back.astype(outs[k].dtype)
        normal, _ = norm_parts(xs[k][...])
        gain_part = jnp.sum(back * normal, axis=0, keepdims=True)
        shift_part = jnp.sum(back, axis=0, keepdims=True)
        gain_sum = gain_part if gain_sum is None else gain_sum + gain_part
        shift_sum = shift_part if shift_sum is None else shift_sum + shift_part
    sums_ref[...] = jnp.zeros_like(sums_ref)
    sums_ref[0:1] = gain_sum
    sums_ref[1:2] = shift_sum


def latent_back(back_q, back_k, back_v, wq, wk, wv, blocks):
    n_t = len(blocks)
    rows, width = blocks[0].shape
    inner, keys = back_k.shape
    tail = pl.BlockSpec((inner, rows), lambda i: (0, keys // rows - 1))
    whole = pl.BlockSpec((width, inner), lambda i: (0, 0))
    return pl.pallas_call(
        partial(latent_back_kernel, n_t),
        grid=(1,),
        in_specs=[pl.BlockSpec(back_q.shape, lambda i: (0, 0)), tail, tail, whole, whole, whole]
        + [pl.BlockSpec((rows, width), lambda i: (0, 0))] * n_t,
        out_specs=[pl.BlockSpec((rows, width), lambda i: (0, 0))] * n_t
        + [pl.BlockSpec((8, width), lambda i: (0, 0))],
        out_shape=[jax.ShapeDtypeStruct((rows, width), BF if k else F32) for k in range(n_t)]
        + [jax.ShapeDtypeStruct((8, width), F32)],
        compiler_params=pltpu.CompilerParams(vmem_limit_bytes=50 * 1024 * 1024),
    )(back_q, back_k, back_v, wq, wk, wv, *blocks)


def blocks_of_product_kernel(n_t, a_ref, b_ref, *outs):
    total = jnp.dot(a_ref[...], b_ref[...], preferred_element_type=F32)
    rows = outs[0].shape[0]
    for k in range(n_t):
        outs[k][...] = total[k * rows : (k + 1) * rows].astype(outs[k].dtype)


def blocks_of_product(a, b, n_t):
    shape = a.shape[0] // n_t, b.shape[1]
    return list(
        pl.pallas_call(
            partial(blocks_of_product_kernel, n_t),
            out_shape=[jax.ShapeDtypeStruct(shape, BF if k else F32) for k in range(n_t)],
            compiler_params=pltpu.CompilerParams(vmem_limit_bytes=VMEM_LIMIT),
        )(a, b)
    )


def finish_kernel(n_t, columns, *refs):
    results, latent_terms, feeds = refs[:n_t], refs[n_t : 2 * n_t], refs[2 * n_t : 2 * n_t + 4]
    middle_ref, back_ref, x_ref, gain_ref, *outs = refs[2 * n_t + 4 :]
    outs[0][...] = (middle_ref[...] + add_up([r[...] for r in results])).astype(BF)
    normal, root = norm_parts(x_ref[...])
    back = add_up([r[...] for r in latent_terms])
    outs[1][...] = back_ref[...] + norm_backward(back, normal, root, gain_ref[...])
    for m in range(2):
        keep, got = feeds[2 * m], feeds[2 * m + 1]
        outs[2 + m][...] = keep[0, :, :columns].astype(F32) + got[0, :, :columns].astype(F32)


def finish(result_terms, latent_terms, feed_pair, middle, back_middle, latents, gain, columns):
    feeds = [x for pair in feed_pair for x in pair]
    unit, width = feeds[0].shape[1], middle.shape[1]
    return pl.pallas_call(
        partial(finish_kernel, len(result_terms), columns),
        out_shape=[
            jax.ShapeDtypeStruct(middle.shape, BF),
            jax.ShapeDtypeStruct(middle.shape, F32),
            jax.ShapeDtypeStruct((unit, columns), F32),
            jax.ShapeDtypeStruct((unit, columns), F32),
        ],
        compiler_params=pltpu.CompilerParams(vmem_limit_bytes=20 * 1024 * 1024),
    )(*result_terms, *latent_terms, *feeds, middle, back_middle, latents, gain[None])


def dot(equation, a, b):
    return jnp.einsum(equation, a, b, preferred_element_type=F32)


def local(
    latents,
    features,
    lengths,
    valid_media,
    media_gain,
    media_shift,
    latent_gain,
    latent_shift,
    feed_gain,
    feed_shift,
    query_weight,
    key_value_weight,
    output_weight,
    up_weight,
    down_weight,
    cotangent,
):
    n_t = lax.axis_size("tensor")
    n_dp = lax.axis_size("dp")
    z, p = lax.axis_index("tensor"), lax.axis_index("dp")
    at = jnp.stack([z, p]).astype(jnp.int32)
    latents, features, cotangent = latents[0], features[0], cotangent[0]
    lengths, valid = lengths[0], valid_media[0]
    width = latents.shape[1]
    own_rows, own_patches = latents.shape[0], features.shape[0]
    inner = query_weight.shape[1] * n_t
    heads = inner // HD
    images = lengths.shape[0]


    ends = jnp.sum(
        jnp.where(jnp.arange(images)[:, None] <= jnp.arange(images)[None, :], lengths[:, None], 0),
        axis=0,
    )
    positions = z * own_patches + jnp.arange(own_patches, dtype=jnp.int32)
    segment = jnp.sum((positions[:, None] >= ends[None, :]).astype(jnp.int32), axis=1)
    hit = segment[:, None] == jnp.arange(images, dtype=jnp.int32)[None, :]
    patch_valid = jnp.sum(jnp.where(hit, valid[None, :], 0), axis=1)
    patch_segment = jnp.where(patch_valid > 0, segment, -1)
    own_images = (z * own_rows + jnp.arange(own_rows, dtype=jnp.int32)) // LAT
    key_image = jnp.concatenate([patch_segment, own_images])[:, None]
    block_of = (z - jnp.arange(n_t, dtype=jnp.int32) + n_t) % n_t
    row_index = block_of[:, None] * own_rows + jnp.arange(own_rows, dtype=jnp.int32)[None, :]
    row_image = (row_index // LAT).reshape(1, -1)
    rows_each = own_rows // LAT
    local_ends = jnp.clip(ends - z * own_patches, 0, own_patches)
    local_starts = jnp.clip(ends - lengths - z * own_patches, 0, own_patches)
    block_image = block_of * rows_each
    at_image = jnp.arange(images, dtype=jnp.int32)[None, :]
    low = jnp.sum(jnp.where(at_image == block_image[:, None], local_starts[None, :], 0), axis=1)
    high = jnp.sum(
        jnp.where(at_image == block_image[:, None] + rows_each - 1, local_ends[None, :], 0), axis=1
    )
    span = jnp.stack([low // CHUNK, (high + CHUNK - 1) // CHUNK]).astype(jnp.int32)
    row_valid = jnp.sum(
        jnp.where(row_image.T == jnp.arange(images, dtype=jnp.int32)[None, :], valid[None, :], 0),
        axis=1,
    ).astype(F32)[None, :]

    orders = bit_orders(n_dp)
    steps = range(len(orders[0]))
    offsets = [widen_offsets(order) for order in orders]
    unit, part = width // n_dp, query_weight.shape[1]
    keyval = jnp.moveaxis(share_of(key_value_weight, 0, n_dp), 1, 0)
    kv_z = rotations(keyval, n_t)
    media_hat, media_root = norm_parts(features)
    media_normed = (media_hat * media_gain + media_shift).astype(BF)
    own_hat, own_root = norm_parts(latents)
    own_normed = (own_hat * latent_gain + latent_shift).astype(BF)
    key_input = jnp.concatenate([media_normed, own_normed], axis=0)
    kv_own = [key_value_weight[:, 0], key_value_weight[:, 1]]
    *kv_z, key_input, k_own, v_own = after([*kv_z, key_input, *kv_own])
    q_share = share_of(query_weight, 0, n_dp).reshape(2, unit // 2, part)
    o_share = share_of(output_weight, 0, n_dp)
    o_unit = o_share.shape[0]
    o_share = o_share.reshape(o_unit, 2, -1, part).transpose(1, 2, 0, 3).reshape(2, -1, part)
    qo_share = jnp.concatenate([q_share, o_share], axis=1)
    qo_z = rotations(after(qo_share, *kv_z), n_t)
    k_held, v_held = [jnp.stack([x[m] for x in kv_z])[None] for m in range(2)]
    for step in steps[:-1]:
        k_held, v_held = widen(k_held, v_held, step, orders, n_dp)
    k_held, v_held = after([k_held, v_held], *qo_z)
    gathered = lax.all_gather(jnp.stack(after([latents, cotangent], *qo_z)), "tensor", axis=0)
    others = [
        lax.dynamic_index_in_dim(gathered, (z - k + n_t) % n_t, 0, keepdims=False)
        for k in range(1, n_t)
    ]
    latent_blocks = [latents] + [x[0] for x in others]
    cot_blocks = [cotangent] + [x[1] for x in others]
    k_held, v_held = widen(k_held, v_held, steps[-1], orders, n_dp)
    k_pieces, v_pieces = cores(k_held, v_held, n_dp)
    qo_held = [jnp.stack([x[m] for x in qo_z])[None] for m in range(2)]
    qo_held = after(qo_held, k_held, v_held)
    whole = [(0, 0, unit, 0, 0)]
    wk, keys, key_input_t = place(k_own, [k_pieces], offsets[:1], whole, unit, False, at, n_dp, n_t, key_input)
    wv, values, _ = place(v_own, [v_pieces], offsets[1:], whole, unit, False, at, n_dp, n_t, key_input)
    for step in steps[:-1]:
        qo_held = widen(*qo_held, step, orders, n_dp, keys)
    qo_held = widen(*qo_held, steps[-1], orders, n_dp, values)
    qo_pieces = cores(*qo_held, n_dp)
    latent_all = jnp.concatenate(latent_blocks, axis=0)
    latent_hat, latent_root = norm_parts(latent_all)
    latent_normed = (latent_hat * latent_gain + latent_shift).astype(BF)
    cuts = [(h, 0, unit // 2, h * unit // 2, 0) for h in range(2)]
    wq, queries, latent_t = place(
        query_weight, qo_pieces, offsets, cuts, unit, False, at, n_dp, n_t, latent_normed
    )
    cuts = [
        (h, unit // 2 + c * o_unit, o_unit, 0, h * width // 2 + c * part)
        for h in range(2)
        for c in range(width // 2 // part)
    ]
    wo = place(output_weight, qo_pieces, offsets, cuts, o_unit, True, at, n_dp, n_t)
    sent = attend_forward(queries, keys, values, key_image, row_image, span, n_t)
    got = [sent[0]] + [rotate(sent[k], n_t, -k) for k in range(1, n_t)]
    count_part = after(jnp.full((8, 128), jnp.sum(valid).astype(F32)), *sent[1:])
    count_total = all_sum(count_part, [("dp", n_dp)])[0, 0]
    got = after(got, count_total, wo)
    attended, stat = combine(got, heads)
    entropy = stat[:heads] - stat[heads:]
    own_valid = row_valid[:, :own_rows]
    penalty_part = jnp.sum(entropy * own_valid)

    latent_own = latents.astype(F32)
    middle = latent_own + dot("hr,hd->rd", attended, wo)
    feed_hat, feed_root = norm_parts(middle)
    feed_normed = (feed_hat * feed_gain + feed_shift).astype(BF)
    feed_all = jnp.concatenate(gather_blocks(feed_normed, n_t), axis=0)
    cot_all = jnp.concatenate(after(cot_blocks, feed_normed), axis=0)
    hidden = dot("rd,df->rf", feed_all, up_weight)
    cdf = 0.5 * (1.0 + lax.erf(hidden * (0.5**0.5)))
    slope = cdf + hidden * jnp.exp(-0.5 * hidden * hidden) * (0.5 / jnp.pi) ** 0.5
    activation = (hidden * cdf).astype(BF)
    back_activation = dot("rd,fd->rf", cot_all, down_weight)
    back_hidden = (back_activation * slope).astype(BF)
    back_terms = dot("rf,df->rd", back_hidden, up_weight).astype(BF)
    back_blocks = [back_terms[k * own_rows : (k + 1) * own_rows] for k in range(n_t)]
    back_arrived = send_blocks(back_blocks, n_t)
    late_activation, late_hidden = after([activation, back_hidden], back_terms)
    down_keep, down_send = gradient(cot_all, late_activation, True, at, n_dp, True)
    up_keep, up_send = gradient(feed_all, late_hidden, True, at, n_dp, True)
    result_terms = blocks_of_product(late_activation, down_weight, n_t)
    back_feed = add_up(after(back_arrived, down_send, up_send, *result_terms))
    down_got, up_got = partner(down_send, "dp", n_dp, 1), partner(up_send, "dp", n_dp, 1)

    back_middle = cotangent.astype(F32) + norm_backward(back_feed, feed_hat, feed_root, feed_gain)
    back_branch = back_middle.astype(BF)
    back_attended = dot("hd,rd->hr", wo, back_branch).astype(BF)
    own_coef = own_valid / count_total
    message = make_message(back_attended, attended, stat, own_coef, heads)
    messages = gather_blocks(message, n_t)
    out_keep, out_send = gradient(back_branch, attended, False, at, n_dp, True)
    out_got = partner(out_send, "dp", n_dp, 1)
    down_got, up_got, out_got = after([down_got, up_got, out_got], message)
    feed_pair = first_cut((down_keep, down_got), (up_keep, up_got), (out_keep, out_got), orders, n_dp)
    messages = after(messages, *[send for _, send in feed_pair])
    result_terms[1:] = after(result_terms[1:], *messages)
    result_terms = send_blocks(result_terms, n_t)
    back_q, back_k, back_v = attend_backward(
        queries, keys, values, key_image, row_image, row_valid / count_total, span, messages
    )
    feed_pair = cross(feed_pair, orders, 0, n_dp)
    for i in steps[1:]:
        feed_pair = next_cut(feed_pair, orders, i, n_dp)
        if i == steps[1]:
            back_q, back_k, back_v = after([back_q, back_k, back_v], *[send for _, send in feed_pair])
        feed_pair = cross(feed_pair, orders, i, n_dp)

    v_keep, v_send = gradient(key_input_t, back_v, False, at, n_dp)
    k_keep, k_send = gradient(key_input_t, after(back_k, v_send), False, at, n_dp)
    q_keep, q_send = gradient(latent_t, after(back_q, k_send, *result_terms[1:]), False, at, n_dp)
    v_send, k_send = after([v_send, k_send], q_send)
    v_got, k_got, q_got = [partner(x, "dp", n_dp, 1) for x in (v_send, k_send, q_send)]
    latent_q = after(back_q, q_send)
    *latent_terms, latent_sums = latent_back(latent_q, back_k, back_v, wq, wk, wv, latent_blocks)
    v_got, k_got, q_got = after([v_got, k_got, q_got], latent_sums)
    k_got = after(k_got, *[got for _, got in feed_pair])
    pair = first_cut((v_keep, v_got), (k_keep, k_got), None, orders, n_dp)
    sends = [send for _, send in pair]
    latent_terms[1:] = after(latent_terms[1:], *sends)
    latent_terms = send_blocks(latent_terms, n_t)
    pair = cross(pair, orders, 0, n_dp)
    q_pair = first_cut(None, None, (q_keep, after(q_got, *sends)), orders, n_dp)
    out_blocks = tensor_blocks(feed_pair, [None], inner, at, n_t)
    features_grad, media_sums = media_back(
        after(back_k, latent_sums, *out_blocks, *[send for _, send in q_pair]),
        back_v, wk, wv, features, media_gain, own_patches,
    )
    for i in steps[1:]:
        gots = after([got for _, got in pair], features_grad)
        pair = [(keep, got) for (keep, _), got in zip(pair, gots)]
        pair = next_cut(pair, orders, i, n_dp)
        if i == steps[1]:
            q_sends = after([send for _, send in q_pair], *[send for _, send in pair], *latent_terms[1:])
            q_pair = [(keep, send) for (keep, _), send in zip(q_pair, q_sends)]
        pair = cross(pair, orders, i, n_dp)
    q_pair = cross(q_pair, orders, 0, n_dp)
    blocks = send_blocks(tensor_blocks(pair, [1, 0], inner, at, n_t), n_t)
    for i in steps[1:]:
        gots = after([got for _, got in q_pair], blocks[1], blocks[-1])
        q_pair = [(keep, got) for (keep, _), got in zip(q_pair, gots)]
        q_pair = cross(next_cut(q_pair, orders, i, n_dp), orders, i, n_dp)
    q_blocks = tensor_blocks(q_pair, [None], inner, at, n_t)
    grad_kv = add_up(after(blocks, *q_blocks))
    result, latents_grad, down_share, up_share = finish(
        after(result_terms, *q_blocks), latent_terms, feed_pair, middle, back_middle, latents, latent_gain, inner
    )

    qo_blocks = [jnp.concatenate(x, axis=0) for x in zip(q_blocks, out_blocks)]
    grad_qo = add_up(after(send_blocks(qo_blocks, n_t), result))
    grad_q, grad_o = grad_qo[0], grad_qo[1]

    sums = [media_sums[0], media_sums[1], latent_sums[0], latent_sums[1]] + gain_shift(back_feed, feed_hat)
    sums = jnp.stack(sums + [jnp.full((width,), penalty_part)] * 2)
    sums = after(sums, features_grad)
    sums = after(all_sum(sums, [("dp", n_dp)]), *q_blocks)
    sums = all_sum(sums, [("tensor", n_t)])
    penalty = sums[6, 0] / count_total
    share = width // (n_dp * n_t)
    mine = lax.dynamic_index_in_dim(
        sums.reshape(8, n_dp * n_t, share), p * n_t + z, 1, keepdims=False
    )
    return (
        result[None],
        penalty,
        latents_grad[None],
        features_grad[None],
        mine[0],
        mine[1],
        mine[2],
        mine[3],
        mine[4],
        mine[5],
        grad_q,
        jnp.moveaxis(grad_kv, 0, 1),
        grad_o.T,
        up_share,
        down_share.T,
    )


def solution(mesh):
    return jax.shard_map(
        local,
        mesh=mesh,
        in_specs=(
            P("dp", "tensor", None),
            P("dp", "tensor", None),
            P("dp", None),
            P("dp", None),
            P(),
            P(),
            P(),
            P(),
            P(),
            P(),
            P(None, "tensor"),
            P(None, None, "tensor"),
            P("tensor", None),
            P(None, "tensor"),
            P("tensor", None),
            P("dp", "tensor", None),
        ),
        out_specs=(
            P("dp", "tensor", None),
            P(),
            P("dp", "tensor", None),
            P("dp", "tensor", None),
            P(("dp", "tensor")),
            P(("dp", "tensor")),
            P(("dp", "tensor")),
            P(("dp", "tensor")),
            P(("dp", "tensor")),
            P(("dp", "tensor")),
            P("dp", "tensor"),
            P("dp", None, "tensor"),
            P("tensor", "dp"),
            P("dp", "tensor"),
            P("tensor", "dp"),
        ),
        check_vma=False,
    )
```
